256 devices in a mesh: row: 64 (over y, z, core), col: 4 (over x).
Axes of the slice: x: 4, y: 4, z: 8, core: 2. Of those that a mesh axis runs over, the one named last changes fastest.
Arguments:
- layout: bfloat16 [512, 8192], P('row', 'col'), may hold values from -1 to 1
- target: bfloat16 [512, 8192], P('row', 'col'), may hold values from 0 to 1
- kernel_real: float32 [24, 128, 128], replicated, may hold values from -320 to 320
- kernel_imaginary: float32 [24, 128, 128], replicated, may hold values from -320 to 320
- weights: float32 [24], replicated, may hold values from 0.02 to 0.5
- first_taps: float32 [9, 64], replicated, may hold values from -2 to 2
- first_bias: float32 [64], replicated, may hold values from -3 to 3
- second_taps: float32 [9, 64], replicated, may hold values from -0.25 to 0.25
- second_bias: float32 [1], replicated, may hold values from -3 to 3
Outputs:
- resist: float32 [512, 8192], P('row', 'col')
- kernel_grads: float32 [2, 24, 128, 128], P(None, None, None, 'row')
The draws below stay inside these ranges and needn't reach their ends.
All inputs are finite; a program needn't handle non-finite values.
Results may differ from the reference program's by a relative error of at most 0.0003.
Values may be sent and summed in bfloat16 or wider, within the bound.
No kernel may reach another device: no remote copies, remote signals or barrier semaphores. Data moves between devices by JAX's collectives and lax.ppermute only.
A program may use at most 64 MiB of HBM per device.

```python
import math
import jax
import jax.numpy as jnp
from jax import lax

TILE = 512
BAND = 128
KERNELS = 24
CHANNELS = 64
ROWS = 512
COLS = 8192


def envelope(key, spread, offset):
    key = jax.random.fold_in(key, 101)
    first_key, second_key = jax.random.split(key)
    row_scale = jnp.exp(jax.random.uniform(first_key, (BAND,), jnp.float32, -spread, spread))
    ramp = jnp.arange(BAND, dtype=jnp.float32) / BAND
    col_scale = jnp.exp(jax.random.uniform(second_key, (BAND,), jnp.float32, -0.5, 0.5)) * (offset + ramp)
    return row_scale[:, None] * col_scale[None, :]


def spread_noise(key):
    own_key = jax.random.fold_in(key, 0)
    return jax.random.truncated_normal(own_key, -4.0, 4.0, (KERNELS, BAND, BAND), jnp.float32)


def draw_kernel_real(key, part):
    shape_scale = envelope(key, 1.0, 0.5)
    key = jax.random.fold_in(key, 3)
    amplitude = math.sqrt(ROWS * TILE) / BAND
    noise = spread_noise(key)
    return (amplitude * shape_scale[None] * noise).astype(jnp.float32)


def draw_kernel_imaginary(key, part):
    shape_scale = envelope(key, 1.0, 0.5)
    key = jax.random.fold_in(key, 7)
    amplitude = math.sqrt(ROWS * TILE) / BAND
    noise = spread_noise(key)
    return (amplitude * shape_scale[None] * noise).astype(jnp.float32)


def levels(rng, shape, cuts, smallest, high):
    loudness, own = 1.0, jax.random.fold_in(rng, 6)
    for axis_at, parts in cuts:
        heights = jnp.exp(jax.random.uniform(jax.random.fold_in(own, axis_at), (parts,), jnp.float32, smallest / len(cuts), high / len(cuts)))
        loudness = loudness * jnp.repeat(heights, shape[axis_at] // parts).reshape([-1 if axis == axis_at else 1 for axis in range(len(shape))])
    return loudness


def bell_draw(key, shape, width, reach, kind=jnp.bfloat16):
    entries = jax.random.normal(key, shape, jnp.float32) * width
    return jnp.minimum(jnp.maximum(entries, -reach), reach).astype(kind)


def setup_inputs(seed: int = 0) -> dict:
    arg_keys = jax.random.split(jax.random.key(seed), 10)
    layout = jnp.clip(jax.random.uniform(arg_keys[0], (ROWS, COLS), jnp.float32, -1.0, 1.0) * levels(arg_keys[0], (ROWS, COLS), ((0, 64), (1, 4)), -0.4, 0.0), -1.0, 1.0).astype(jnp.bfloat16)
    target = jnp.clip(1.0 * jax.random.uniform(arg_keys[1], (ROWS, COLS), jnp.float32) ** levels(arg_keys[1], (ROWS, COLS), ((0, 64), (1, 4)), -0.2, 0.2), 0.0, 1.0).astype(jnp.bfloat16)
    kernel_real = draw_kernel_real(jax.random.fold_in(arg_keys[9], 71), 0)
    kernel_imaginary = draw_kernel_imaginary(jax.random.fold_in(arg_keys[9], 71), 0)
    weights = jnp.clip(jnp.exp(jax.random.uniform(arg_keys[4], (KERNELS,), jnp.float32, math.log(0.02), math.log(0.5))), 0.02, 0.5)
    first_taps = bell_draw(arg_keys[5], (9, CHANNELS), 9 ** -0.5, 2.0, jnp.float32)
    first_bias = bell_draw(arg_keys[6], (CHANNELS,), 0.5, 3.0, jnp.float32)
    second_taps = bell_draw(arg_keys[7], (9, CHANNELS), (9 * CHANNELS) ** -0.5, 0.25, jnp.float32)
    second_bias = bell_draw(arg_keys[8], (1,), 0.5, 3.0, jnp.float32)
    return dict(layout=layout, target=target, kernel_real=kernel_real, kernel_imaginary=kernel_imaginary, weights=weights, first_taps=first_taps, first_bias=first_bias, second_taps=second_taps, second_bias=second_bias)


HIGHEST = lax.Precision.HIGHEST

def phase_pair(band_size, positions, period):
    frequency = jnp.arange(band_size, dtype=jnp.int32) - band_size // 2
    product = jnp.mod(frequency[:, None] * positions[None, :], period)
    angles = product.astype(jnp.float32) * (2.0 * math.pi / period)
    return (jnp.cos(angles), jnp.sin(angles))

def inside_mask(first_row, first_col, height, col_span, row_total, col_total):
    rows_here = first_row + jnp.arange(height, dtype=jnp.int32)
    cols_here = first_col + jnp.arange(col_span, dtype=jnp.int32)
    row_valid = (rows_here >= 0) & (rows_here < row_total)
    col_valid = (cols_here >= 0) & (cols_here < col_total)
    return (row_valid[:, None] & col_valid[None, :]).astype(jnp.float32)

def tap_views(source, height, col_span, reverse):
    pieces = []
    for tap_index in range(9):
        shift_row = tap_index // 3
        shift_col = tap_index % 3
        if reverse:
            shift_row = 2 - shift_row
            shift_col = 2 - shift_col
        pieces.append(source[shift_row:shift_row + height, shift_col:shift_col + col_span])
    return jnp.stack(pieces, axis=0)

def shifted_sum(stacked, height, col_span, reverse):
    running = None
    for tap_index in range(9):
        shift_row = tap_index // 3
        shift_col = tap_index % 3
        if reverse:
            shift_row = 2 - shift_row
            shift_col = 2 - shift_col
        piece = stacked[tap_index, shift_row:shift_row + height, shift_col:shift_col + col_span]
        running = piece if running is None else running + piece
    return running

def resist_forward(window, first_taps, first_bias, second_taps, second_bias, validity):
    height = window.shape[0] - 2
    col_span = window.shape[1] - 2
    views = tap_views(window, height, col_span, False)
    hidden = jnp.tanh(jnp.einsum('tc,tnm->cnm', first_taps, views, precision=HIGHEST) + first_bias[:, None, None]) * validity
    mixing = jnp.einsum('tc,cnm->tnm', second_taps, hidden, precision=HIGHEST)
    logits = second_bias[0] + shifted_sum(mixing, height - 2, col_span - 2, False)
    return (hidden, logits)

def tile_intensity(tile_block, kernel_real, kernel_imaginary, weights):
    norm_factor = 1.0 / math.sqrt(ROWS * TILE)
    row_cos, row_sin = phase_pair(BAND, jnp.arange(ROWS, dtype=jnp.int32), ROWS)
    col_cos, col_sin = phase_pair(BAND, jnp.arange(TILE, dtype=jnp.int32), TILE)
    part_real = jnp.dot(tile_block, col_cos.T, precision=HIGHEST, preferred_element_type=jnp.float32)
    part_imag = -jnp.dot(tile_block, col_sin.T, precision=HIGHEST, preferred_element_type=jnp.float32)
    spectrum_real = (jnp.dot(row_cos, part_real, precision=HIGHEST, preferred_element_type=jnp.float32) + jnp.dot(row_sin, part_imag, precision=HIGHEST, preferred_element_type=jnp.float32)) * norm_factor
    spectrum_imag = (jnp.dot(row_cos, part_imag, precision=HIGHEST, preferred_element_type=jnp.float32) - jnp.dot(row_sin, part_real, precision=HIGHEST, preferred_element_type=jnp.float32)) * norm_factor
    prod_real = kernel_real * spectrum_real[None] - kernel_imaginary * spectrum_imag[None]
    prod_imag = kernel_real * spectrum_imag[None] + kernel_imaginary * spectrum_real[None]
    rows_real = jnp.einsum('fn,kfg->kng', row_cos, prod_real, precision=HIGHEST) - jnp.einsum('fn,kfg->kng', row_sin, prod_imag, precision=HIGHEST)
    rows_imag = jnp.einsum('fn,kfg->kng', row_cos, prod_imag, precision=HIGHEST) + jnp.einsum('fn,kfg->kng', row_sin, prod_real, precision=HIGHEST)
    field_real = (jnp.einsum('kng,gb->knb', rows_real, col_cos, precision=HIGHEST) - jnp.einsum('kng,gb->knb', rows_imag, col_sin, precision=HIGHEST)) * norm_factor
    field_imag = (jnp.einsum('kng,gb->knb', rows_real, col_sin, precision=HIGHEST) + jnp.einsum('kng,gb->knb', rows_imag, col_cos, precision=HIGHEST)) * norm_factor
    return jnp.einsum('k,knb->nb', weights, field_real * field_real + field_imag * field_imag, precision=HIGHEST)

def reference(layout, target, kernel_real, kernel_imaginary, weights, first_taps, first_bias, second_taps, second_bias):
    tiles_total = COLS // TILE
    tile_blocks = jnp.transpose(layout.astype(jnp.float32).reshape(ROWS, tiles_total, TILE), (1, 0, 2))
    target_float = target.astype(jnp.float32)

    def loss_of(kernel_part_real, kernel_part_imag):
        per_tile = jax.checkpoint(lambda tile_block: tile_intensity(tile_block, kernel_part_real, kernel_part_imag, weights))
        intensity = lax.map(per_tile, tile_blocks)
        grid_field = jnp.transpose(intensity, (1, 0, 2)).reshape(ROWS, COLS)
        padded = jnp.pad(grid_field, 2)

        def tile_resist(tile_index):
            col_start = tile_index * TILE
            window = lax.dynamic_slice(padded, (jnp.int32(0), col_start), (ROWS + 4, TILE + 4))
            validity = inside_mask(-1, col_start - 1, ROWS + 2, TILE + 2, ROWS, COLS)
            hidden, logits = resist_forward(window, first_taps, first_bias, second_taps, second_bias, validity)
            truth_tile = lax.dynamic_slice(target_float, (jnp.int32(0), col_start), (ROWS, TILE))
            tile_cost = jnp.sum(jax.nn.softplus(logits) - truth_tile * logits)
            return (tile_cost, jax.nn.sigmoid(logits))
        tile_costs, resist_tiles = lax.map(jax.checkpoint(tile_resist), jnp.arange(tiles_total, dtype=jnp.int32))
        resist_grid = jnp.transpose(resist_tiles, (1, 0, 2)).reshape(ROWS, COLS)
        return (jnp.sum(tile_costs) / tiles_total, resist_grid)
    loss_value, pullback, resist = jax.vjp(loss_of, kernel_real, kernel_imaginary, has_aux=True)
    grad_real, grad_imag = pullback(jnp.ones((), dtype=jnp.float32))
    gradient = jnp.stack([grad_real, grad_imag])
    kernel_grads = gradient / jnp.sqrt(jnp.mean(gradient * gradient) + 1e-06)
    return (resist, kernel_grads)
```

```python
import math

import jax
import jax.numpy as jnp
import numpy as np
from jax import lax
from jax.sharding import Mesh, PartitionSpec as P

TILE = 512
BAND = 128
ROW = ("y", "z", "core")
ALL = ("y", "z", "core", "x")
HIGH = lax.Precision.HIGH


def gather_on(x, axes, n):
    return lax.all_to_all(jnp.broadcast_to(x[None], (n,) + x.shape), axes, 0, 0, tiled=True)


def sum_cols(x):
    one, two, three = (lax.ppermute(x, "x", [(i, (i + k) % 4) for i in range(4)]) for k in (1, 2, 3))
    return (x + two) + (one + three)


def phase_angles(freqs, positions):
    return 2.0 * math.pi * ((freqs[:, None] * positions[None, :]) % TILE) / TILE


def col_tables():
    b = np.arange(TILE)
    g = np.arange(BAND) - BAND // 2
    ang = phase_angles(g, b)
    return np.cos(ang).astype(np.float32), np.sin(ang).astype(np.float32)


def half_tables():
    b = np.arange(TILE)
    q = np.arange(65)
    ang = phase_angles(q, b)
    half = np.concatenate([np.cos(ang[:64]), np.sin(ang[1:]), np.cos(ang[64:])], 0)
    expand = np.zeros((129, 256))
    for g in range(BAND):
        f = g - 64
        m = abs(f)
        expand[m if m < 64 else 128, g] = 1.0
        if m:
            expand[63 + m, BAND + g] = -1.0 if f > 0 else 1.0
    return half.T.astype(np.float32), expand.astype(np.float32)


def row_phase(positions):
    freq = jnp.arange(BAND, dtype=jnp.int32) - BAND // 2
    prod = jnp.mod(freq[:, None] * positions[None, :], TILE)
    ang = prod.astype(jnp.float32) * (2.0 * math.pi / TILE)
    return jnp.cos(ang), jnp.sin(ang)


def inside(first, count, total):
    at = first + jnp.arange(count, dtype=jnp.int32)
    return (at >= 0) & (at < total)


def inside_mask(first_row, first_col, height, width, rows, cols):
    return (inside(first_row, height, rows)[:, None] & inside(first_col, width, cols)[None]).astype(
        jnp.float32
    )


def tap_views(source, height, width, reverse):
    pieces = []
    for tap in range(9):
        i, j = tap // 3, tap % 3
        if reverse:
            i, j = 2 - i, 2 - j
        pieces.append(source[i : i + height, j : j + width])
    return jnp.stack(pieces, axis=0)


def shifted_sum(stacked, height, width, reverse):
    running = None
    for tap in range(9):
        i, j = tap // 3, tap % 3
        if reverse:
            i, j = 2 - i, 2 - j
        piece = stacked[tap, i : i + height, j : j + width]
        running = piece if running is None else running + piece
    return running


def dot(spec, a, b, precision=HIGH):
    return jnp.einsum(spec, a, b, precision=precision, preferred_element_type=jnp.float32)


def resist_block(window, target, first_taps, first_bias, second_taps, second_bias, row0, col0, dims):
    rows, cols = dims
    h, w = window.shape[0] - 8, window.shape[1] - 8
    valid3 = inside_mask(row0 - 3, col0 - 3, h + 6, w + 6, rows, cols)
    views = tap_views(window, h + 6, w + 6, False)
    hidden = jnp.tanh(dot("tc,tnm->cnm", first_taps, views) + first_bias[:, None, None]) * valid3
    mixing = dot("tc,cnm->tnm", second_taps, hidden)
    logits = second_bias[0] + shifted_sum(mixing, h + 4, w + 4, False)
    resist = jax.nn.sigmoid(logits)
    valid2 = inside_mask(row0 - 2, col0 - 2, h + 4, w + 4, rows, cols)
    slope = (resist - target) * (valid2 / (cols // TILE))
    spread = tap_views(slope, h + 2, w + 2, True)
    mid = hidden[:, 2:-2, 2:-2]
    valid1 = inside_mask(row0 - 1, col0 - 1, h + 2, w + 2, rows, cols)
    hidden_grad = dot("tc,tnm->cnm", second_taps, spread) * (1.0 - mid * mid) * valid1
    per_tap = dot("tc,cnm->tnm", first_taps, hidden_grad)
    return resist[2:-2, 2:-2], shifted_sum(per_tap, h, w, True)


def on_device(
    layout, target, kernel_real, kernel_imaginary, weights, first_taps, first_bias, second_taps, second_bias
):
    height, width = layout.shape
    tiles = width // TILE
    kernels = kernel_real.shape[0]
    rows, cols = height * 64, width * 4
    r = lax.axis_index(ROW)
    c = lax.axis_index("x")
    row0, col0 = r * height, c * width
    norm = 1.0 / math.sqrt(rows * TILE)

    t_up = lax.ppermute(target[-2:], ROW, [(i, i + 1) for i in range(63)])
    t_down = lax.ppermute(target[:2], ROW, [(i + 1, i) for i in range(63)])
    t_ext = jnp.concatenate([t_up, target, t_down], 0)
    t_left = lax.ppermute(t_ext[:, -2:], "x", [(i, i + 1) for i in range(3)])
    t_right = lax.ppermute(t_ext[:, :2], "x", [(i + 1, i) for i in range(3)])
    t_ext = jnp.concatenate([t_left, t_ext, t_right], 1).astype(jnp.float32)

    half, expand = half_tables()
    part = dot("nb,bg->ng", layout.astype(jnp.float32).reshape(height * tiles, TILE), half)
    extra = jnp.pad(part[:, 128].reshape(1, -1), ((0, 0), (0, 128 - height * tiles)))
    packed = jnp.concatenate([part[:, :128], extra], 0)
    gathered = gather_on(gather_on(packed, "z", 8), ("y", "core"), 8).reshape(64, -1, 128)
    main = gathered[:, : height * tiles].reshape(rows, tiles, 128)
    last = gathered[:, height * tiles, : height * tiles].reshape(rows, tiles, 1)
    full = dot("nth,hg->ntg", jnp.concatenate([main, last], -1), expand)
    n = np.arange(rows).reshape(4, 8, 2, height).transpose(0, 2, 1, 3).reshape(-1)
    ang = phase_angles(np.arange(BAND) - 64, n)
    table = np.concatenate([np.cos(ang), np.sin(ang)], 0).astype(np.float32)
    u = dot("fn,ntg->tfg", table, full)
    spec_re = (u[:, :BAND, :BAND] + u[:, BAND:, BAND:]) * norm
    spec_im = (u[:, :BAND, BAND:] - u[:, BAND:, :BAND]) * norm

    prod_re = kernel_real[:, None] * spec_re[None] - kernel_imaginary[:, None] * spec_im[None]
    prod_im = kernel_real[:, None] * spec_im[None] + kernel_imaginary[:, None] * spec_re[None]
    prod = jnp.concatenate([prod_re, prod_im], 2)
    at = row0 + jnp.array(list(range(height)) + [-4, -3, -2, -1] + [height + i for i in range(4)], jnp.int32)
    rc, rs = row_phase(at)
    row_table = jnp.stack([jnp.concatenate([rc, -rs], 0), jnp.concatenate([rs, rc], 0)], 0)
    lines = dot("iFn,ktFg->ktnig", row_table, prod)
    cc, cs = col_tables()
    synth = np.stack([np.concatenate([cc, cs], 1), np.concatenate([-cs, cc], 1)], 0) * norm
    fields = dot("ktnig,igb->ktnb", lines, synth)
    energy = jnp.sum(fields * fields * weights[:, None, None, None], 0)
    intensity = (energy[..., :TILE] + energy[..., TILE:]) * ((at >= 0) & (at < rows))[None, :, None]
    intensity = intensity.transpose(1, 0, 2).reshape(height + 8, width)
    intensity = jnp.concatenate([intensity[height : height + 4], intensity[:height], intensity[height + 4 :]], 0)
    left = lax.ppermute(intensity[:, -4:], "x", [(i, i + 1) for i in range(3)])
    right = lax.ppermute(intensity[:, :4], "x", [(i + 1, i) for i in range(3)])
    window = jnp.concatenate([left, intensity, right], 1)

    resist, grad = resist_block(
        window, t_ext, first_taps, first_bias, second_taps, second_bias, row0, col0, (rows, cols)
    )

    grad_tiles = grad.reshape(height, tiles, TILE).transpose(1, 0, 2)
    doubled = jnp.concatenate([grad_tiles, grad_tiles], -1)
    field_grad = fields[:, :, :height] * doubled[None] * (2.0 * weights)[:, None, None, None]
    field_grad = field_grad.reshape(kernels * tiles * height, 2 * TILE)
    back = synth.reshape(2, 64, 2, 2 * TILE).transpose(1, 2, 0, 3).reshape(64, 4, 2 * TILE)
    send = dot("dqb,lb->dql", back, field_grad)
    got = lax.all_to_all(send, ROW, 0, 0, tiled=True)
    freq = np.arange(BAND) - 64
    wide = phase_angles(height * np.arange(64), freq)
    w = np.stack([np.concatenate([np.cos(wide), -np.sin(wide)], 1), np.concatenate([np.sin(wide), np.cos(wide)], 1)], 0)
    y = dot("sgil,isx->glx", got.reshape(64, 2, 2, -1), w.astype(np.float32))
    y = y.reshape(2, kernels, tiles, height, 2, BAND)
    near = phase_angles(np.arange(height), freq)
    nc, ns = np.cos(near).astype(np.float32), np.sin(near).astype(np.float32)
    z_re = jnp.sum(y[..., 0, :] * nc + y[..., 1, :] * ns, 3)
    z_im = jnp.sum(y[..., 1, :] * nc - y[..., 0, :] * ns, 3)
    s_re = lax.dynamic_slice_in_dim(spec_re, 2 * r, 2, 2).transpose(2, 0, 1)[:, None]
    s_im = lax.dynamic_slice_in_dim(spec_im, 2 * r, 2, 2).transpose(2, 0, 1)[:, None]
    mine = jnp.stack([jnp.sum(z_re * s_re + z_im * s_im, 2), jnp.sum(z_im * s_re - z_re * s_im, 2)])
    whole = sum_cols(mine)
    squares = jnp.broadcast_to(jnp.sum(whole * whole), (1, 128))
    total = jnp.sum(gather_on(squares, ROW, 64)[:, 0, 0])
    entries = 2 * kernels * BAND * BAND
    return resist, whole.transpose(0, 2, 3, 1) * lax.rsqrt(total / entries + 1e-06)


def solution(mesh):
    devices = mesh.devices.reshape(4, 8, 2, 4)
    fine = Mesh(devices, ALL)
    grid = P(ROW, "x")
    in_specs = (grid, grid, P(), P(), P(), P(), P(), P(), P())
    out_specs = (grid, P(None, None, None, ROW))
    return jax.shard_map(on_device, mesh=fine, in_specs=in_specs, out_specs=out_specs, check_vma=False)
```

```python
import functools
import math

import jax
import jax.numpy as jnp
import numpy as np
from jax import lax
from jax.experimental import pallas as pl
from jax.experimental.pallas import tpu as pltpu
from jax.sharding import Mesh, PartitionSpec as P

TILE = 512
BAND = 128
ROW = ("y", "z", "core")
ALL = ("y", "z", "core", "x")
HIGH = lax.Precision.HIGH


def gather_on(x, axes, n):
    return lax.all_to_all(jnp.broadcast_to(x[None], (n,) + x.shape), axes, 0, 0, tiled=True)


def sum_cols(x):
    one, two, three = (lax.ppermute(x, "x", [(i, (i + k) % 4) for i in range(4)]) for k in (1, 2, 3))
    return (x + two) + (one + three)


def phase_angles(freqs, positions):
    return 2.0 * math.pi * ((freqs[:, None] * positions[None, :]) % TILE) / TILE


def dot(a, b):
    return jnp.dot(a, b, preferred_element_type=jnp.float32)


def constant_split(x):
    x = np.asarray(x, np.float32)
    hi = x.astype(jnp.bfloat16)
    return hi, (x - hi.astype(np.float32)).astype(jnp.bfloat16)


VMEM = pl.BlockSpec(memory_space=pltpu.VMEM)
SMEM = pl.BlockSpec(memory_space=pltpu.SMEM)
HERE = pl.BlockSpec(memory_space=pltpu.HBM)


def homes(*arrays):
    return [pltpu.with_memory_space_constraint(jnp.asarray(x), pltpu.HBM) for x in arrays]


def fetch(sources, targets, sems):
    copies = [pltpu.make_async_copy(a, b, sems.at[i]) for i, (a, b) in enumerate(zip(sources, targets, strict=True))]
    for copy in copies:
        copy.start()
    return copies


def params(mib):
    return pltpu.CompilerParams(vmem_limit_bytes=mib * 1024 * 1024)


FREQ = np.arange(BAND) - BAND // 2


def analysis_table():
    ang = phase_angles(np.arange(65), np.arange(TILE))
    table = np.zeros((TILE, 2 * BAND))
    table[:, :64], table[:, 64:BAND] = np.cos(ang[:64]).T, np.sin(ang[1:]).T
    table[:, BAND : BAND + 4] = np.cos(ang[64])[:, None]
    return np.concatenate(constant_split(table), 0)


def row_transform_tables():
    tables = []
    for y in range(4):
        for core in range(2):
            slabs = [128 * ((y - k) % 4) + 8 * (core ^ other) for other in range(2) for k in range(4)]
            n = (np.array(slabs)[:, None, None] + 16 * np.arange(8)[:, None] + np.arange(8)).reshape(-1)
            ang = phase_angles(FREQ, n)
            tables.append(np.concatenate(constant_split(np.concatenate([np.cos(ang), np.sin(ang)], 0)), 0))
    return np.stack(tables)


def expand_table(tiles, norm):
    table = np.zeros((tiles + 1, 2, BAND, 2, BAND))
    for g in range(BAND):
        q = g - 64
        m = abs(q)
        if m < 64:
            table[0, 0, m, 0, g] = 1.0
            table[0, 1, m, 1, g] = -1.0
        else:
            for t in range(tiles):
                table[1 + t, 0, t, 0, g] = 1.0
                table[1 + t, 1, t, 1, g] = -1.0
        if m:
            sign = -1.0 if q > 0 else 1.0
            table[0, 1, 63 + m, 0, g] = sign
            table[0, 0, 63 + m, 1, g] = sign
    return (table.reshape(tiles + 1, 2 * BAND, 2 * BAND) * norm).astype(jnp.bfloat16)


def synthesis_table(norm):
    ang = phase_angles(FREQ, np.arange(TILE))
    c, s = np.cos(ang), np.sin(ang)
    return np.concatenate([np.concatenate([c, s], 1), np.concatenate([-s, c], 1)], 0) * norm


def line_tables(groups, height):
    at = np.arange(groups)[:, None] * height + np.array(FIELD_ROWS)[None, :]
    ang = phase_angles(at.reshape(-1), FREQ)
    return np.concatenate([np.cos(ang), np.sin(ang)], 1).reshape(groups, 16, 2 * BAND).astype(np.float32)


FIELD_ROWS = list(range(8)) + [-4, -3, -2, -1, 8, 9, 10, 11]
HIDDEN_ROWS = list(range(-1, 9)) + [-3, -2, 9, 10]
SLOPE_ROWS = list(range(8)) + [-2, -1, 8, 9] + [None] * 4
WIDE = 17 * 128


def halves(x):
    hi = x.astype(jnp.bfloat16)
    return hi, (x - hi.astype(jnp.float32)).astype(jnp.bfloat16)


def pick(out_rows, in_rows, sign):
    hit = lambda a, b, dy: float(a is not None and b is not None and b - a == sign * (dy - 1))
    return np.array([[[hit(a, b, dy) for b in in_rows] for a in out_rows] for dy in range(3)])


INNER = HIDDEN_ROWS[:10]
CHANNELS = 64


def choose_tables():
    choose = np.zeros((3, 48, 7, 256))
    for dy in range(3):
        for dx in range(3):
            for slot in range(16):
                lane = 16 * dx + slot
                for part, section in ((0, 0), (1, 1), (0, 2)):
                    choose[part, 3 * dy + dx, dy, 48 * section + lane] = 1.0
                    choose[part, 16 + 3 * dy + dx, 4 + dy, 48 * section + lane] = 1.0
    for part in range(3):
        choose[part, 32, 3, 144 + part] = 1.0
    return choose.reshape(144, 7 * 256).astype(jnp.bfloat16)


def lane_masks():
    fore = pick(HIDDEN_ROWS, FIELD_ROWS, 1).transpose(1, 0, 2)
    back = pick(INNER, SLOPE_ROWS, -1).transpose(1, 0, 2)
    masks = np.zeros((80, 256), np.float32)
    masks[:42, :144] = np.tile(fore, (1, 1, 9)).reshape(42, 144)
    masks[42:72, :144] = np.tile(back, (1, 1, 9)).reshape(30, 144)
    return masks


def row_masks():
    fore = np.repeat(pick(SLOPE_ROWS, HIDDEN_ROWS, 1), CHANNELS, 2)
    back = np.repeat(pick(list(range(8)), INNER, -1), CHANNELS, 2)
    return fore.astype(np.float32), back.astype(np.float32)


def tables_kernel(
    first_taps_any, second_taps_any, bias_any, choose_any, lane_masks_any, fore_any, aft_any,
    first_ref, second_ref, second_back_ref, first_back_ref,
    first_taps_ref, second_taps_ref, bias_ref, choose_ref, lane_masks_ref, fore_ref, aft_ref, wide_ref, sems, *, rows
):
    sources = (first_taps_any, second_taps_any, bias_any, choose_any, lane_masks_any, fore_any, aft_any)
    targets = (first_taps_ref, second_taps_ref, bias_ref, choose_ref, lane_masks_ref, fore_ref, aft_ref)
    for copy in fetch(sources, targets, sems):
        copy.wait()
    row0 = lax.axis_index(ROW) * 8
    wide_ref[...] = jnp.zeros_like(wide_ref)
    wide_ref[0:9, 0:CHANNELS] = first_taps_ref[...]
    wide_ref[16:25, 0:CHANNELS] = second_taps_ref[...]
    wide_ref[32:33, 0:CHANNELS] = bias_ref[...]
    tall = wide_ref[...].T[:CHANNELS, :48]
    hi = tall.astype(jnp.bfloat16)
    rest = tall - hi.astype(jnp.float32)
    mid = rest.astype(jnp.bfloat16)
    low = (rest - mid.astype(jnp.float32)).astype(jnp.bfloat16)
    parts = dot(jnp.concatenate([hi, mid, low], 1), choose_ref[...])
    for h, n in enumerate(HIDDEN_ROWS):
        here = row0 + n
        valid = jnp.where((here >= 0) & (here < rows), 1.0, 0.0)
        block = parts[:, 768:1024]
        for dy in range(3):
            block = block + parts[:, 256 * dy : 256 * dy + 256] * lane_masks_ref[3 * h + dy : 3 * h + dy + 1]
        first_ref[64 * h : 64 * h + 64] = (block * valid)[:, :160].astype(jnp.bfloat16)
        if h < 10:
            block = 0.0
            for dy in range(3):
                at = 1024 + 256 * dy
                block = block + parts[:, at : at + 256] * lane_masks_ref[42 + 3 * h + dy : 43 + 3 * h + dy]
            second_back_ref[64 * h : 64 * h + 64] = (block * valid)[:, :144].astype(jnp.bfloat16)
    for taps_ref, mask_ref, out_ref, height in ((second_taps_ref, fore_ref, second_ref, 16), (first_taps_ref, aft_ref, first_back_ref, 8)):
        lanes = out_ref.shape[1]
        taps = taps_ref[...]
        taps = jnp.concatenate([taps] * (lanes // CHANNELS), 1)
        taps_hi = taps.astype(jnp.bfloat16).astype(jnp.float32)
        for at, part in ((0, taps_hi), (out_ref.shape[0] // 2, taps - taps_hi)):
            blocks = []
            for dx in range(3):
                block = 0.0
                for dy in range(3):
                    block = block + part[3 * dy + dx : 3 * dy + dx + 1] * mask_ref[dy]
                blocks.append(block)
            if height == 8:
                blocks.append(jnp.zeros((8, lanes), jnp.float32))
            whole = jnp.concatenate(blocks, 0)
            out_ref[at : at + whole.shape[0]] = whole.astype(jnp.bfloat16)


def resist_tables(first_taps, first_bias, second_taps, rows):
    args = (first_taps, second_taps, first_bias.reshape(1, -1), choose_tables(), lane_masks(), *row_masks())
    return pl.pallas_call(
        functools.partial(tables_kernel, rows=rows),
        out_shape=[
            jax.ShapeDtypeStruct((14 * CHANNELS, 160), jnp.bfloat16),
            jax.ShapeDtypeStruct((96, 14 * CHANNELS), jnp.bfloat16),
            jax.ShapeDtypeStruct((10 * CHANNELS, 144), jnp.bfloat16),
            jax.ShapeDtypeStruct((64, 10 * CHANNELS), jnp.bfloat16),
        ],
        in_specs=[HERE] * 7,
        out_specs=[VMEM] * 4,
        scratch_shapes=[pltpu.VMEM(a.shape, a.dtype) for a in args]
        + [pltpu.VMEM((BAND, BAND), jnp.float32), pltpu.SemaphoreType.DMA((7,))],
        compiler_params=params(12),
        name="tables",
    )(*homes(*args))


def resist_kernel(
    field_ref, target_ref, left_ref, right_ref, first_ref, second_ref, second_back_ref, first_back_ref, offset_ref,
    weights_any, fields_any, back_any,
    resist_ref, out_ref, weights_ref, fields_ref, back_ref,
    views_ref, keep_ref, mixed_ref, spread_ref, summed_ref, all_ref, sems, *, rows, cols
):
    copies = fetch((weights_any, fields_any, back_any), (weights_ref, fields_ref, back_ref), sems)
    row0 = lax.axis_index(ROW) * resist_ref.shape[0]
    col0 = lax.axis_index("x") * resist_ref.shape[1]
    width = resist_ref.shape[1]
    inner = keep_ref.shape[0]

    def columns(shape):
        lane = lax.broadcasted_iota(jnp.int32, shape, 1)
        m = jnp.where(lane < width + 64, lane, lane - WIDE)
        return m, (col0 + m >= 0) & (col0 + m < cols)

    chunks = [(i * 256, 256) for i in range(8)] + [(2048, 128)]
    m, in_grid = columns((16, WIDE))
    keep_col = (in_grid & (m >= -3) & (m < width + 3)).astype(jnp.float32)
    lane = lax.broadcasted_iota(jnp.int32, (16, BAND), 1)
    gap = [jnp.where(lane < 64, right_ref[i : i + 16], left_ref[i : i + 16]) for i in (0, 16)]
    field = jnp.concatenate([field_ref[...], gap[0]], 1)
    target = jnp.concatenate([target_ref[...], gap[1]], 1)
    for dx in range(3):
        moved = (field if dx == 1 else pltpu.roll(field, (1 - dx) % WIDE, 1)) * keep_col
        hi, lo = halves(moved)
        views_ref[16 * dx : 16 * dx + 16] = hi
        views_ref[48 + 16 * dx : 64 + 16 * dx] = hi
        views_ref[96 + 16 * dx : 112 + 16 * dx] = lo
    views_ref[144:160] = keep_col.astype(jnp.bfloat16)

    for at, size in chunks:
        here = slice(at, at + size)
        hidden = jnp.tanh(jnp.dot(first_ref[...], views_ref[:, here], preferred_element_type=jnp.float32))
        keep_ref[:, here] = 1.0 - hidden[:inner] * hidden[:inner]
        hi, lo = halves(hidden)
        both = jnp.dot(second_ref[...], hi, preferred_element_type=jnp.float32)
        small = jnp.dot(second_ref[0:48], lo, preferred_element_type=jnp.float32)
        mixed_ref[:, here] = both[:48] + both[48:] + small

    logits = offset_ref[0] + mixed_ref[16:32] + pltpu.roll(mixed_ref[0:16], 1, 1) + pltpu.roll(mixed_ref[32:48], WIDE - 1, 1)
    resist = 1.0 / (1.0 + jnp.exp(-logits))
    resist_ref[...] = resist[:8, :width]
    slot = lax.broadcasted_iota(jnp.int32, (16, WIDE), 0)
    n = jnp.where(slot < 8, slot, jnp.where(slot < 10, slot - 10, slot - 2))
    use = in_grid & (m >= -2) & (m < width + 2) & (slot < 12) & (row0 + n >= 0) & (row0 + n < rows)
    slope = jnp.where(use, (resist - target) * (TILE / cols), 0.0)
    grid_col = in_grid.astype(jnp.float32)
    for dx in range(3):
        moved = (slope if dx == 1 else pltpu.roll(slope, (dx - 1) % WIDE, 1)) * grid_col
        hi, lo = halves(moved)
        spread_ref[16 * dx : 16 * dx + 16] = hi
        spread_ref[48 + 16 * dx : 64 + 16 * dx] = hi
        spread_ref[96 + 16 * dx : 112 + 16 * dx] = lo

    for at, size in chunks:
        here = slice(at, at + size)
        hidden_grad = jnp.dot(second_back_ref[...], spread_ref[:, here], preferred_element_type=jnp.float32)
        hi, lo = halves(hidden_grad * keep_ref[:, here])
        both = jnp.dot(first_back_ref[...], hi, preferred_element_type=jnp.float32)
        small = jnp.dot(first_back_ref[0:32], lo, preferred_element_type=jnp.float32)
        summed_ref[:, here] = both[:32] + both[32:] + small
    grad = summed_ref[8:16] + pltpu.roll(summed_ref[0:8], WIDE - 1, 1) + pltpu.roll(summed_ref[16:24], 1, 1)
    for copy in copies:
        copy.wait()
    grad = jnp.concatenate([grad[:, t * TILE : (t + 1) * TILE] for t in range(4)], 0)
    grad = jnp.concatenate([grad, grad], 1) * 2.0
    half = back_ref.shape[0] // 2
    for i in range(3):
        piece = jnp.concatenate([fields_ref[8 * i + j] * (grad * weights_ref[8 * i + j]) for j in range(8)], 0)
        hi, lo = halves(piece)
        sides = (((1,), (1,)), ((), ()))
        both = lax.dot_general(back_ref[...], hi, sides, preferred_element_type=jnp.float32)
        small = lax.dot_general(back_ref[0:half], lo, sides, preferred_element_type=jnp.float32)
        all_ref[:, 256 * i : 256 * i + 256] = both[:half] + both[half:] + small
    low = lax.broadcasted_iota(jnp.int32, (8, 384), 0) < 4
    for d in range(32):
        first, second = all_ref[8 * d : 8 * d + 8, 0:384], all_ref[8 * d : 8 * d + 8, 384:768]
        out_ref[2 * d] = jnp.where(low, first, pltpu.roll(second, 4, 0))
        out_ref[2 * d + 1] = jnp.where(low, pltpu.roll(first, 4, 0), second)


def resist_block(field, target, left, right, tables, second_bias, weights, fields, back, dims):
    rows, cols = dims
    inner, width = tables[2].shape[0], field.shape[1]
    return pl.pallas_call(
        functools.partial(resist_kernel, rows=rows, cols=cols),
        out_shape=[jax.ShapeDtypeStruct((8, width), jnp.float32), jax.ShapeDtypeStruct((64, 8, 384), jnp.float32)],
        in_specs=[VMEM] * 8 + [SMEM] + [HERE] * 3,
        out_specs=[VMEM] * 2,
        scratch_shapes=[
            pltpu.SMEM(weights.shape, jnp.float32),
            pltpu.VMEM(fields.shape, jnp.float32),
            pltpu.VMEM(back.shape, jnp.bfloat16),
            pltpu.VMEM((160, WIDE), jnp.bfloat16),
            pltpu.VMEM((inner, WIDE), jnp.float32),
            pltpu.VMEM((48, WIDE), jnp.float32),
            pltpu.VMEM((144, WIDE), jnp.bfloat16),
            pltpu.VMEM((32, WIDE), jnp.float32),
            pltpu.VMEM((256, 768), jnp.float32),
            pltpu.SemaphoreType.DMA((3,)),
        ],
        compiler_params=params(28),
        name="resist",
    )(field, target, left, right, *tables, second_bias, *homes(weights, fields, back))


def analyse_kernel(layout_any, table_any, out_ref, layout_ref, table_ref, sems):
    for copy in fetch((layout_any, table_any), (layout_ref, table_ref), sems):
        copy.wait()
    x = layout_ref[...].astype(jnp.float32)
    x = jnp.concatenate([x[:, t * TILE : (t + 1) * TILE] for t in range(4)], 0).astype(jnp.bfloat16)
    sums = dot(x, table_ref[0:TILE]) + dot(x, table_ref[TILE:])
    lane = lax.broadcasted_iota(jnp.int32, (8, BAND), 1)
    last = jnp.zeros((8, BAND), jnp.float32)
    for t in range(4):
        last = jnp.where(lane == t, sums[8 * t : 8 * t + 8, BAND:], last)
    packed = jnp.concatenate([sums[:, :BAND], last], 0)
    for i in range(out_ref.shape[0]):
        out_ref[i] = packed


def fields_kernel(*refs, rows):
    slab_any, refs = refs[:8], refs[8:]
    (
        rows_any, expand_any, line_any, synth_any, real_any, imag_any, weights_any, target_any, above_any, below_any,
        spec_ref, fields_any, intensity_ref, wanted_ref, first_edge_ref, last_edge_ref, *refs
    ) = refs
    slabs, refs = refs[:8], refs[8:]
    (
        rows_ref, expand_ref, line_ref, synth_ref, real_ref, imag_ref, weights_ref, target_ref, above_ref, below_ref,
        fields_ref, seen_ref, line_hi_ref, line_lo_ref, sum_ref, sems, out_sems
    ) = refs
    at = 2 * lax.axis_index("y") + lax.axis_index("core")
    r = lax.axis_index(ROW)
    sources = (*slab_any, rows_any.at[at], expand_any, line_any.at[r], synth_any, real_any, imag_any, weights_any, target_any, above_any, below_any)
    targets = (*slabs, rows_ref, expand_ref, line_ref, synth_ref, real_ref, imag_ref, weights_ref, target_ref, above_ref, below_ref)
    copies = fetch(sources, targets, sems)
    row0 = r * 8
    kernels = real_ref.shape[0]
    for p, slab in enumerate(slabs):
        copies[p].wait()
        for t in range(5):
            hi, lo = halves(slab[:, 8 * t : 8 * t + 8, :].reshape(64, BAND))
            seen_ref[64 * p : 64 * p + 64, t * BAND : (t + 1) * BAND] = hi
            seen_ref[rows + 64 * p : rows + 64 * p + 64, t * BAND : (t + 1) * BAND] = lo
    copies[8].wait()
    table_hi = rows_ref[0 : 2 * BAND]
    u = dot(table_hi, seen_ref[0:rows]) + dot(rows_ref[2 * BAND :], seen_ref[0:rows]) + dot(table_hi, seen_ref[rows:])

    def pair(t):
        both = u[:, t * BAND : (t + 1) * BAND]
        return halves(jnp.concatenate([both[:BAND], both[BAND:]], 1))

    copies[9].wait()
    last_hi, last_lo = pair(4)
    for t in range(4):
        hi, lo = pair(t)
        spec_ref[t] = (
            dot(hi, expand_ref[0]) + dot(lo, expand_ref[0]) + dot(last_hi, expand_ref[1 + t]) + dot(last_lo, expand_ref[1 + t])
        )

    for copy in copies[10:]:
        copy.wait()
    phase = line_ref[...]
    c, s = phase[:, :BAND], phase[:, BAND:]
    table = jnp.concatenate([jnp.concatenate([c, -s], 1), jnp.concatenate([s, c], 1)], 0)
    lines_hi, lines_lo = halves(table)
    lines_both = jnp.concatenate([lines_hi, lines_lo], 0)
    sum_ref[...] = jnp.zeros_like(sum_ref)

    def lines(k, slot, j):
        kr, ki = real_ref[k], imag_ref[k]
        pieces = []
        for p in range(2):
            columns = []
            for t in (2 * p, 2 * p + 1):
                sr, si = spec_ref[t, :, :BAND], spec_ref[t, :, BAND:]
                columns.append(jnp.concatenate([kr * sr - ki * si, kr * si + ki * sr], 0))
            hi, lo = halves(jnp.concatenate(columns, 1))
            both = dot(lines_both, hi)
            out = both[:32] + both[32:] + dot(lines_hi, lo)
            for t in range(2):
                pieces.append(jnp.concatenate([out[:16, t * BAND : (t + 1) * BAND], out[16:, t * BAND : (t + 1) * BAND]], 1))
        hi, lo = halves(jnp.concatenate(pieces, 0))
        line_hi_ref[slot, 64 * j : 64 * j + 64] = hi
        line_lo_ref[slot, 64 * j : 64 * j + 64] = lo

    def waves(k0, slot, q):
        here = slice(q * 256, q * 256 + 256)
        synth_hi = synth_ref[0 : 2 * BAND, here]
        line_hi = line_hi_ref[slot]
        f = dot(line_hi, synth_hi) + dot(line_lo_ref[slot], synth_hi) + dot(line_hi, synth_ref[2 * BAND :, here])
        total = sum_ref[:, here]
        for j in range(4):
            part = f[64 * j : 64 * j + 64]
            total = total + weights_ref[k0 + j] * (part * part)
            fields_ref[k0 + j, :, here] = jnp.concatenate([part[16 * t : 16 * t + 8] for t in range(4)], 0)
        sum_ref[:, here] = total

    sent = []
    for j in range(4):
        lines(j, 0, j)
    for i in range(kernels // 4):
        for j in range(4):
            waves(4 * i, i % 2, j)
            if 4 * i + 4 < kernels:
                lines(4 * i + 4 + j, (i + 1) % 2, j)
        sent.append(pltpu.make_async_copy(fields_ref.at[4 * i : 4 * i + 4], fields_any.at[4 * i : 4 * i + 4], out_sems.at[i]))
        sent[-1].start()
    slot = lax.broadcasted_iota(jnp.int32, (16, TILE), 0)
    n = row0 + jnp.where(slot < 8, slot, jnp.where(slot < 12, slot - 12, slot - 4))
    inside = (n >= 0) & (n < rows)
    for t in range(4):
        both = sum_ref[16 * t : 16 * t + 16]
        intensity_ref[:, t * TILE : (t + 1) * TILE] = jnp.where(inside, both[:, :TILE] + both[:, TILE:], 0.0)
    wanted_ref[0:8] = target_ref[...].astype(jnp.float32)
    above, below = above_ref[...].astype(jnp.float32), below_ref[...].astype(jnp.float32)
    wanted_ref[8:16] = jnp.concatenate([above[6:8], below[0:2], jnp.zeros((4, above.shape[1]), jnp.float32)], 0)
    width = intensity_ref.shape[1]
    for i, ref in ((0, intensity_ref), (16, wanted_ref)):
        first_edge_ref[i : i + 16] = ref[:, 0:BAND]
        last_edge_ref[i : i + 16] = ref[:, width - BAND :]
    for copy in sent:
        copy.wait()


def on_device(
    layout, target, kernel_real, kernel_imaginary, weights, first_taps, first_bias, second_taps, second_bias
):
    height, width = layout.shape
    tiles = width // TILE
    kernels = kernel_real.shape[0]
    rows, cols = height * 64, width * 4
    r = lax.axis_index(ROW)
    norm = 1.0 / math.sqrt(rows * TILE)

    above = lax.ppermute(target, ROW, [(i, i + 1) for i in range(63)])
    below = lax.ppermute(target, ROW, [(i + 1, i) for i in range(63)])
    tables = resist_tables(first_taps, first_bias, second_taps, rows)

    packed = pl.pallas_call(
        analyse_kernel,
        out_shape=jax.ShapeDtypeStruct((8, 40, BAND), jnp.float32),
        in_specs=[HERE] * 2,
        out_specs=VMEM,
        scratch_shapes=[
            pltpu.VMEM(layout.shape, jnp.bfloat16),
            pltpu.VMEM((2 * TILE, 2 * BAND), jnp.bfloat16),
            pltpu.SemaphoreType.DMA((2,)),
        ],
        compiler_params=params(8),
        name="analyse",
    )(*homes(layout, analysis_table()))
    gathered = lax.all_to_all(packed, "z", 0, 0, tiled=True)
    gathered, above, below, *tables = lax.optimization_barrier((gathered, above, below, *tables))
    slabs = [gathered] + [lax.ppermute(gathered, "y", [(i, (i + k) % 4) for i in range(4)]) for k in (1, 2, 3)]
    slabs = slabs + [lax.ppermute(slab, "core", [(0, 1), (1, 0)]) for slab in slabs]

    synth = synthesis_table(norm)
    spec, fields, intensity, wanted, first_edge, last_edge = pl.pallas_call(
        functools.partial(fields_kernel, rows=rows),
        out_shape=[
            jax.ShapeDtypeStruct((tiles, BAND, 2 * BAND), jnp.float32),
            pltpu.HBM((kernels, tiles * height, 2 * TILE), jnp.float32),
            jax.ShapeDtypeStruct((16, width), jnp.float32),
            jax.ShapeDtypeStruct((16, width), jnp.float32),
            jax.ShapeDtypeStruct((32, BAND), jnp.float32),
            jax.ShapeDtypeStruct((32, BAND), jnp.float32),
        ],
        in_specs=[HERE] * 18,
        out_specs=[VMEM, HERE] + [VMEM] * 4,
        scratch_shapes=[pltpu.VMEM((8, 40, BAND), jnp.float32)] * 8
        + [
            pltpu.VMEM((4 * BAND, rows), jnp.bfloat16),
            pltpu.VMEM((tiles + 1, 2 * BAND, 2 * BAND), jnp.bfloat16),
            pltpu.VMEM((16, 2 * BAND), jnp.float32),
            pltpu.VMEM((4 * BAND, 2 * TILE), jnp.bfloat16),
            pltpu.VMEM(kernel_real.shape, jnp.float32),
            pltpu.VMEM(kernel_real.shape, jnp.float32),
            pltpu.SMEM(weights.shape, jnp.float32),
            pltpu.VMEM(target.shape, jnp.bfloat16),
            pltpu.VMEM(target.shape, jnp.bfloat16),
            pltpu.VMEM(target.shape, jnp.bfloat16),
            pltpu.VMEM((kernels, tiles * height, 2 * TILE), jnp.float32),
            pltpu.VMEM((2 * rows, 5 * BAND), jnp.bfloat16),
            pltpu.VMEM((2, 256, 2 * BAND), jnp.bfloat16),
            pltpu.VMEM((2, 256, 2 * BAND), jnp.bfloat16),
            pltpu.VMEM((64, 2 * TILE), jnp.float32),
            pltpu.SemaphoreType.DMA((18,)),
            pltpu.SemaphoreType.DMA((kernels // 4,)),
        ],
        compiler_params=params(28),
        name="fields",
    )(
        *homes(
            *slabs, row_transform_tables(), expand_table(tiles, norm), line_tables(64, height),
            np.concatenate(constant_split(synth), 0), kernel_real, kernel_imaginary, weights, target, above, below,
        )
    )
    left = lax.ppermute(last_edge, "x", [(i, i + 1) for i in range(3)])
    right = lax.ppermute(first_edge, "x", [(i + 1, i) for i in range(3)])
    back = synth.reshape(2, 64, 2, 2 * TILE).transpose(1, 2, 0, 3).reshape(256, 2 * TILE)
    back = np.concatenate(constant_split(back), 0)
    resist, send = resist_block(
        intensity, wanted, left, right, tables, second_bias, weights, fields, back, (rows, cols)
    )

    got = lax.all_to_all(send, ROW, 0, 0, tiled=True)
    wide = phase_angles(height * np.arange(64), FREQ)
    w = np.stack([np.concatenate([np.cos(wide), -np.sin(wide)], 1), np.concatenate([np.sin(wide), np.cos(wide)], 1)], 0)
    y = jnp.einsum(
        "shgil,isx->ghlx", got.reshape(64, 2, 2, 2, -1), w.astype(np.float32), precision=HIGH, preferred_element_type=jnp.float32
    )
    y = y.reshape(2, kernels, tiles, height, 2, BAND)
    near = phase_angles(np.arange(height), FREQ)
    nc, ns = np.cos(near).astype(np.float32), np.sin(near).astype(np.float32)
    z_re = jnp.sum(y[..., 0, :] * nc + y[..., 1, :] * ns, 3)
    z_im = jnp.sum(y[..., 1, :] * nc - y[..., 0, :] * ns, 3)
    s_re = lax.dynamic_slice_in_dim(spec, 2 * r, 2, 2).transpose(2, 0, 1)[:, None]
    s_im = lax.dynamic_slice_in_dim(spec, BAND + 2 * r, 2, 2).transpose(2, 0, 1)[:, None]
    mine = jnp.stack([jnp.sum(z_re * s_re + z_im * s_im, 2), jnp.sum(z_im * s_re - z_re * s_im, 2)])
    whole = sum_cols(mine)
    squares = jnp.broadcast_to(jnp.sum(whole * whole), (1, 128))
    total = jnp.sum(gather_on(squares, ROW, 64)[:, 0, 0])
    entries = 2 * kernels * BAND * BAND
    return resist, whole.transpose(0, 2, 3, 1) * lax.rsqrt(total / entries + 1e-06)


def solution(mesh):
    devices = mesh.devices.reshape(4, 8, 2, 4)
    fine = Mesh(devices, ALL)
    grid = P(ROW, "x")
    in_specs = (grid, grid, P(), P(), P(), P(), P(), P(), P())
    out_specs = (grid, P(None, None, None, ROW))
    return jax.shard_map(on_device, mesh=fine, in_specs=in_specs, out_specs=out_specs, check_vma=False)
```

```python
import functools
import math

import jax
import jax.numpy as jnp
import numpy as np
from jax import lax
from jax.experimental import pallas as pl
from jax.experimental.pallas import tpu as pltpu
from jax.sharding import Mesh, PartitionSpec as P

TILE = 512
BAND = 128
ROW = ("y", "z", "core")
ALL = ("y", "z", "core", "x")


def phase_angles(freqs, positions):
    return 2.0 * math.pi * ((freqs[:, None] * positions[None, :]) % TILE) / TILE


def dot(a, b):
    return jnp.dot(a, b, preferred_element_type=jnp.float32)


def constant_split(x):
    x = np.asarray(x, np.float32)
    hi = x.astype(jnp.bfloat16)
    return hi, (x - hi.astype(np.float32)).astype(jnp.bfloat16)


VMEM = pl.BlockSpec(memory_space=pltpu.VMEM)
SMEM = pl.BlockSpec(memory_space=pltpu.SMEM)
HERE = pl.BlockSpec(memory_space=pltpu.HBM)


def near(*arrays):
    return [pltpu.with_memory_space_constraint(jnp.asarray(x), pltpu.VMEM) for x in arrays]


def homes(*arrays):
    return [pltpu.with_memory_space_constraint(jnp.asarray(x), pltpu.HBM) for x in arrays]


def fetch(sources, targets, sems):
    copies = [pltpu.make_async_copy(a, b, sems.at[i]) for i, (a, b) in enumerate(zip(sources, targets, strict=True))]
    for copy in copies:
        copy.start()
    return copies


def params(mib):
    return pltpu.CompilerParams(vmem_limit_bytes=mib * 1024 * 1024)


FREQ = np.arange(BAND) - BAND // 2


def analysis_table():
    ang = phase_angles(np.arange(65), np.arange(TILE))
    table = np.zeros((TILE, 2 * BAND))
    table[:, :64], table[:, 64:BAND] = np.cos(ang[:64]).T, np.sin(ang[1:]).T
    table[:, BAND : BAND + 4] = np.cos(ang[64])[:, None]
    return np.concatenate(constant_split(table), 0)


def row_transform_tables():
    tables = []
    for y in range(4):
        for core in range(2):
            slabs = [128 * ((y - k) % 4) + 8 * (core ^ other) for other in range(2) for k in range(4)]
            n = (np.array(slabs)[:, None, None] + 16 * np.arange(8)[:, None] + np.arange(8)).reshape(-1)
            ang = phase_angles(FREQ, n)
            tables.append(np.concatenate(constant_split(np.concatenate([np.cos(ang), np.sin(ang)], 0)), 0))
    return np.stack(tables)


def expand_table(norm):
    table = np.zeros((2, BAND, 2, BAND))
    for g in range(BAND):
        q = g - 64
        m = abs(q)
        if m < 64:
            table[0, m, 0, g] = 1.0
            table[1, m, 1, g] = -1.0
        if m:
            sign = -1.0 if q > 0 else 1.0
            table[1, 63 + m, 0, g] = sign
            table[0, 63 + m, 1, g] = sign
    return (table.reshape(2 * BAND, 2 * BAND) * norm).astype(jnp.bfloat16)


def synthesis_table(norm):
    ang = phase_angles(FREQ, np.arange(TILE))
    c, s = np.cos(ang), np.sin(ang)
    return np.concatenate([np.concatenate([c, s], 1), np.concatenate([-s, c], 1)], 0) * norm


def line_tables(groups, height):
    at = np.arange(groups)[:, None] * height + np.array(FIELD_ROWS)[None, :]
    ang = phase_angles(at.reshape(-1), FREQ)
    return np.concatenate([np.cos(ang), np.sin(ang)], 1).reshape(groups, 16, 2 * BAND).astype(np.float32)


FIELD_ROWS = list(range(8)) + [-4, -3, -2, -1, 8, 9, 10, 11]
HIDDEN_ROWS = list(range(-1, 9)) + [-3, -2, 9, 10]
SLOPE_ROWS = list(range(8)) + [-2, -1, 8, 9] + [None] * 4
WIDE = 17 * 128


def halves(x):
    hi = x.astype(jnp.bfloat16)
    return hi, (x - hi.astype(jnp.float32)).astype(jnp.bfloat16)


def pick(out_rows, in_rows, sign):
    hit = lambda a, b, dy: float(a is not None and b is not None and b - a == sign * (dy - 1))
    return np.array([[[hit(a, b, dy) for b in in_rows] for a in out_rows] for dy in range(3)])


INNER = HIDDEN_ROWS[:10]
CHANNELS = 64


def choose_tables():
    choose = np.zeros((3, 48, 7, 256))
    for dy in range(3):
        for dx in range(3):
            for slot in range(16):
                lane = 16 * dx + slot
                for part, section in ((0, 0), (1, 1), (0, 2)):
                    choose[part, 3 * dy + dx, dy, 48 * section + lane] = 1.0
                    choose[part, 16 + 3 * dy + dx, 4 + dy, 48 * section + lane] = 1.0
    for part in range(3):
        choose[part, 32, 3, 144 + part] = 1.0
    return choose.reshape(144, 7 * 256).astype(jnp.bfloat16)


def lane_masks():
    fore = pick(HIDDEN_ROWS, FIELD_ROWS, 1).transpose(1, 0, 2)
    back = pick(INNER, SLOPE_ROWS, -1).transpose(1, 0, 2)
    masks = np.zeros((80, 256), np.float32)
    masks[:42, :144] = np.tile(fore, (1, 1, 9)).reshape(42, 144)
    masks[42:72, :144] = np.tile(back, (1, 1, 9)).reshape(30, 144)
    return masks


def row_masks():
    fore = np.repeat(pick(SLOPE_ROWS, HIDDEN_ROWS, 1), CHANNELS, 2)
    back = np.repeat(pick(list(range(8)), INNER, -1), CHANNELS, 2)
    return fore.astype(np.float32), back.astype(np.float32)


def tables_kernel(
    first_taps_any, second_taps_any, bias_any, choose_any, lane_masks_any, fore_any, aft_any,
    first_ref, second_ref, second_back_ref, first_back_ref,
    first_taps_ref, second_taps_ref, bias_ref, choose_ref, lane_masks_ref, fore_ref, aft_ref, wide_ref, sems, *, rows
):
    sources = (first_taps_any, second_taps_any, bias_any, choose_any, lane_masks_any, fore_any, aft_any)
    targets = (first_taps_ref, second_taps_ref, bias_ref, choose_ref, lane_masks_ref, fore_ref, aft_ref)
    for copy in fetch(sources, targets, sems):
        copy.wait()
    row0 = lax.axis_index(ROW) * 8
    wide_ref[...] = jnp.zeros_like(wide_ref)
    wide_ref[0:9, 0:CHANNELS] = first_taps_ref[...]
    wide_ref[16:25, 0:CHANNELS] = second_taps_ref[...]
    wide_ref[32:33, 0:CHANNELS] = bias_ref[...]
    tall = wide_ref[...].T[:CHANNELS, :48]
    hi = tall.astype(jnp.bfloat16)
    rest = tall - hi.astype(jnp.float32)
    mid = rest.astype(jnp.bfloat16)
    low = (rest - mid.astype(jnp.float32)).astype(jnp.bfloat16)
    parts = dot(jnp.concatenate([hi, mid, low], 1), choose_ref[...])
    for h, n in enumerate(HIDDEN_ROWS):
        here = row0 + n
        valid = jnp.where((here >= 0) & (here < rows), 1.0, 0.0)
        block = parts[:, 768:1024]
        for dy in range(3):
            block = block + parts[:, 256 * dy : 256 * dy + 256] * lane_masks_ref[3 * h + dy : 3 * h + dy + 1]
        first_ref[64 * h : 64 * h + 64] = (block * valid)[:, :160].astype(jnp.bfloat16)
        if h < 10:
            block = 0.0
            for dy in range(3):
                at = 1024 + 256 * dy
                block = block + parts[:, at : at + 256] * lane_masks_ref[42 + 3 * h + dy : 43 + 3 * h + dy]
            second_back_ref[64 * h : 64 * h + 64] = (block * valid)[:, :144].astype(jnp.bfloat16)
    for taps_ref, mask_ref, out_ref, height in ((second_taps_ref, fore_ref, second_ref, 16), (first_taps_ref, aft_ref, first_back_ref, 8)):
        lanes = out_ref.shape[1]
        taps = taps_ref[...]
        taps = jnp.concatenate([taps] * (lanes // CHANNELS), 1)
        taps_hi = taps.astype(jnp.bfloat16).astype(jnp.float32)
        for at, part in ((0, taps_hi), (out_ref.shape[0] // 2, taps - taps_hi)):
            blocks = []
            for dx in range(3):
                block = 0.0
                for dy in range(3):
                    block = block + part[3 * dy + dx : 3 * dy + dx + 1] * mask_ref[dy]
                blocks.append(block)
            if height == 8:
                blocks.append(jnp.zeros((8, lanes), jnp.float32))
            whole = jnp.concatenate(blocks, 0)
            out_ref[at : at + whole.shape[0]] = whole.astype(jnp.bfloat16)


def resist_tables(first_taps, first_bias, second_taps, rows):
    args = (first_taps, second_taps, first_bias.reshape(1, -1), choose_tables(), lane_masks(), *row_masks())
    return pl.pallas_call(
        functools.partial(tables_kernel, rows=rows),
        out_shape=[
            jax.ShapeDtypeStruct((14 * CHANNELS, 160), jnp.bfloat16),
            jax.ShapeDtypeStruct((96, 14 * CHANNELS), jnp.bfloat16),
            jax.ShapeDtypeStruct((10 * CHANNELS, 144), jnp.bfloat16),
            jax.ShapeDtypeStruct((64, 10 * CHANNELS), jnp.bfloat16),
        ],
        in_specs=[HERE] * 7,
        out_specs=[VMEM] * 4,
        scratch_shapes=[pltpu.VMEM(a.shape, a.dtype) for a in args]
        + [pltpu.VMEM((BAND, BAND), jnp.float32), pltpu.SemaphoreType.DMA((7,))],
        compiler_params=params(12),
        name="tables",
    )(*homes(*args))


def resist_kernel(
    field_ref, target_ref, left_ref, right_ref, first_ref, second_ref, second_back_ref, first_back_ref, offset_ref,
    fields_ref, weights_any, back_any,
    resist_ref, out_ref, weights_ref, back_ref,
    views_ref, keep_ref, mixed_ref, spread_ref, summed_ref, all_ref, sems, *, rows, cols
):
    copies = fetch((weights_any, back_any), (weights_ref, back_ref), sems)
    row0 = lax.axis_index(ROW) * resist_ref.shape[0]
    col0 = lax.axis_index("x") * resist_ref.shape[1]
    width = resist_ref.shape[1]
    inner = keep_ref.shape[0]

    def columns(shape):
        lane = lax.broadcasted_iota(jnp.int32, shape, 1)
        m = jnp.where(lane < width + 64, lane, lane - WIDE)
        return m, (col0 + m >= 0) & (col0 + m < cols)

    chunks = [(i * 256, 256) for i in range(8)] + [(2048, 128)]
    m, in_grid = columns((16, WIDE))
    keep_col = (in_grid & (m >= -3) & (m < width + 3)).astype(jnp.float32)
    lane = lax.broadcasted_iota(jnp.int32, (16, BAND), 1)
    gap = [jnp.where(lane < 64, right_ref[i : i + 16], left_ref[i : i + 16]) for i in (0, 16)]
    field = jnp.concatenate([field_ref[...], gap[0]], 1)
    target = jnp.concatenate([target_ref[...], gap[1]], 1)
    for dx in range(3):
        moved = (field if dx == 1 else pltpu.roll(field, (1 - dx) % WIDE, 1)) * keep_col
        hi, lo = halves(moved)
        views_ref[16 * dx : 16 * dx + 16] = hi
        views_ref[48 + 16 * dx : 64 + 16 * dx] = hi
        views_ref[96 + 16 * dx : 112 + 16 * dx] = lo
    views_ref[144:160] = keep_col.astype(jnp.bfloat16)

    for at, size in chunks:
        here = slice(at, at + size)
        hidden = jnp.tanh(jnp.dot(first_ref[...], views_ref[:, here], preferred_element_type=jnp.float32))
        keep_ref[:, here] = 1.0 - hidden[:inner] * hidden[:inner]
        hi, lo = halves(hidden)
        both = jnp.dot(second_ref[...], hi, preferred_element_type=jnp.float32)
        small = jnp.dot(second_ref[0:48], lo, preferred_element_type=jnp.float32)
        mixed_ref[:, here] = both[:48] + both[48:] + small

    logits = offset_ref[0] + mixed_ref[16:32] + pltpu.roll(mixed_ref[0:16], 1, 1) + pltpu.roll(mixed_ref[32:48], WIDE - 1, 1)
    resist = 1.0 / (1.0 + jnp.exp(-logits))
    resist_ref[...] = resist[:8, :width]
    slot = lax.broadcasted_iota(jnp.int32, (16, WIDE), 0)
    n = jnp.where(slot < 8, slot, jnp.where(slot < 10, slot - 10, slot - 2))
    use = in_grid & (m >= -2) & (m < width + 2) & (slot < 12) & (row0 + n >= 0) & (row0 + n < rows)
    slope = jnp.where(use, (resist - target) * (TILE / cols), 0.0)
    grid_col = in_grid.astype(jnp.float32)
    for dx in range(3):
        moved = (slope if dx == 1 else pltpu.roll(slope, (dx - 1) % WIDE, 1)) * grid_col
        hi, lo = halves(moved)
        spread_ref[16 * dx : 16 * dx + 16] = hi
        spread_ref[48 + 16 * dx : 64 + 16 * dx] = hi
        spread_ref[96 + 16 * dx : 112 + 16 * dx] = lo

    for at, size in chunks:
        here = slice(at, at + size)
        hidden_grad = jnp.dot(second_back_ref[...], spread_ref[:, here], preferred_element_type=jnp.float32)
        hi, lo = halves(hidden_grad * keep_ref[:, here])
        both = jnp.dot(first_back_ref[...], hi, preferred_element_type=jnp.float32)
        small = jnp.dot(first_back_ref[0:32], lo, preferred_element_type=jnp.float32)
        summed_ref[:, here] = both[:32] + both[32:] + small
    grad = summed_ref[8:16] + pltpu.roll(summed_ref[0:8], WIDE - 1, 1) + pltpu.roll(summed_ref[16:24], 1, 1)
    for copy in copies:
        copy.wait()
    grad = jnp.concatenate([grad[:, t * TILE : (t + 1) * TILE] for t in range(4)], 0)
    grad = jnp.concatenate([grad, grad], 1) * 2.0
    half = back_ref.shape[0] // 2
    for i in range(3):
        piece = jnp.concatenate([fields_ref[8 * i + j] * (grad * weights_ref[8 * i + j]) for j in range(8)], 0)
        hi, lo = halves(piece)
        sides = (((1,), (1,)), ((), ()))
        both = lax.dot_general(back_ref[...], hi, sides, preferred_element_type=jnp.float32)
        small = lax.dot_general(back_ref[0:half], lo, sides, preferred_element_type=jnp.float32)
        all_ref[:, 256 * i : 256 * i + 256] = both[:half] + both[half:] + small
    low = lax.broadcasted_iota(jnp.int32, (8, 384), 0) < 4
    for d in range(32):
        first, second = all_ref[8 * d : 8 * d + 8, 0:384], all_ref[8 * d : 8 * d + 8, 384:768]
        even, odd = jnp.where(low, first, pltpu.roll(second, 4, 0)), jnp.where(low, pltpu.roll(first, 4, 0), second)
        for b in range(3):
            out_ref[2 * d, 8 * b : 8 * b + 8] = even[:, BAND * b : BAND * (b + 1)]
            out_ref[2 * d + 1, 8 * b : 8 * b + 8] = odd[:, BAND * b : BAND * (b + 1)]


def resist_block(field, target, left, right, tables, second_bias, weights, fields, back, dims):
    rows, cols = dims
    inner, width = tables[2].shape[0], field.shape[1]
    return pl.pallas_call(
        functools.partial(resist_kernel, rows=rows, cols=cols),
        out_shape=[jax.ShapeDtypeStruct((8, width), jnp.float32), jax.ShapeDtypeStruct((64, 24, BAND), jnp.float32)],
        in_specs=[VMEM] * 8 + [SMEM, VMEM] + [HERE] * 2,
        out_specs=[VMEM] * 2,
        scratch_shapes=[
            pltpu.SMEM(weights.shape, jnp.float32),
            pltpu.VMEM(back.shape, jnp.bfloat16),
            pltpu.VMEM((160, WIDE), jnp.bfloat16),
            pltpu.VMEM((inner, WIDE), jnp.float32),
            pltpu.VMEM((48, WIDE), jnp.float32),
            pltpu.VMEM((144, WIDE), jnp.bfloat16),
            pltpu.VMEM((32, WIDE), jnp.float32),
            pltpu.VMEM((256, 768), jnp.float32),
            pltpu.SemaphoreType.DMA((2,)),
        ],
        compiler_params=params(28),
        name="resist",
    )(field, target, left, right, *tables, second_bias, *near(fields), *homes(weights, back))


def analyse_kernel(layout_any, table_any, out_ref, layout_ref, table_ref, sems):
    for copy in fetch((layout_any, table_any), (layout_ref, table_ref), sems):
        copy.wait()
    x = layout_ref[...].astype(jnp.float32)
    x = jnp.concatenate([x[:, t * TILE : (t + 1) * TILE] for t in range(4)], 0).astype(jnp.bfloat16)
    sums = dot(x, table_ref[0:TILE]) + dot(x, table_ref[TILE:])
    lane = lax.broadcasted_iota(jnp.int32, (8, BAND), 1)
    last = jnp.zeros((8, BAND), jnp.float32)
    for t in range(4):
        last = jnp.where(lane == t, sums[8 * t : 8 * t + 8, BAND:], last)
    packed = jnp.concatenate([sums[:, :BAND], last], 0)
    for i in range(out_ref.shape[0]):
        out_ref[i] = packed


def fields_kernel(*refs, rows, norm):
    slabs, refs = refs[:8], refs[8:]
    (
        target_ref, above_ref, below_ref, rows_any, expand_any, line_any, weights_any, synth_any, real_any, imag_any,
        cols_ref, fields_ref, intensity_ref, wanted_ref, first_edge_ref, last_edge_ref, *refs
    ) = refs
    (
        rows_ref, expand_ref, line_ref, weights_ref, synth_ref, real_ref, imag_ref,
        spec_ref, seen_ref, line_hi_ref, line_lo_ref, sum_ref, sems
    ) = refs
    at = 2 * lax.axis_index("y") + lax.axis_index("core")
    r = lax.axis_index(ROW)
    sources = [rows_any.at[at], expand_any, line_any.at[r], weights_any, synth_any]
    targets = [rows_ref, expand_ref, line_ref, weights_ref, synth_ref]
    for i in range(0, real_ref.shape[0], 4):
        sources += [real_any.at[i : i + 4], imag_any.at[i : i + 4]]
        targets += [real_ref.at[i : i + 4], imag_ref.at[i : i + 4]]
    copies = fetch(sources, targets, sems)
    row0 = r * 8
    kernels = real_ref.shape[0]
    for p, slab in enumerate(slabs):
        for t in range(5):
            hi, lo = halves(slab[:, 8 * t : 8 * t + 8, :].reshape(64, BAND))
            seen_ref[64 * p : 64 * p + 64, t * BAND : (t + 1) * BAND] = hi
            seen_ref[rows + 64 * p : rows + 64 * p + 64, t * BAND : (t + 1) * BAND] = lo
    copies[0].wait()
    table_hi = rows_ref[0 : 2 * BAND]
    u = dot(table_hi, seen_ref[0:rows]) + dot(rows_ref[2 * BAND :], seen_ref[0:rows]) + dot(table_hi, seen_ref[rows:])

    def pair(t):
        both = u[:, t * BAND : (t + 1) * BAND]
        return halves(jnp.concatenate([both[:BAND], both[BAND:]], 1))

    copies[1].wait()
    lane = lax.broadcasted_iota(jnp.int32, (BAND, 2 * BAND), 1)
    last = u[:, 4 * BAND :] * norm
    for t in range(4):
        hi, lo = pair(t)
        moved = pltpu.roll(last, (BAND - t) % BAND, 1)
        moved = jnp.concatenate([moved[:BAND], -moved[BAND:]], 1)
        spec_ref[t] = dot(hi, expand_ref[...]) + dot(lo, expand_ref[...]) + jnp.where((lane == 0) | (lane == BAND), moved, 0.0)

    copies[2].wait()
    phase = line_ref[...]
    c, s = phase[:, :BAND], phase[:, BAND:]
    table = jnp.concatenate([jnp.concatenate([c, -s], 1), jnp.concatenate([s, c], 1)], 0)
    lines_hi, lines_lo = halves(table)
    lines_both = jnp.concatenate([lines_hi, lines_lo], 0)
    sum_ref[...] = jnp.zeros_like(sum_ref)

    def lines(k, slot, j):
        kr, ki = real_ref[k], imag_ref[k]
        pieces = []
        for p in range(2):
            columns = []
            for t in (2 * p, 2 * p + 1):
                sr, si = spec_ref[t, :, :BAND], spec_ref[t, :, BAND:]
                columns.append(jnp.concatenate([kr * sr - ki * si, kr * si + ki * sr], 0))
            hi, lo = halves(jnp.concatenate(columns, 1))
            both = dot(lines_both, hi)
            out = both[:32] + both[32:] + dot(lines_hi, lo)
            for t in range(2):
                pieces.append(jnp.concatenate([out[:16, t * BAND : (t + 1) * BAND], out[16:, t * BAND : (t + 1) * BAND]], 1))
        hi, lo = halves(jnp.concatenate(pieces, 0))
        line_hi_ref[slot, 64 * j : 64 * j + 64] = hi
        line_lo_ref[slot, 64 * j : 64 * j + 64] = lo

    def waves(k0, slot, q):
        here = slice(q * 256, q * 256 + 256)
        synth_hi = synth_ref[0 : 2 * BAND, here]
        line_hi = line_hi_ref[slot]
        f = dot(line_hi, synth_hi) + dot(line_lo_ref[slot], synth_hi) + dot(line_hi, synth_ref[2 * BAND :, here])
        total = sum_ref[:, here]
        for j in range(4):
            part = f[64 * j : 64 * j + 64]
            total = total + weights_ref[k0 + j] * (part * part)
            fields_ref[k0 + j, :, here] = jnp.concatenate([part[16 * t : 16 * t + 8] for t in range(4)], 0)
        sum_ref[:, here] = total

    for copy in copies[5:7]:
        copy.wait()
    for j in range(4):
        lines(j, 0, j)
    for copy in copies[3:5]:
        copy.wait()
    for i in range(kernels // 4):
        for copy in copies[7 + 2 * i : 9 + 2 * i]:
            copy.wait()
        for j in range(4):
            waves(4 * i, i % 2, j)
            if 4 * i + 4 < kernels:
                lines(4 * i + 4 + j, (i + 1) % 2, j)
    row = lax.broadcasted_iota(jnp.int32, (16, 2 * BAND), 0)
    lane = lax.broadcasted_iota(jnp.int32, (16, 2 * BAND), 1)
    chosen = ((row < 4) & (lane == 2 * r + row % 2 + BAND * (row // 2))).astype(jnp.bfloat16)
    for t in range(4):
        hi, lo = halves(spec_ref[t])
        sides = (((1,), (1,)), ((), ()))
        picked = lax.dot_general(chosen, hi, sides, preferred_element_type=jnp.float32)
        cols_ref[t] = (picked + lax.dot_general(chosen, lo, sides, preferred_element_type=jnp.float32))[:8]
    slot = lax.broadcasted_iota(jnp.int32, (16, TILE), 0)
    n = row0 + jnp.where(slot < 8, slot, jnp.where(slot < 12, slot - 12, slot - 4))
    inside = (n >= 0) & (n < rows)
    for t in range(4):
        both = sum_ref[16 * t : 16 * t + 16]
        intensity_ref[:, t * TILE : (t + 1) * TILE] = jnp.where(inside, both[:, :TILE] + both[:, TILE:], 0.0)
    wanted_ref[0:8] = target_ref[...].astype(jnp.float32)
    above, below = above_ref[...].astype(jnp.float32), below_ref[...].astype(jnp.float32)
    wanted_ref[8:16] = jnp.concatenate([above[6:8], below[0:2], jnp.zeros((4, above.shape[1]), jnp.float32)], 0)
    width = intensity_ref.shape[1]
    for i, ref in ((0, intensity_ref), (16, wanted_ref)):
        first_edge_ref[i : i + 16] = ref[:, 0:BAND]
        last_edge_ref[i : i + 16] = ref[:, width - BAND :]


def adjoint_tables():
    wide = phase_angles(8 * np.arange(64), FREQ)
    c, s = np.cos(wide), np.sin(wide)
    w = np.concatenate([np.concatenate([c, -s], 1), np.concatenate([s, c], 1)], 0)
    near_rows = phase_angles(np.arange(8), FREQ)
    return np.concatenate(constant_split(w), 0), np.concatenate([np.cos(near_rows), np.sin(near_rows)], 0).astype(np.float32)


def adjoint_kernel(got_ref, columns_ref, table_any, turn_any, out_ref, table_ref, turn_ref, sems):
    for copy in fetch((table_any, turn_any), (table_ref, turn_ref), sems):
        copy.wait()
    table_hi, table_lo = table_ref[0:BAND], table_ref[BAND:]
    c, s = turn_ref[0:8], turn_ref[8:16]
    for g in range(2):
        turned = []
        for t in range(4):
            re, im = columns_ref[t, g : g + 1], columns_ref[t, 2 + g : 3 + g]
            turned.append((c * re - s * im, s * re + c * im))
        a, b = (jnp.concatenate([x[i] for x in turned], 0)[None] for i in range(2))
        for h in range(2):
            at = 4 * h + 2 * g
            x = [[got_ref[pl.ds(8 * b + at + i, 64, stride=24), :] for b in range(3)] for i in range(2)]
            x = jnp.concatenate([jnp.concatenate(part, 1) for part in x], 0)
            hi, lo = halves(x)
            sides = (((0,), (0,)), ((), ()))
            y = lax.dot_general(hi, table_hi, sides, preferred_element_type=jnp.float32)
            y = y + lax.dot_general(lo, table_hi, sides, preferred_element_type=jnp.float32)
            y = y + lax.dot_general(hi, table_lo, sides, preferred_element_type=jnp.float32)
            y = y.reshape(12, 32, 2 * BAND)
            re, im = y[:, :, :BAND], y[:, :, BAND:]
            out_ref[0, g, 12 * h : 12 * h + 12] = jnp.sum(re * a + im * b, 1)
            out_ref[1, g, 12 * h : 12 * h + 12] = jnp.sum(im * a - re * b, 1)


def total_kernel(x_ref, one_ref, two_ref, three_ref, whole_ref, square_ref):
    whole = (x_ref[...] + two_ref[...]) + (one_ref[...] + three_ref[...])
    whole_ref[...] = whole
    flat = jnp.sum(whole * whole, (0, 1, 2))[None]
    square_ref[...] = jnp.broadcast_to(flat[None], square_ref.shape)


def scale_kernel(whole_ref, squares_ref, out_ref, *, entries):
    total = jnp.sum(jnp.sum(squares_ref[...], 0), 1, keepdims=True)
    factor = lax.rsqrt(total / entries + 1e-06)
    for i in range(2):
        for g in range(2):
            out_ref[i, :, g, :] = whole_ref[i, g] * factor


def fields_block(slabs, synth, kernel_real, kernel_imaginary, weights, target, above, below, norm):
    kernels = kernel_real.shape[0]
    height, width = target.shape
    tiles, rows = width // TILE, 64 * height
    return pl.pallas_call(
        functools.partial(fields_kernel, rows=rows, norm=norm),
        out_shape=[
            jax.ShapeDtypeStruct((tiles, 8, BAND), jnp.float32),
            pltpu.VMEM((kernels, tiles * height, 2 * TILE), jnp.float32),
            jax.ShapeDtypeStruct((16, width), jnp.float32),
            jax.ShapeDtypeStruct((16, width), jnp.float32),
            jax.ShapeDtypeStruct((32, BAND), jnp.float32),
            jax.ShapeDtypeStruct((32, BAND), jnp.float32),
        ],
        in_specs=[VMEM] * 11 + [HERE] * 7,
        out_specs=[VMEM] * 6,
        scratch_shapes=[
            pltpu.VMEM((4 * BAND, rows), jnp.bfloat16),
            pltpu.VMEM((2 * BAND, 2 * BAND), jnp.bfloat16),
            pltpu.VMEM((16, 2 * BAND), jnp.float32),
            pltpu.SMEM(weights.shape, jnp.float32),
            pltpu.VMEM((4 * BAND, 2 * TILE), jnp.bfloat16),
            pltpu.VMEM(kernel_real.shape, jnp.float32),
            pltpu.VMEM(kernel_real.shape, jnp.float32),
            pltpu.VMEM((tiles, BAND, 2 * BAND), jnp.float32),
            pltpu.VMEM((2 * rows, 5 * BAND), jnp.bfloat16),
            pltpu.VMEM((2, 256, 2 * BAND), jnp.bfloat16),
            pltpu.VMEM((2, 256, 2 * BAND), jnp.bfloat16),
            pltpu.VMEM((64, 2 * TILE), jnp.float32),
            pltpu.SemaphoreType.DMA((5 + kernels // 2,)),
        ],
        compiler_params=params(28),
        name="fields",
    )(
        *near(*slabs, target, above, below),
        *homes(
            row_transform_tables(), expand_table(norm), line_tables(64, height), weights,
            np.concatenate(constant_split(synth), 0), kernel_real, kernel_imaginary,
        ),
    )


def on_device(
    layout, target, kernel_real, kernel_imaginary, weights, first_taps, first_bias, second_taps, second_bias
):
    height, width = layout.shape
    tiles = width // TILE
    kernels = kernel_real.shape[0]
    rows, cols = height * 64, width * 4
    r = lax.axis_index(ROW)
    norm = 1.0 / math.sqrt(rows * TILE)

    above = lax.ppermute(target, ROW, [(i, i + 1) for i in range(63)])
    below = lax.ppermute(target, ROW, [(i + 1, i) for i in range(63)])

    packed = pl.pallas_call(
        analyse_kernel,
        out_shape=jax.ShapeDtypeStruct((8, 40, BAND), jnp.float32),
        in_specs=[HERE] * 2,
        out_specs=VMEM,
        scratch_shapes=[
            pltpu.VMEM(layout.shape, jnp.bfloat16),
            pltpu.VMEM((2 * TILE, 2 * BAND), jnp.bfloat16),
            pltpu.SemaphoreType.DMA((2,)),
        ],
        compiler_params=params(8),
        name="analyse",
    )(*homes(layout, analysis_table()))
    gathered = lax.all_to_all(packed, "z", 0, 0, tiled=True)
    tables = resist_tables(first_taps, first_bias, second_taps, rows)
    gathered, above, below, *tables = lax.optimization_barrier((gathered, above, below, *tables))
    slabs = [gathered] + [lax.ppermute(gathered, "y", [(i, (i + k) % 4) for i in range(4)]) for k in (1, 2, 3)]
    slabs = slabs + [lax.ppermute(slab, "core", [(0, 1), (1, 0)]) for slab in slabs]

    synth = synthesis_table(norm)
    columns, fields, intensity, wanted, first_edge, last_edge = fields_block(
        slabs, synth, kernel_real, kernel_imaginary, weights, target, above, below, norm
    )
    left = lax.ppermute(last_edge, "x", [(i, i + 1) for i in range(3)])
    right = lax.ppermute(first_edge, "x", [(i + 1, i) for i in range(3)])
    back = synth.reshape(2, 64, 2, 2 * TILE).transpose(1, 2, 0, 3).reshape(256, 2 * TILE)
    back = np.concatenate(constant_split(back), 0)
    resist, send = resist_block(
        intensity, wanted, left, right, tables, second_bias, weights, fields, back, (rows, cols)
    )

    got = lax.all_to_all(send, ROW, 0, 0, tiled=True)
    table, turn = adjoint_tables()
    mine = pl.pallas_call(
        adjoint_kernel,
        out_shape=jax.ShapeDtypeStruct((2, 2, kernels, BAND), jnp.float32),
        in_specs=[VMEM] * 2 + [HERE] * 2,
        out_specs=VMEM,
        scratch_shapes=[
            pltpu.VMEM(table.shape, jnp.bfloat16),
            pltpu.VMEM(turn.shape, jnp.float32),
            pltpu.SemaphoreType.DMA((2,)),
        ],
        compiler_params=params(12),
        name="adjoint",
    )(*near(got.reshape(64 * 24, BAND), columns), *homes(table, turn))
    others = [lax.ppermute(mine, "x", [(i, (i + k) % 4) for i in range(4)]) for k in (1, 2, 3)]
    whole, squares = pl.pallas_call(
        total_kernel,
        out_shape=[jax.ShapeDtypeStruct(mine.shape, jnp.float32), jax.ShapeDtypeStruct((64, 1, BAND), jnp.float32)],
        in_specs=[VMEM] * 4,
        out_specs=[VMEM] * 2,
        compiler_params=params(8),
        name="total",
    )(mine, *others)
    squares = lax.all_to_all(squares, ROW, 0, 0, tiled=True)
    grads = pl.pallas_call(
        functools.partial(scale_kernel, entries=2 * kernels * BAND * BAND),
        out_shape=jax.ShapeDtypeStruct((2, kernels, 2, BAND), jnp.float32),
        in_specs=[VMEM] * 2,
        out_specs=VMEM,
        compiler_params=params(8),
        name="scale",
    )(whole, squares)
    return resist, grads.transpose(0, 1, 3, 2)


def solution(mesh):
    devices = mesh.devices.reshape(4, 8, 2, 4)
    fine = Mesh(devices, ALL)
    grid = P(ROW, "x")
    in_specs = (grid, grid, P(), P(), P(), P(), P(), P(), P())
    out_specs = (grid, P(None, None, None, ROW))
    return jax.shard_map(on_device, mesh=fine, in_specs=in_specs, out_specs=out_specs, check_vma=False)
```

```python
import functools
import math

import jax
import jax.numpy as jnp
import numpy as np
from jax import lax
from jax.experimental import pallas as pl
from jax.experimental.pallas import tpu as pltpu
from jax.sharding import Mesh, PartitionSpec as P

TILE = 512
BAND = 128
ROW = ("y", "z", "core")
ALL = ("y", "z", "core", "x")


def phase_angles(freqs, positions):
    return 2.0 * math.pi * ((freqs[:, None] * positions[None, :]) % TILE) / TILE


def dot(a, b):
    return jnp.dot(a, b, preferred_element_type=jnp.float32)


def constant_split(x):
    x = np.asarray(x, np.float32)
    hi = x.astype(jnp.bfloat16)
    return hi, (x - hi.astype(np.float32)).astype(jnp.bfloat16)


VMEM = pl.BlockSpec(memory_space=pltpu.VMEM)
SMEM = pl.BlockSpec(memory_space=pltpu.SMEM)
HERE = pl.BlockSpec(memory_space=pltpu.HBM)


def near(*arrays):
    return [pltpu.with_memory_space_constraint(jnp.asarray(x), pltpu.VMEM) for x in arrays]


def homes(*arrays):
    return [pltpu.with_memory_space_constraint(jnp.asarray(x), pltpu.HBM) for x in arrays]


def fetch(sources, targets, sems):
    copies = [pltpu.make_async_copy(a, b, sems.at[i]) for i, (a, b) in enumerate(zip(sources, targets, strict=True))]
    for copy in copies:
        copy.start()
    return copies


def params(mib):
    return pltpu.CompilerParams(vmem_limit_bytes=mib * 1024 * 1024)


FREQ = np.arange(BAND) - BAND // 2


def analysis_table():
    ang = phase_angles(np.arange(65), np.arange(TILE))
    table = np.zeros((TILE, 2 * BAND))
    table[:, :64], table[:, 64:BAND] = np.cos(ang[:64]).T, np.sin(ang[1:]).T
    table[:, BAND : BAND + 4] = np.cos(ang[64])[:, None]
    return np.concatenate(constant_split(table), 0)


def row_transform_tables():
    tables = []
    for y in range(4):
        for core in range(2):
            slabs = [128 * ((y - k) % 4) + 8 * (core ^ other) for other in range(2) for k in range(4)]
            n = (np.array(slabs)[:, None, None] + 16 * np.arange(8)[:, None] + np.arange(8)).reshape(-1)
            ang = phase_angles(FREQ, n)
            tables.append(np.concatenate(constant_split(np.concatenate([np.cos(ang), np.sin(ang)], 0)), 0))
    return np.stack(tables)


def expand_table(norm):
    table = np.zeros((2, BAND, 2, BAND))
    for g in range(BAND):
        q = g - 64
        m = abs(q)
        if m < 64:
            table[0, m, 0, g] = 1.0
            table[1, m, 1, g] = -1.0
        if m:
            sign = -1.0 if q > 0 else 1.0
            table[1, 63 + m, 0, g] = sign
            table[0, 63 + m, 1, g] = sign
    return (table.reshape(2 * BAND, 2 * BAND) * norm).astype(jnp.bfloat16)


def synthesis_table(norm):
    ang = phase_angles(FREQ, np.arange(TILE))
    c, s = np.cos(ang), np.sin(ang)
    return np.concatenate([np.concatenate([c, s], 1), np.concatenate([-s, c], 1)], 0) * norm


def line_tables(groups, height):
    at = np.arange(groups)[:, None] * height + np.array(FIELD_ROWS)[None, :]
    ang = phase_angles(at.reshape(-1), FREQ)
    return np.concatenate([np.cos(ang), np.sin(ang)], 1).reshape(groups, 16, 2 * BAND).astype(np.float32)


FIELD_ROWS = list(range(8)) + [-4, -3, -2, -1, 8, 9, 10, 11]
HIDDEN_ROWS = list(range(-1, 9)) + [-3, -2, 9, 10]
SLOPE_ROWS = list(range(8)) + [-2, -1, 8, 9] + [None] * 4
WIDE = 17 * 128


def halves(x):
    hi = x.astype(jnp.bfloat16)
    return hi, (x - hi.astype(jnp.float32)).astype(jnp.bfloat16)


def pick(out_rows, in_rows, sign):
    hit = lambda a, b, dy: float(a is not None and b is not None and b - a == sign * (dy - 1))
    return np.array([[[hit(a, b, dy) for b in in_rows] for a in out_rows] for dy in range(3)])


INNER = HIDDEN_ROWS[:10]
CHANNELS = 64


def choose_tables():
    choose = np.zeros((3, 48, 7, 256))
    for dy in range(3):
        for dx in range(3):
            for slot in range(16):
                lane = 16 * dx + slot
                for part, section in ((0, 0), (1, 1), (0, 2)):
                    choose[part, 3 * dy + dx, dy, 48 * section + lane] = 1.0
                    choose[part, 16 + 3 * dy + dx, 4 + dy, 48 * section + lane] = 1.0
    for part in range(3):
        choose[part, 32, 3, 144 + part] = 1.0
    return choose.reshape(144, 7 * 256).astype(jnp.bfloat16)


def lane_masks():
    fore = pick(HIDDEN_ROWS, FIELD_ROWS, 1).transpose(1, 0, 2)
    back = pick(INNER, SLOPE_ROWS, -1).transpose(1, 0, 2)
    masks = np.zeros((80, 256), np.float32)
    masks[:42, :144] = np.tile(fore, (1, 1, 9)).reshape(42, 144)
    masks[42:72, :144] = np.tile(back, (1, 1, 9)).reshape(30, 144)
    return masks


def row_masks():
    fore = np.repeat(pick(SLOPE_ROWS, HIDDEN_ROWS, 1), CHANNELS, 2)
    back = np.repeat(pick(list(range(8)), INNER, -1), CHANNELS, 2)
    return fore.astype(np.float32), back.astype(np.float32)


def tables_kernel(
    first_taps_any, second_taps_any, bias_any, choose_any, lane_masks_any, fore_any, aft_any,
    first_ref, second_ref, second_back_ref, first_back_ref,
    first_taps_ref, second_taps_ref, bias_ref, choose_ref, lane_masks_ref, fore_ref, aft_ref, wide_ref, sems, *, rows
):
    sources = (first_taps_any, second_taps_any, bias_any, choose_any, lane_masks_any, fore_any, aft_any)
    targets = (first_taps_ref, second_taps_ref, bias_ref, choose_ref, lane_masks_ref, fore_ref, aft_ref)
    for copy in fetch(sources, targets, sems):
        copy.wait()
    row0 = lax.axis_index(ROW) * 8
    wide_ref[...] = jnp.zeros_like(wide_ref)
    wide_ref[0:9, 0:CHANNELS] = first_taps_ref[...]
    wide_ref[16:25, 0:CHANNELS] = second_taps_ref[...]
    wide_ref[32:33, 0:CHANNELS] = bias_ref[...]
    tall = wide_ref[...].T[:CHANNELS, :48]
    hi = tall.astype(jnp.bfloat16)
    rest = tall - hi.astype(jnp.float32)
    mid = rest.astype(jnp.bfloat16)
    low = (rest - mid.astype(jnp.float32)).astype(jnp.bfloat16)
    parts = dot(jnp.concatenate([hi, mid, low], 1), choose_ref[...])
    for h, n in enumerate(HIDDEN_ROWS):
        here = row0 + n
        valid = jnp.where((here >= 0) & (here < rows), 1.0, 0.0)
        block = parts[:, 768:1024]
        for dy in range(3):
            block = block + parts[:, 256 * dy : 256 * dy + 256] * lane_masks_ref[3 * h + dy : 3 * h + dy + 1]
        first_ref[64 * h : 64 * h + 64] = (block * valid)[:, :160].astype(jnp.bfloat16)
        if h < 10:
            block = 0.0
            for dy in range(3):
                at = 1024 + 256 * dy
                block = block + parts[:, at : at + 256] * lane_masks_ref[42 + 3 * h + dy : 43 + 3 * h + dy]
            second_back_ref[64 * h : 64 * h + 64] = (block * valid)[:, :144].astype(jnp.bfloat16)
    for taps_ref, mask_ref, out_ref, height in ((second_taps_ref, fore_ref, second_ref, 16), (first_taps_ref, aft_ref, first_back_ref, 8)):
        lanes = out_ref.shape[1]
        taps = taps_ref[...]
        taps = jnp.concatenate([taps] * (lanes // CHANNELS), 1)
        taps_hi = taps.astype(jnp.bfloat16).astype(jnp.float32)
        for at, part in ((0, taps_hi), (out_ref.shape[0] // 2, taps - taps_hi)):
            blocks = []
            for dx in range(3):
                block = 0.0
                for dy in range(3):
                    block = block + part[3 * dy + dx : 3 * dy + dx + 1] * mask_ref[dy]
                blocks.append(block)
            if height == 8:
                blocks.append(jnp.zeros((8, lanes), jnp.float32))
            whole = jnp.concatenate(blocks, 0)
            out_ref[at : at + whole.shape[0]] = whole.astype(jnp.bfloat16)


def resist_tables(first_taps, first_bias, second_taps, rows):
    args = (first_taps, second_taps, first_bias.reshape(1, -1), choose_tables(), lane_masks(), *row_masks())
    return pl.pallas_call(
        functools.partial(tables_kernel, rows=rows),
        out_shape=[
            jax.ShapeDtypeStruct((14 * CHANNELS, 160), jnp.bfloat16),
            jax.ShapeDtypeStruct((96, 14 * CHANNELS), jnp.bfloat16),
            jax.ShapeDtypeStruct((10 * CHANNELS, 144), jnp.bfloat16),
            jax.ShapeDtypeStruct((64, 10 * CHANNELS), jnp.bfloat16),
        ],
        in_specs=[HERE] * 7,
        out_specs=[VMEM] * 4,
        scratch_shapes=[pltpu.VMEM(a.shape, a.dtype) for a in args]
        + [pltpu.VMEM((BAND, BAND), jnp.float32), pltpu.SemaphoreType.DMA((7,))],
        compiler_params=params(12),
        name="tables",
    )(*homes(*args))


def resist_kernel(
    field_ref, target_ref, left_ref, right_ref, first_ref, second_ref, second_back_ref, first_back_ref, offset_ref,
    fields_ref, weights_any, back_any,
    resist_any, out_ref, resist_ref, weights_ref, back_ref,
    views_ref, keep_ref, mixed_ref, spread_ref, summed_ref, all_ref, sems, *, rows, cols
):
    copies = fetch((weights_any, back_any), (weights_ref, back_ref), sems)
    row0 = lax.axis_index(ROW) * resist_ref.shape[0]
    col0 = lax.axis_index("x") * resist_ref.shape[1]
    width = resist_ref.shape[1]
    inner = keep_ref.shape[0]

    def columns(shape):
        lane = lax.broadcasted_iota(jnp.int32, shape, 1)
        m = jnp.where(lane < width + 64, lane, lane - WIDE)
        return m, (col0 + m >= 0) & (col0 + m < cols)

    def sweep(step, times, size):
        lax.fori_loop(0, width // size, lambda i, c: (step(pl.ds(pl.multiple_of(i * size, size), size)), c)[1], 0, unroll=times)
        step(slice(width, WIDE))

    m, in_grid = columns((16, WIDE))
    keep_col = (in_grid & (m >= -3) & (m < width + 3)).astype(jnp.float32)
    lane = lax.broadcasted_iota(jnp.int32, (16, BAND), 1)
    gap = [jnp.where(lane < 64, right_ref[i : i + 16], left_ref[i : i + 16]) for i in (0, 16)]
    field = jnp.concatenate([field_ref[...], gap[0]], 1)
    target = jnp.concatenate([target_ref[...], gap[1]], 1)
    for dx in range(3):
        moved = (field if dx == 1 else pltpu.roll(field, (1 - dx) % WIDE, 1)) * keep_col
        hi, lo = halves(moved)
        views_ref[16 * dx : 16 * dx + 16] = hi
        views_ref[48 + 16 * dx : 64 + 16 * dx] = hi
        views_ref[96 + 16 * dx : 112 + 16 * dx] = lo
    views_ref[144:160] = keep_col.astype(jnp.bfloat16)

    def forward(here):
        hidden = jnp.tanh(jnp.dot(first_ref[...], views_ref[:, here], preferred_element_type=jnp.float32))
        keep_ref[:, here] = 1.0 - hidden[:inner] * hidden[:inner]
        hi, lo = halves(hidden)
        both = jnp.dot(second_ref[...], hi, preferred_element_type=jnp.float32)
        small = jnp.dot(second_ref[0:48], lo, preferred_element_type=jnp.float32)
        mixed_ref[:, here] = both[:48] + both[48:] + small

    sweep(forward, 4, 256)
    logits = offset_ref[0] + mixed_ref[16:32] + pltpu.roll(mixed_ref[0:16], 1, 1) + pltpu.roll(mixed_ref[32:48], WIDE - 1, 1)
    resist = 1.0 / (1.0 + jnp.exp(-logits))
    resist_ref[...] = resist[:8, :width]
    sent = pltpu.make_async_copy(resist_ref, resist_any, sems.at[2])
    sent.start()
    slot = lax.broadcasted_iota(jnp.int32, (16, WIDE), 0)
    n = jnp.where(slot < 8, slot, jnp.where(slot < 10, slot - 10, slot - 2))
    use = in_grid & (m >= -2) & (m < width + 2) & (slot < 12) & (row0 + n >= 0) & (row0 + n < rows)
    slope = jnp.where(use, (resist - target) * (TILE / cols), 0.0)
    grid_col = in_grid.astype(jnp.float32)
    for dx in range(3):
        moved = (slope if dx == 1 else pltpu.roll(slope, (dx - 1) % WIDE, 1)) * grid_col
        hi, lo = halves(moved)
        spread_ref[16 * dx : 16 * dx + 16] = hi
        spread_ref[48 + 16 * dx : 64 + 16 * dx] = hi
        spread_ref[96 + 16 * dx : 112 + 16 * dx] = lo

    def backward(here):
        hidden_grad = jnp.dot(second_back_ref[...], spread_ref[:, here], preferred_element_type=jnp.float32)
        hi, lo = halves(hidden_grad * keep_ref[:, here])
        both = jnp.dot(first_back_ref[...], hi, preferred_element_type=jnp.float32)
        small = jnp.dot(first_back_ref[0:32], lo, preferred_element_type=jnp.float32)
        summed_ref[:, here] = both[:32] + both[32:] + small

    sweep(backward, 1, 1024)
    grad = summed_ref[8:16] + pltpu.roll(summed_ref[0:8], WIDE - 1, 1) + pltpu.roll(summed_ref[16:24], 1, 1)
    for copy in copies:
        copy.wait()
    grad = jnp.concatenate([grad[:, t * TILE : (t + 1) * TILE] for t in range(4)], 0)
    grad = jnp.concatenate([grad, grad], 1) * 2.0
    half = back_ref.shape[0] // 2
    for i in range(3):
        piece = jnp.concatenate([fields_ref[8 * i + j] * (grad * weights_ref[8 * i + j]) for j in range(8)], 0)
        hi, lo = halves(piece)
        sides = (((1,), (1,)), ((), ()))
        both = lax.dot_general(back_ref[...], hi, sides, preferred_element_type=jnp.float32)
        small = lax.dot_general(back_ref[0:half], lo, sides, preferred_element_type=jnp.float32)
        all_ref[:, 256 * i : 256 * i + 256] = both[:half] + both[half:] + small
    low = lax.broadcasted_iota(jnp.int32, (8, 384), 0) < 4
    for d in range(32):
        first, second = all_ref[8 * d : 8 * d + 8, 0:384], all_ref[8 * d : 8 * d + 8, 384:768]
        even, odd = jnp.where(low, first, pltpu.roll(second, 4, 0)), jnp.where(low, pltpu.roll(first, 4, 0), second)
        for b in range(3):
            out_ref[2 * d, 8 * b : 8 * b + 8] = even[:, BAND * b : BAND * (b + 1)]
            out_ref[2 * d + 1, 8 * b : 8 * b + 8] = odd[:, BAND * b : BAND * (b + 1)]
    sent.wait()


def resist_block(field, target, left, right, tables, second_bias, weights, fields, back, dims):
    rows, cols = dims
    inner, width = tables[2].shape[0], field.shape[1]
    return pl.pallas_call(
        functools.partial(resist_kernel, rows=rows, cols=cols),
        out_shape=[pltpu.HBM((8, width), jnp.float32), pltpu.VMEM((64, 24, BAND), jnp.float32)],
        in_specs=[VMEM] * 8 + [SMEM, VMEM] + [HERE] * 2,
        out_specs=[HERE, VMEM],
        scratch_shapes=[
            pltpu.VMEM((8, width), jnp.float32),
            pltpu.SMEM(weights.shape, jnp.float32),
            pltpu.VMEM(back.shape, jnp.bfloat16),
            pltpu.VMEM((160, WIDE), jnp.bfloat16),
            pltpu.VMEM((inner, WIDE), jnp.float32),
            pltpu.VMEM((48, WIDE), jnp.float32),
            pltpu.VMEM((144, WIDE), jnp.bfloat16),
            pltpu.VMEM((32, WIDE), jnp.float32),
            pltpu.VMEM((256, 768), jnp.float32),
            pltpu.SemaphoreType.DMA((3,)),
        ],
        compiler_params=params(28),
        name="resist",
    )(field, target, left, right, *tables, second_bias, *near(fields), *homes(weights, back))


def analyse_kernel(layout_any, table_any, out_ref, layout_ref, table_ref, sems):
    for copy in fetch((layout_any, table_any), (layout_ref, table_ref), sems):
        copy.wait()
    x = layout_ref[...].astype(jnp.float32)
    x = jnp.concatenate([x[:, t * TILE : (t + 1) * TILE] for t in range(4)], 0).astype(jnp.bfloat16)
    sums = dot(x, table_ref[0:TILE]) + dot(x, table_ref[TILE:])
    lane = lax.broadcasted_iota(jnp.int32, (8, BAND), 1)
    last = jnp.zeros((8, BAND), jnp.float32)
    for t in range(4):
        last = jnp.where(lane == t, sums[8 * t : 8 * t + 8, BAND:], last)
    packed = jnp.concatenate([sums[:, :BAND], last], 0)
    for i in range(out_ref.shape[0]):
        out_ref[i] = packed


def fields_kernel(*refs, rows, norm):
    slabs, refs = refs[:8], refs[8:]
    (
        above_ref, below_ref, rows_ref, expand_any, line_any, weights_any, synth_any, target_any, real_any, imag_any,
        cols_ref, fields_ref, intensity_ref, wanted_ref, first_edge_ref, last_edge_ref, *refs
    ) = refs
    (
        expand_ref, line_ref, weights_ref, synth_ref, target_ref, real_ref, imag_ref,
        spec_ref, seen_ref, line_hi_ref, line_lo_ref, sum_ref, sems
    ) = refs
    r = lax.axis_index(ROW)
    sources = [expand_any, line_any.at[r], weights_any, synth_any, target_any]
    targets = [expand_ref, line_ref, weights_ref, synth_ref, target_ref]
    for i in range(0, real_ref.shape[0], 4):
        sources += [real_any.at[i : i + 4], imag_any.at[i : i + 4]]
        targets += [real_ref.at[i : i + 4], imag_ref.at[i : i + 4]]
    copies = fetch(sources, targets, sems)
    row0 = r * 8
    kernels = real_ref.shape[0]
    for p, slab in enumerate(slabs):
        for t in range(5):
            hi, lo = halves(slab[:, 8 * t : 8 * t + 8, :].reshape(64, BAND))
            seen_ref[64 * p : 64 * p + 64, t * BAND : (t + 1) * BAND] = hi
            seen_ref[rows + 64 * p : rows + 64 * p + 64, t * BAND : (t + 1) * BAND] = lo
    table_hi = rows_ref[0 : 2 * BAND]
    u = dot(table_hi, seen_ref[0:rows]) + dot(rows_ref[2 * BAND :], seen_ref[0:rows]) + dot(table_hi, seen_ref[rows:])

    def pair(t):
        both = u[:, t * BAND : (t + 1) * BAND]
        return halves(jnp.concatenate([both[:BAND], both[BAND:]], 1))

    copies[0].wait()
    lane = lax.broadcasted_iota(jnp.int32, (BAND, 2 * BAND), 1)
    last = u[:, 4 * BAND :] * norm
    for t in range(4):
        hi, lo = pair(t)
        moved = pltpu.roll(last, (BAND - t) % BAND, 1)
        moved = jnp.concatenate([moved[:BAND], -moved[BAND:]], 1)
        spec_ref[t] = dot(hi, expand_ref[...]) + dot(lo, expand_ref[...]) + jnp.where((lane == 0) | (lane == BAND), moved, 0.0)

    copies[1].wait()
    phase = line_ref[...]
    c, s = phase[:, :BAND], phase[:, BAND:]
    table = jnp.concatenate([jnp.concatenate([c, -s], 1), jnp.concatenate([s, c], 1)], 0)
    lines_hi, lines_lo = halves(table)
    lines_both = jnp.concatenate([lines_hi, lines_lo], 0)
    sum_ref[...] = jnp.zeros_like(sum_ref)

    def lines(k, slot, j):
        kr, ki = real_ref[k], imag_ref[k]
        pieces = []
        for p in range(2):
            columns = []
            for t in (2 * p, 2 * p + 1):
                sr, si = spec_ref[t, :, :BAND], spec_ref[t, :, BAND:]
                columns.append(jnp.concatenate([kr * sr - ki * si, kr * si + ki * sr], 0))
            hi, lo = halves(jnp.concatenate(columns, 1))
            both = dot(lines_both, hi)
            out = both[:32] + both[32:] + dot(lines_hi, lo)
            for t in range(2):
                pieces.append(jnp.concatenate([out[:16, t * BAND : (t + 1) * BAND], out[16:, t * BAND : (t + 1) * BAND]], 1))
        hi, lo = halves(jnp.concatenate(pieces, 0))
        line_hi_ref[slot, 64 * j : 64 * j + 64] = hi
        line_lo_ref[slot, 64 * j : 64 * j + 64] = lo

    def waves(k0, slot, q):
        here = slice(q * 256, q * 256 + 256)
        synth_hi = synth_ref[0 : 2 * BAND, here]
        line_hi = line_hi_ref[slot]
        f = dot(line_hi, synth_hi) + dot(line_lo_ref[slot], synth_hi) + dot(line_hi, synth_ref[2 * BAND :, here])
        total = sum_ref[:, here]
        for j in range(4):
            part = f[64 * j : 64 * j + 64]
            total = total + weights_ref[k0 + j] * (part * part)
            fields_ref[k0 + j, :, here] = jnp.concatenate([part[16 * t : 16 * t + 8] for t in range(4)], 0)
        sum_ref[:, here] = total

    for copy in copies[5:7]:
        copy.wait()
    for j in range(4):
        lines(j, 0, j)
    for copy in copies[2:5]:
        copy.wait()
    for copy in copies[7:]:
        copy.wait()

    def group(i, slot, more):
        for j in range(4):
            waves(4 * i, slot, j)
            if more:
                lines(4 * i + 4 + j, 1 - slot, j)

    def both(m, carry):
        group(2 * m, 0, True)
        group(2 * m + 1, 1, True)
        return carry

    lax.fori_loop(0, 2, both, 0)
    group(4, 0, True)
    group(5, 1, False)
    row = lax.broadcasted_iota(jnp.int32, (16, 2 * BAND), 0)
    lane = lax.broadcasted_iota(jnp.int32, (16, 2 * BAND), 1)
    chosen = ((row < 4) & (lane == 2 * r + row % 2 + BAND * (row // 2))).astype(jnp.bfloat16)
    for t in range(4):
        hi, lo = halves(spec_ref[t])
        sides = (((1,), (1,)), ((), ()))
        picked = lax.dot_general(chosen, hi, sides, preferred_element_type=jnp.float32)
        cols_ref[t] = (picked + lax.dot_general(chosen, lo, sides, preferred_element_type=jnp.float32))[:8]
    slot = lax.broadcasted_iota(jnp.int32, (16, TILE), 0)
    n = row0 + jnp.where(slot < 8, slot, jnp.where(slot < 12, slot - 12, slot - 4))
    inside = (n >= 0) & (n < rows)
    for t in range(4):
        both = sum_ref[16 * t : 16 * t + 16]
        intensity_ref[:, t * TILE : (t + 1) * TILE] = jnp.where(inside, both[:, :TILE] + both[:, TILE:], 0.0)
    wanted_ref[0:8] = target_ref[...].astype(jnp.float32)
    above, below = above_ref[...].astype(jnp.float32), below_ref[...].astype(jnp.float32)
    wanted_ref[8:16] = jnp.concatenate([above[6:8], below[0:2], jnp.zeros((4, above.shape[1]), jnp.float32)], 0)
    width = intensity_ref.shape[1]
    for i, ref in ((0, intensity_ref), (16, wanted_ref)):
        first_edge_ref[i : i + 16] = ref[:, 0:BAND]
        last_edge_ref[i : i + 16] = ref[:, width - BAND :]


def adjoint_tables():
    wide = phase_angles(8 * np.arange(64), FREQ)
    c, s = np.cos(wide), np.sin(wide)
    w = np.concatenate([np.concatenate([c, -s], 1), np.concatenate([s, c], 1)], 0)
    near_rows = phase_angles(np.arange(8), FREQ)
    return np.concatenate(constant_split(w), 0), np.concatenate([np.cos(near_rows), np.sin(near_rows)], 0).astype(np.float32)


def adjoint_kernel(got_ref, columns_ref, table_any, turn_any, out_ref, table_ref, turn_ref, sems):
    for copy in fetch((table_any, turn_any), (table_ref, turn_ref), sems):
        copy.wait()
    table_hi, table_lo = table_ref[0:BAND], table_ref[BAND:]
    c, s = turn_ref[0:8], turn_ref[8:16]
    for g in range(2):
        turned = []
        for t in range(4):
            re, im = columns_ref[t, g : g + 1], columns_ref[t, 2 + g : 3 + g]
            turned.append((c * re - s * im, s * re + c * im))
        a, b = (jnp.concatenate([x[i] for x in turned], 0)[None] for i in range(2))
        for h in range(2):
            at = 4 * h + 2 * g
            x = [[got_ref[pl.ds(8 * b + at + i, 64, stride=24), :] for b in range(3)] for i in range(2)]
            x = jnp.concatenate([jnp.concatenate(part, 1) for part in x], 0)
            hi, lo = halves(x)
            sides = (((0,), (0,)), ((), ()))
            y = lax.dot_general(hi, table_hi, sides, preferred_element_type=jnp.float32)
            y = y + lax.dot_general(lo, table_hi, sides, preferred_element_type=jnp.float32)
            y = y + lax.dot_general(hi, table_lo, sides, preferred_element_type=jnp.float32)
            y = y.reshape(12, 32, 2 * BAND)
            re, im = y[:, :, :BAND], y[:, :, BAND:]
            out_ref[0, g, 12 * h : 12 * h + 12] = jnp.sum(re * a + im * b, 1)
            out_ref[1, g, 12 * h : 12 * h + 12] = jnp.sum(im * a - re * b, 1)


def total_kernel(x_ref, one_ref, two_ref, three_ref, whole_ref, square_ref):
    whole = (x_ref[...] + two_ref[...]) + (one_ref[...] + three_ref[...])
    whole_ref[...] = whole
    flat = jnp.sum(whole * whole, (0, 1, 2))[None]
    square_ref[...] = jnp.broadcast_to(flat[None], square_ref.shape)


def scale_kernel(whole_ref, squares_ref, out_ref, *, entries):
    total = jnp.sum(jnp.sum(squares_ref[...], 0), 1, keepdims=True)
    factor = lax.rsqrt(total / entries + 1e-06)
    for i in range(2):
        for g in range(2):
            out_ref[i, :, g, :] = whole_ref[i, g] * factor


def fields_block(slabs, row_table, synth, kernel_real, kernel_imaginary, weights, target, above, below, norm):
    kernels = kernel_real.shape[0]
    height, width = target.shape
    tiles, rows = width // TILE, 64 * height
    return pl.pallas_call(
        functools.partial(fields_kernel, rows=rows, norm=norm),
        out_shape=[
            jax.ShapeDtypeStruct((tiles, 8, BAND), jnp.float32),
            pltpu.VMEM((kernels, tiles * height, 2 * TILE), jnp.float32),
            jax.ShapeDtypeStruct((16, width), jnp.float32),
            jax.ShapeDtypeStruct((16, width), jnp.float32),
            jax.ShapeDtypeStruct((32, BAND), jnp.float32),
            jax.ShapeDtypeStruct((32, BAND), jnp.float32),
        ],
        in_specs=[VMEM] * 11 + [HERE] * 7,
        out_specs=[VMEM] * 6,
        scratch_shapes=[
            pltpu.VMEM((2 * BAND, 2 * BAND), jnp.bfloat16),
            pltpu.VMEM((16, 2 * BAND), jnp.float32),
            pltpu.SMEM(weights.shape, jnp.float32),
            pltpu.VMEM((4 * BAND, 2 * TILE), jnp.bfloat16),
            pltpu.VMEM(target.shape, jnp.bfloat16),
            pltpu.VMEM(kernel_real.shape, jnp.float32),
            pltpu.VMEM(kernel_real.shape, jnp.float32),
            pltpu.VMEM((tiles, BAND, 2 * BAND), jnp.float32),
            pltpu.VMEM((2 * rows, 5 * BAND), jnp.bfloat16),
            pltpu.VMEM((2, 256, 2 * BAND), jnp.bfloat16),
            pltpu.VMEM((2, 256, 2 * BAND), jnp.bfloat16),
            pltpu.VMEM((64, 2 * TILE), jnp.float32),
            pltpu.SemaphoreType.DMA((5 + kernels // 2,)),
        ],
        compiler_params=params(28),
        name="fields",
    )(
        *near(*slabs, above, below, row_table),
        *homes(
            expand_table(norm), line_tables(64, height), weights,
            np.concatenate(constant_split(synth), 0), target, kernel_real, kernel_imaginary,
        ),
    )


def on_device(
    layout, target, kernel_real, kernel_imaginary, weights, first_taps, first_bias, second_taps, second_bias
):
    height, width = layout.shape
    tiles = width // TILE
    kernels = kernel_real.shape[0]
    rows, cols = height * 64, width * 4
    r = lax.axis_index(ROW)
    norm = 1.0 / math.sqrt(rows * TILE)

    above = lax.ppermute(target, ROW, [(i, i + 1) for i in range(63)])
    below = lax.ppermute(target, ROW, [(i + 1, i) for i in range(63)])

    packed = pl.pallas_call(
        analyse_kernel,
        out_shape=jax.ShapeDtypeStruct((8, 40, BAND), jnp.float32),
        in_specs=[HERE] * 2,
        out_specs=VMEM,
        scratch_shapes=[
            pltpu.VMEM(layout.shape, jnp.bfloat16),
            pltpu.VMEM((2 * TILE, 2 * BAND), jnp.bfloat16),
            pltpu.SemaphoreType.DMA((2,)),
        ],
        compiler_params=params(8),
        name="analyse",
    )(*homes(layout, analysis_table()))
    gathered = lax.all_to_all(packed, "z", 0, 0, tiled=True)
    tables = resist_tables(first_taps, first_bias, second_taps, rows)
    at = 2 * lax.axis_index("y") + lax.axis_index("core")
    row_table = lax.dynamic_index_in_dim(row_transform_tables(), at, 0, keepdims=False)
    gathered, above, below, row_table, *tables = lax.optimization_barrier((gathered, above, below, row_table, *tables))
    slabs = [gathered] + [lax.ppermute(gathered, "y", [(i, (i + k) % 4) for i in range(4)]) for k in (1, 2, 3)]
    slabs = slabs + [lax.ppermute(slab, "core", [(0, 1), (1, 0)]) for slab in slabs]

    synth = synthesis_table(norm)
    columns, fields, intensity, wanted, first_edge, last_edge = fields_block(
        slabs, row_table, synth, kernel_real, kernel_imaginary, weights, target, above, below, norm
    )
    left = lax.ppermute(last_edge, "x", [(i, i + 1) for i in range(3)])
    right = lax.ppermute(first_edge, "x", [(i + 1, i) for i in range(3)])
    back = synth.reshape(2, 64, 2, 2 * TILE).transpose(1, 2, 0, 3).reshape(256, 2 * TILE)
    back = np.concatenate(constant_split(back), 0)
    resist, send = resist_block(
        intensity, wanted, left, right, tables, second_bias, weights, fields, back, (rows, cols)
    )

    got = lax.all_to_all(send, ROW, 0, 0, tiled=True)
    table, turn = adjoint_tables()
    mine = pl.pallas_call(
        adjoint_kernel,
        out_shape=jax.ShapeDtypeStruct((2, 2, kernels, BAND), jnp.float32),
        in_specs=[VMEM] * 2 + [HERE] * 2,
        out_specs=VMEM,
        scratch_shapes=[
            pltpu.VMEM(table.shape, jnp.bfloat16),
            pltpu.VMEM(turn.shape, jnp.float32),
            pltpu.SemaphoreType.DMA((2,)),
        ],
        compiler_params=params(12),
        name="adjoint",
    )(*near(got.reshape(64 * 24, BAND), columns), *homes(table, turn))
    others = [lax.ppermute(mine, "x", [(i, (i + k) % 4) for i in range(4)]) for k in (1, 2, 3)]
    whole, squares = pl.pallas_call(
        total_kernel,
        out_shape=[jax.ShapeDtypeStruct(mine.shape, jnp.float32), jax.ShapeDtypeStruct((64, 1, BAND), jnp.float32)],
        in_specs=[VMEM] * 4,
        out_specs=[VMEM] * 2,
        compiler_params=params(8),
        name="total",
    )(mine, *others)
    squares = lax.all_to_all(squares, ROW, 0, 0, tiled=True)
    grads = pl.pallas_call(
        functools.partial(scale_kernel, entries=2 * kernels * BAND * BAND),
        out_shape=jax.ShapeDtypeStruct((2, kernels, 2, BAND), jnp.float32),
        in_specs=[VMEM] * 2,
        out_specs=VMEM,
        compiler_params=params(8),
        name="scale",
    )(whole, squares)
    return resist, grads.transpose(0, 1, 3, 2)


def solution(mesh):
    devices = mesh.devices.reshape(4, 8, 2, 4)
    fine = Mesh(devices, ALL)
    grid = P(ROW, "x")
    in_specs = (grid, grid, P(), P(), P(), P(), P(), P(), P())
    out_specs = (grid, P(None, None, None, ROW))
    return jax.shard_map(on_device, mesh=fine, in_specs=in_specs, out_specs=out_specs, check_vma=False)
```

```python
import functools
import math

import jax
import jax.numpy as jnp
import numpy as np
from jax import lax
from jax.experimental import pallas as pl
from jax.experimental.pallas import tpu as pltpu
from jax.sharding import Mesh, PartitionSpec as P

TILE = 512
BAND = 128
ROW = ("y", "z", "core")
ALL = ("y", "z", "core", "x")


def phase_angles(freqs, positions):
    return 2.0 * math.pi * ((freqs[:, None] * positions[None, :]) % TILE) / TILE


def dot(a, b):
    return jnp.dot(a, b, preferred_element_type=jnp.float32)


def constant_split(x):
    x = np.asarray(x, np.float32)
    hi = x.astype(jnp.bfloat16)
    return hi, (x - hi.astype(np.float32)).astype(jnp.bfloat16)


VMEM = pl.BlockSpec(memory_space=pltpu.VMEM)
SMEM = pl.BlockSpec(memory_space=pltpu.SMEM)
HERE = pl.BlockSpec(memory_space=pltpu.HBM)


def near(*arrays):
    return [pltpu.with_memory_space_constraint(jnp.asarray(x), pltpu.VMEM) for x in arrays]


def homes(*arrays):
    return [pltpu.with_memory_space_constraint(jnp.asarray(x), pltpu.HBM) for x in arrays]


def fetch(sources, targets, sems):
    copies = [pltpu.make_async_copy(a, b, sems.at[i]) for i, (a, b) in enumerate(zip(sources, targets, strict=True))]
    for copy in copies:
        copy.start()
    return copies


def params(mib):
    return pltpu.CompilerParams(vmem_limit_bytes=mib * 1024 * 1024)


FREQ = np.arange(BAND) - BAND // 2


def analysis_table():
    ang = phase_angles(np.arange(65), np.arange(TILE))
    table = np.zeros((TILE, 2 * BAND))
    table[:, :64], table[:, 64:BAND] = np.cos(ang[:64]).T, np.sin(ang[1:]).T
    table[:, BAND : BAND + 4] = np.cos(ang[64])[:, None]
    return np.concatenate(constant_split(table), 0)


def row_transform_tables():
    tables = []
    for y in range(4):
        for core in range(2):
            slabs = [128 * ((y - k) % 4) + 8 * (core ^ other) for other in range(2) for k in range(4)]
            n = (np.array(slabs)[:, None, None] + 16 * np.arange(8)[:, None] + np.arange(8)).reshape(-1)
            ang = phase_angles(FREQ, n)
            tables.append(np.concatenate(constant_split(np.concatenate([np.cos(ang), np.sin(ang)], 0)), 0))
    return np.stack(tables)


def expand_table(norm):
    table = np.zeros((2, BAND, 2, BAND))
    for g in range(BAND):
        q = g - 64
        m = abs(q)
        if m < 64:
            table[0, m, 0, g] = 1.0
            table[1, m, 1, g] = -1.0
        if m:
            sign = -1.0 if q > 0 else 1.0
            table[1, 63 + m, 0, g] = sign
            table[0, 63 + m, 1, g] = sign
    return (table.reshape(2 * BAND, 2 * BAND) * norm).astype(jnp.bfloat16)


def synthesis_table(norm):
    ang = phase_angles(FREQ, np.arange(TILE))
    c, s = np.cos(ang), np.sin(ang)
    return np.concatenate([np.concatenate([c, s], 1), np.concatenate([-s, c], 1)], 0) * norm


def line_tables(groups, height):
    at = np.arange(groups)[:, None] * height + np.array(FIELD_ROWS)[None, :]
    ang = phase_angles(at.reshape(-1), FREQ)
    return np.concatenate([np.cos(ang), np.sin(ang)], 1).reshape(groups, 16, 2 * BAND).astype(np.float32)


FIELD_ROWS = list(range(8)) + [-4, -3, -2, -1, 8, 9, 10, 11]
HIDDEN_ROWS = list(range(-1, 9)) + [-3, -2, 9, 10]
SLOPE_ROWS = list(range(8)) + [-2, -1, 8, 9] + [None] * 4
WIDE = 17 * 128


def halves(x):
    hi = x.astype(jnp.bfloat16)
    return hi, (x - hi.astype(jnp.float32)).astype(jnp.bfloat16)


def pick(out_rows, in_rows, sign):
    hit = lambda a, b, dy: float(a is not None and b is not None and b - a == sign * (dy - 1))
    return np.array([[[hit(a, b, dy) for b in in_rows] for a in out_rows] for dy in range(3)])


INNER = HIDDEN_ROWS[:10]
CHANNELS = 64


def choose_tables():
    choose = np.zeros((3, 48, 7, 256))
    for dy in range(3):
        for dx in range(3):
            for slot in range(16):
                lane = 16 * dx + slot
                for part, section in ((0, 0), (1, 1), (0, 2)):
                    choose[part, 3 * dy + dx, dy, 48 * section + lane] = 1.0
                    choose[part, 16 + 3 * dy + dx, 4 + dy, 48 * section + lane] = 1.0
    for part in range(3):
        choose[part, 32, 3, 144 + part] = 1.0
    return choose.reshape(144, 7 * 256).astype(jnp.bfloat16)


def lane_masks():
    fore = pick(HIDDEN_ROWS, FIELD_ROWS, 1).transpose(1, 0, 2)
    back = pick(INNER, SLOPE_ROWS, -1).transpose(1, 0, 2)
    masks = np.zeros((80, 256), np.float32)
    masks[:42, :144] = np.tile(fore, (1, 1, 9)).reshape(42, 144)
    masks[42:72, :144] = np.tile(back, (1, 1, 9)).reshape(30, 144)
    return masks


def row_masks():
    fore = np.repeat(pick(SLOPE_ROWS, HIDDEN_ROWS, 1), CHANNELS, 2)
    back = np.repeat(pick(list(range(8)), INNER, -1), CHANNELS, 2)
    return fore.astype(np.float32), back.astype(np.float32)


def tables_kernel(
    first_taps_any, second_taps_any, bias_any, choose_any, lane_masks_any, fore_any, aft_any,
    first_ref, second_ref, second_back_ref, first_back_ref,
    first_taps_ref, second_taps_ref, bias_ref, choose_ref, lane_masks_ref, fore_ref, aft_ref, wide_ref, sems, *, rows
):
    sources = (first_taps_any, second_taps_any, bias_any, choose_any, lane_masks_any, fore_any, aft_any)
    targets = (first_taps_ref, second_taps_ref, bias_ref, choose_ref, lane_masks_ref, fore_ref, aft_ref)
    for copy in fetch(sources, targets, sems):
        copy.wait()
    row0 = lax.axis_index(ROW) * 8
    wide_ref[...] = jnp.zeros_like(wide_ref)
    wide_ref[0:9, 0:CHANNELS] = first_taps_ref[...]
    wide_ref[16:25, 0:CHANNELS] = second_taps_ref[...]
    wide_ref[32:33, 0:CHANNELS] = bias_ref[...]
    tall = wide_ref[...].T[:CHANNELS, :48]
    hi = tall.astype(jnp.bfloat16)
    rest = tall - hi.astype(jnp.float32)
    mid = rest.astype(jnp.bfloat16)
    low = (rest - mid.astype(jnp.float32)).astype(jnp.bfloat16)
    parts = dot(jnp.concatenate([hi, mid, low], 1), choose_ref[...])
    for h, n in enumerate(HIDDEN_ROWS):
        here = row0 + n
        valid = jnp.where((here >= 0) & (here < rows), 1.0, 0.0)
        block = parts[:, 768:1024]
        for dy in range(3):
            block = block + parts[:, 256 * dy : 256 * dy + 256] * lane_masks_ref[3 * h + dy : 3 * h + dy + 1]
        first_ref[64 * h : 64 * h + 64] = (block * valid)[:, :160].astype(jnp.bfloat16)
        if h < 10:
            block = 0.0
            for dy in range(3):
                at = 1024 + 256 * dy
                block = block + parts[:, at : at + 256] * lane_masks_ref[42 + 3 * h + dy : 43 + 3 * h + dy]
            second_back_ref[64 * h : 64 * h + 64] = (block * valid)[:, :144].astype(jnp.bfloat16)
    for taps_ref, mask_ref, out_ref, height in ((second_taps_ref, fore_ref, second_ref, 16), (first_taps_ref, aft_ref, first_back_ref, 8)):
        lanes = out_ref.shape[1]
        taps = taps_ref[...]
        taps = jnp.concatenate([taps] * (lanes // CHANNELS), 1)
        taps_hi = taps.astype(jnp.bfloat16).astype(jnp.float32)
        for at, part in ((0, taps_hi), (out_ref.shape[0] // 2, taps - taps_hi)):
            blocks = []
            for dx in range(3):
                block = 0.0
                for dy in range(3):
                    block = block + part[3 * dy + dx : 3 * dy + dx + 1] * mask_ref[dy]
                blocks.append(block)
            if height == 8:
                blocks.append(jnp.zeros((8, lanes), jnp.float32))
            whole = jnp.concatenate(blocks, 0)
            out_ref[at : at + whole.shape[0]] = whole.astype(jnp.bfloat16)


def resist_tables(first_taps, first_bias, second_taps, rows):
    args = (first_taps, second_taps, first_bias.reshape(1, -1), choose_tables(), lane_masks(), *row_masks())
    return pl.pallas_call(
        functools.partial(tables_kernel, rows=rows),
        out_shape=[
            jax.ShapeDtypeStruct((14 * CHANNELS, 160), jnp.bfloat16),
            jax.ShapeDtypeStruct((96, 14 * CHANNELS), jnp.bfloat16),
            jax.ShapeDtypeStruct((10 * CHANNELS, 144), jnp.bfloat16),
            jax.ShapeDtypeStruct((64, 10 * CHANNELS), jnp.bfloat16),
        ],
        in_specs=[HERE] * 7,
        out_specs=[VMEM] * 4,
        scratch_shapes=[pltpu.VMEM(a.shape, a.dtype) for a in args]
        + [pltpu.VMEM((BAND, BAND), jnp.float32), pltpu.SemaphoreType.DMA((7,))],
        compiler_params=params(12),
        name="tables",
    )(*homes(*args))


SIDE = 256


def hide(first_ref, second_ref, views_ref, here, inner):
    hidden = jnp.tanh(dot(first_ref[...], views_ref[:, here]))
    hi, lo = halves(hidden)
    both = dot(second_ref[...], hi)
    return both[:48] + both[48:] + dot(second_ref[0:48], lo), 1.0 - hidden[:inner] * hidden[:inner]


def place_views(views_ref, dx, moved):
    hi, lo = halves(moved)
    views_ref[16 * dx : 16 * dx + 16] = hi
    views_ref[48 + 16 * dx : 64 + 16 * dx] = hi
    views_ref[96 + 16 * dx : 112 + 16 * dx] = lo


def middle_kernel(field_ref, first_ref, second_ref, mixed_ref, keep_ref, views_ref):
    width = field_ref.shape[1]
    for dx in range(3):
        place_views(views_ref, dx, field_ref[...] if dx == 1 else pltpu.roll(field_ref[...], (1 - dx) % width, 1))
    views_ref[144:160] = jnp.ones((16, width), jnp.bfloat16)

    def step(i, carry):
        at = pl.multiple_of(i * 256, 256)
        there = pl.ds(pl.multiple_of(at + SIDE, 256), 256)
        mixed_ref[:, pl.ds(at, 256)], keep_ref[:, pl.ds(at, 256)] = hide(first_ref, second_ref, views_ref, there, keep_ref.shape[0])
        return carry

    lax.fori_loop(0, (width - 2 * SIDE) // 256, step, 0, unroll=3)


def resist_kernel(
    field_ref, target_ref, left_ref, right_ref, first_ref, second_ref, second_back_ref, first_back_ref, offset_ref,
    fields_ref, mixed_mid_ref, keep_mid_ref, weights_any, back_any,
    resist_any, out_ref, resist_ref, weights_ref, back_ref,
    views_ref, keep_ref, mixed_ref, spread_ref, summed_ref, all_ref, sems, *, rows, cols
):
    copies = fetch((weights_any, back_any), (weights_ref, back_ref), sems)
    row0 = lax.axis_index(ROW) * resist_ref.shape[0]
    col0 = lax.axis_index("x") * resist_ref.shape[1]
    width = resist_ref.shape[1]
    inner = keep_ref.shape[0]

    def columns(shape):
        lane = lax.broadcasted_iota(jnp.int32, shape, 1)
        m = jnp.where(lane < width + 64, lane, lane - WIDE)
        return m, (col0 + m >= 0) & (col0 + m < cols)

    m, in_grid = columns((16, WIDE))
    keep_col = (in_grid & (m >= -3) & (m < width + 3)).astype(jnp.float32)
    lane = lax.broadcasted_iota(jnp.int32, (16, BAND), 1)
    gap = [jnp.where(lane < 64, right_ref[i : i + 16], left_ref[i : i + 16]) for i in (0, 16)]
    field = jnp.concatenate([field_ref[...], jnp.where(in_grid[:, width:], gap[0], 0.0)], 1)
    target = jnp.concatenate([target_ref[...], gap[1]], 1)
    for dx in range(3):
        place_views(views_ref, dx, (field if dx == 1 else pltpu.roll(field, (1 - dx) % WIDE, 1)) * keep_col)
    views_ref[144:160] = keep_col.astype(jnp.bfloat16)

    edges = (slice(0, SIDE), slice(width - SIDE, width), slice(width, WIDE))
    kept = (slice(0, SIDE), slice(SIDE, 2 * SIDE), slice(2 * SIDE, 2 * SIDE + BAND))
    mixed_ref[:, SIDE : width - SIDE] = mixed_mid_ref[...]
    for here, place in zip(edges, kept, strict=True):
        mixed_ref[:, here], keep_ref[:, place] = hide(first_ref, second_ref, views_ref, here, inner)

    logits = offset_ref[0] + mixed_ref[16:32] + pltpu.roll(mixed_ref[0:16], 1, 1) + pltpu.roll(mixed_ref[32:48], WIDE - 1, 1)
    resist = 1.0 / (1.0 + jnp.exp(-logits))
    resist_ref[...] = resist[:8, :width]
    sent = pltpu.make_async_copy(resist_ref, resist_any, sems.at[2])
    sent.start()
    slot = lax.broadcasted_iota(jnp.int32, (16, WIDE), 0)
    n = jnp.where(slot < 8, slot, jnp.where(slot < 10, slot - 10, slot - 2))
    use = in_grid & (m >= -2) & (m < width + 2) & (slot < 12) & (row0 + n >= 0) & (row0 + n < rows)
    slope = jnp.where(use, (resist - target) * (TILE / cols), 0.0)
    grid_col = in_grid.astype(jnp.float32)
    for dx in range(3):
        place_views(spread_ref, dx, (slope if dx == 1 else pltpu.roll(slope, (dx - 1) % WIDE, 1)) * grid_col)

    def backward(here, kept):
        hidden_grad = dot(second_back_ref[...], spread_ref[:, here])
        hi, lo = halves(hidden_grad * kept)
        both = dot(first_back_ref[...], hi)
        summed_ref[:, here] = both[:32] + both[32:] + dot(first_back_ref[0:32], lo)

    def middle(i, carry):
        at = pl.multiple_of(i * 768, 256)
        backward(pl.ds(pl.multiple_of(SIDE + at, 256), 768), keep_mid_ref[:, pl.ds(at, 768)])
        return carry

    lax.fori_loop(0, keep_mid_ref.shape[1] // 768, middle, 0)
    for here, place in zip(edges, kept, strict=True):
        backward(here, keep_ref[:, place])
    grad = summed_ref[8:16] + pltpu.roll(summed_ref[0:8], WIDE - 1, 1) + pltpu.roll(summed_ref[16:24], 1, 1)
    for copy in copies:
        copy.wait()
    grad = jnp.concatenate([grad[:, t * TILE : (t + 1) * TILE] for t in range(4)], 0)
    grad = jnp.concatenate([grad, grad], 1) * 2.0
    half = back_ref.shape[0] // 2
    for i in range(3):
        piece = jnp.concatenate([fields_ref[8 * i + j] * (grad * weights_ref[8 * i + j]) for j in range(8)], 0)
        hi, lo = halves(piece)
        sides = (((1,), (1,)), ((), ()))
        both = lax.dot_general(back_ref[...], hi, sides, preferred_element_type=jnp.float32)
        small = lax.dot_general(back_ref[0:half], lo, sides, preferred_element_type=jnp.float32)
        all_ref[:, 256 * i : 256 * i + 256] = both[:half] + both[half:] + small
    low = lax.broadcasted_iota(jnp.int32, (8, 384), 0) < 4
    for d in range(32):
        first, second = all_ref[8 * d : 8 * d + 8, 0:384], all_ref[8 * d : 8 * d + 8, 384:768]
        even, odd = jnp.where(low, first, pltpu.roll(second, 4, 0)), jnp.where(low, pltpu.roll(first, 4, 0), second)
        for b in range(3):
            out_ref[2 * d, 8 * b : 8 * b + 8] = even[:, BAND * b : BAND * (b + 1)]
            out_ref[2 * d + 1, 8 * b : 8 * b + 8] = odd[:, BAND * b : BAND * (b + 1)]
    sent.wait()


def middle_block(field, tables):
    inner, width = tables[2].shape[0], field.shape[1]
    return pl.pallas_call(
        middle_kernel,
        out_shape=[pltpu.VMEM((48, width - 2 * SIDE), jnp.float32), pltpu.VMEM((inner, width - 2 * SIDE), jnp.float32)],
        in_specs=[VMEM] * 3,
        out_specs=[VMEM] * 2,
        scratch_shapes=[pltpu.VMEM((160, width), jnp.bfloat16)],
        compiler_params=params(16),
        name="middle",
    )(*near(field, tables[0], tables[1]))


def resist_block(field, target, left, right, tables, second_bias, weights, fields, middle, back, dims):
    rows, cols = dims
    inner, width = tables[2].shape[0], field.shape[1]
    return pl.pallas_call(
        functools.partial(resist_kernel, rows=rows, cols=cols),
        out_shape=[pltpu.HBM((8, width), jnp.float32), pltpu.VMEM((64, 24, BAND), jnp.float32)],
        in_specs=[VMEM] * 8 + [SMEM] + [VMEM] * 3 + [HERE] * 2,
        out_specs=[HERE, VMEM],
        scratch_shapes=[
            pltpu.VMEM((8, width), jnp.float32),
            pltpu.SMEM(weights.shape, jnp.float32),
            pltpu.VMEM(back.shape, jnp.bfloat16),
            pltpu.VMEM((160, WIDE), jnp.bfloat16),
            pltpu.VMEM((inner, 2 * SIDE + BAND), jnp.float32),
            pltpu.VMEM((48, WIDE), jnp.float32),
            pltpu.VMEM((144, WIDE), jnp.bfloat16),
            pltpu.VMEM((32, WIDE), jnp.float32),
            pltpu.VMEM((256, 768), jnp.float32),
            pltpu.SemaphoreType.DMA((3,)),
        ],
        compiler_params=params(28),
        name="resist",
    )(field, target, left, right, *tables, second_bias, *near(fields, *middle), *homes(weights, back))


def analyse_kernel(layout_any, table_any, out_ref, layout_ref, table_ref, sems):
    for copy in fetch((layout_any, table_any), (layout_ref, table_ref), sems):
        copy.wait()
    x = layout_ref[...].astype(jnp.float32)
    x = jnp.concatenate([x[:, t * TILE : (t + 1) * TILE] for t in range(4)], 0).astype(jnp.bfloat16)
    sums = dot(x, table_ref[0:TILE]) + dot(x, table_ref[TILE:])
    lane = lax.broadcasted_iota(jnp.int32, (8, BAND), 1)
    last = jnp.zeros((8, BAND), jnp.float32)
    for t in range(4):
        last = jnp.where(lane == t, sums[8 * t : 8 * t + 8, BAND:], last)
    packed = jnp.concatenate([sums[:, :BAND], last], 0)
    for i in range(out_ref.shape[0]):
        out_ref[i] = packed


def fields_kernel(*refs, rows, norm):
    slabs, refs = refs[:8], refs[8:]
    (
        near_rows_ref, far_rows_ref, rows_ref, expand_any, line_any, weights_any, synth_any, target_any, real_any, imag_any,
        cols_ref, fields_ref, intensity_ref, wanted_ref, first_edge_ref, last_edge_ref, *refs
    ) = refs
    (
        expand_ref, line_ref, weights_ref, synth_ref, target_ref, real_ref, imag_ref,
        spec_ref, seen_ref, line_hi_ref, line_lo_ref, sum_ref, sems
    ) = refs
    r = lax.axis_index(ROW)
    sources = [expand_any, line_any.at[r], weights_any, synth_any, target_any]
    targets = [expand_ref, line_ref, weights_ref, synth_ref, target_ref]
    for i in range(0, real_ref.shape[0], 4):
        sources += [real_any.at[i : i + 4], imag_any.at[i : i + 4]]
        targets += [real_ref.at[i : i + 4], imag_ref.at[i : i + 4]]
    copies = fetch(sources, targets, sems)
    row0 = r * 8
    kernels = real_ref.shape[0]
    for p, slab in enumerate(slabs):
        for t in range(5):
            hi, lo = halves(slab[:, 8 * t : 8 * t + 8, :].reshape(64, BAND))
            seen_ref[64 * p : 64 * p + 64, t * BAND : (t + 1) * BAND] = hi
            seen_ref[rows + 64 * p : rows + 64 * p + 64, t * BAND : (t + 1) * BAND] = lo
    table_hi = rows_ref[0 : 2 * BAND]
    u = dot(table_hi, seen_ref[0:rows]) + dot(rows_ref[2 * BAND :], seen_ref[0:rows]) + dot(table_hi, seen_ref[rows:])

    def pair(t):
        both = u[:, t * BAND : (t + 1) * BAND]
        return halves(jnp.concatenate([both[:BAND], both[BAND:]], 1))

    copies[0].wait()
    lane = lax.broadcasted_iota(jnp.int32, (BAND, 2 * BAND), 1)
    last = u[:, 4 * BAND :] * norm
    for t in range(4):
        hi, lo = pair(t)
        moved = pltpu.roll(last, (BAND - t) % BAND, 1)
        moved = jnp.concatenate([moved[:BAND], -moved[BAND:]], 1)
        spec_ref[t] = dot(hi, expand_ref[...]) + dot(lo, expand_ref[...]) + jnp.where((lane == 0) | (lane == BAND), moved, 0.0)

    copies[1].wait()
    phase = line_ref[...]
    c, s = phase[:, :BAND], phase[:, BAND:]
    table = jnp.concatenate([jnp.concatenate([c, -s], 1), jnp.concatenate([s, c], 1)], 0)
    lines_hi, lines_lo = halves(table)
    lines_both = jnp.concatenate([lines_hi, lines_lo], 0)
    sum_ref[...] = jnp.zeros_like(sum_ref)

    def lines(k, slot, j):
        kr, ki = real_ref[k], imag_ref[k]
        pieces = []
        for p in range(2):
            columns = []
            for t in (2 * p, 2 * p + 1):
                sr, si = spec_ref[t, :, :BAND], spec_ref[t, :, BAND:]
                columns.append(jnp.concatenate([kr * sr - ki * si, kr * si + ki * sr], 0))
            hi, lo = halves(jnp.concatenate(columns, 1))
            both = dot(lines_both, hi)
            out = both[:32] + both[32:] + dot(lines_hi, lo)
            for t in range(2):
                pieces.append(jnp.concatenate([out[:16, t * BAND : (t + 1) * BAND], out[16:, t * BAND : (t + 1) * BAND]], 1))
        hi, lo = halves(jnp.concatenate(pieces, 0))
        line_hi_ref[slot, 64 * j : 64 * j + 64] = hi
        line_lo_ref[slot, 64 * j : 64 * j + 64] = lo

    def waves(k0, slot, q):
        here = slice(q * 256, q * 256 + 256)
        synth_hi = synth_ref[0 : 2 * BAND, here]
        line_hi = line_hi_ref[slot]
        f = dot(line_hi, synth_hi) + dot(line_lo_ref[slot], synth_hi) + dot(line_hi, synth_ref[2 * BAND :, here])
        total = sum_ref[:, here]
        for j in range(4):
            part = f[64 * j : 64 * j + 64]
            total = total + weights_ref[k0 + j] * (part * part)
            fields_ref[k0 + j, :, here] = jnp.concatenate([part[16 * t : 16 * t + 8] for t in range(4)], 0)
        sum_ref[:, here] = total

    for copy in copies[5:7]:
        copy.wait()
    for j in range(4):
        lines(j, 0, j)
    for copy in copies[2:5]:
        copy.wait()
    for copy in copies[7:]:
        copy.wait()

    def group(i, slot, more):
        for j in range(4):
            waves(4 * i, slot, j)
            if more:
                lines(4 * i + 4 + j, 1 - slot, j)

    def both(m, carry):
        group(2 * m, 0, True)
        group(2 * m + 1, 1, True)
        return carry

    lax.fori_loop(0, 2, both, 0)
    group(4, 0, True)
    group(5, 1, False)
    row = lax.broadcasted_iota(jnp.int32, (16, 2 * BAND), 0)
    lane = lax.broadcasted_iota(jnp.int32, (16, 2 * BAND), 1)
    chosen = ((row < 4) & (lane == 2 * r + row % 2 + BAND * (row // 2))).astype(jnp.bfloat16)
    for t in range(4):
        hi, lo = halves(spec_ref[t])
        sides = (((1,), (1,)), ((), ()))
        picked = lax.dot_general(chosen, hi, sides, preferred_element_type=jnp.float32)
        cols_ref[t] = (picked + lax.dot_general(chosen, lo, sides, preferred_element_type=jnp.float32))[:8]
    slot = lax.broadcasted_iota(jnp.int32, (16, TILE), 0)
    n = row0 + jnp.where(slot < 8, slot, jnp.where(slot < 12, slot - 12, slot - 4))
    inside = (n >= 0) & (n < rows)
    for t in range(4):
        both = sum_ref[16 * t : 16 * t + 16]
        intensity_ref[:, t * TILE : (t + 1) * TILE] = jnp.where(inside, both[:, :TILE] + both[:, TILE:], 0.0)
    wanted_ref[0:8] = target_ref[...].astype(jnp.float32)
    one, other = near_rows_ref[...].astype(jnp.float32), far_rows_ref[...].astype(jnp.float32)
    even = r % 2 == 0
    above, below = jnp.where(even, other, one), jnp.where(even, one, other)
    wanted_ref[8:16] = jnp.concatenate([above[6:8], below[0:2], jnp.zeros((4, above.shape[1]), jnp.float32)], 0)
    width = intensity_ref.shape[1]
    for i, ref in ((0, intensity_ref), (16, wanted_ref)):
        first_edge_ref[i : i + 16] = ref[:, 0:BAND]
        last_edge_ref[i : i + 16] = ref[:, width - BAND :]


def adjoint_tables():
    wide = phase_angles(8 * np.arange(64), FREQ)
    c, s = np.cos(wide), np.sin(wide)
    w = np.concatenate([np.concatenate([c, -s], 1), np.concatenate([s, c], 1)], 0)
    near_rows = phase_angles(np.arange(8), FREQ)
    return np.concatenate(constant_split(w), 0), np.concatenate([np.cos(near_rows), np.sin(near_rows)], 0).astype(np.float32)


def adjoint_kernel(got_ref, columns_ref, table_any, turn_any, out_ref, table_ref, turn_ref, sems):
    for copy in fetch((table_any, turn_any), (table_ref, turn_ref), sems):
        copy.wait()
    table_hi, table_lo = table_ref[0:BAND], table_ref[BAND:]
    c, s = turn_ref[0:8], turn_ref[8:16]
    for g in range(2):
        turned = []
        for t in range(4):
            re, im = columns_ref[t, g : g + 1], columns_ref[t, 2 + g : 3 + g]
            turned.append((c * re - s * im, s * re + c * im))
        a, b = (jnp.concatenate([x[i] for x in turned], 0)[None] for i in range(2))
        for h in range(2):
            at = 4 * h + 2 * g
            x = [[got_ref[pl.ds(8 * b + at + i, 64, stride=24), :] for b in range(3)] for i in range(2)]
            x = jnp.concatenate([jnp.concatenate(part, 1) for part in x], 0)
            hi, lo = halves(x)
            sides = (((0,), (0,)), ((), ()))
            y = lax.dot_general(hi, table_hi, sides, preferred_element_type=jnp.float32)
            y = y + lax.dot_general(lo, table_hi, sides, preferred_element_type=jnp.float32)
            y = y + lax.dot_general(hi, table_lo, sides, preferred_element_type=jnp.float32)
            y = y.reshape(12, 32, 2 * BAND)
            re, im = y[:, :, :BAND], y[:, :, BAND:]
            out_ref[0, g, 12 * h : 12 * h + 12] = jnp.sum(re * a + im * b, 1)
            out_ref[1, g, 12 * h : 12 * h + 12] = jnp.sum(im * a - re * b, 1)


def total_kernel(x_ref, one_ref, two_ref, three_ref, whole_ref, square_ref):
    whole = (x_ref[...] + two_ref[...]) + (one_ref[...] + three_ref[...])
    whole_ref[...] = whole
    flat = jnp.sum(whole * whole, (0, 1, 2))[None]
    square_ref[...] = jnp.broadcast_to(flat[None], square_ref.shape)


def scale_kernel(whole_ref, squares_ref, out_ref, *, entries):
    total = jnp.sum(jnp.sum(squares_ref[...], 0), 1, keepdims=True)
    factor = lax.rsqrt(total / entries + 1e-06)
    for i in range(2):
        for g in range(2):
            out_ref[i, :, g, :] = whole_ref[i, g] * factor


def fields_block(slabs, row_table, synth, kernel_real, kernel_imaginary, weights, target, near_rows, far_rows, norm):
    kernels = kernel_real.shape[0]
    height, width = target.shape
    tiles, rows = width // TILE, 64 * height
    return pl.pallas_call(
        functools.partial(fields_kernel, rows=rows, norm=norm),
        out_shape=[
            jax.ShapeDtypeStruct((tiles, 8, BAND), jnp.float32),
            pltpu.VMEM((kernels, tiles * height, 2 * TILE), jnp.float32),
            jax.ShapeDtypeStruct((16, width), jnp.float32),
            jax.ShapeDtypeStruct((16, width), jnp.float32),
            jax.ShapeDtypeStruct((32, BAND), jnp.float32),
            jax.ShapeDtypeStruct((32, BAND), jnp.float32),
        ],
        in_specs=[VMEM] * 11 + [HERE] * 7,
        out_specs=[VMEM] * 6,
        scratch_shapes=[
            pltpu.VMEM((2 * BAND, 2 * BAND), jnp.bfloat16),
            pltpu.VMEM((16, 2 * BAND), jnp.float32),
            pltpu.SMEM(weights.shape, jnp.float32),
            pltpu.VMEM((4 * BAND, 2 * TILE), jnp.bfloat16),
            pltpu.VMEM(target.shape, jnp.bfloat16),
            pltpu.VMEM(kernel_real.shape, jnp.float32),
            pltpu.VMEM(kernel_real.shape, jnp.float32),
            pltpu.VMEM((tiles, BAND, 2 * BAND), jnp.float32),
            pltpu.VMEM((2 * rows, 5 * BAND), jnp.bfloat16),
            pltpu.VMEM((2, 256, 2 * BAND), jnp.bfloat16),
            pltpu.VMEM((2, 256, 2 * BAND), jnp.bfloat16),
            pltpu.VMEM((64, 2 * TILE), jnp.float32),
            pltpu.SemaphoreType.DMA((5 + kernels // 2,)),
        ],
        compiler_params=params(28),
        name="fields",
    )(
        *near(*slabs, near_rows, far_rows, row_table),
        *homes(
            expand_table(norm), line_tables(64, height), weights,
            np.concatenate(constant_split(synth), 0), target, kernel_real, kernel_imaginary,
        ),
    )


def on_device(
    layout, target, kernel_real, kernel_imaginary, weights, first_taps, first_bias, second_taps, second_bias
):
    height, width = layout.shape
    tiles = width // TILE
    kernels = kernel_real.shape[0]
    rows, cols = height * 64, width * 4
    r = lax.axis_index(ROW)
    norm = 1.0 / math.sqrt(rows * TILE)

    near_rows = lax.ppermute(target, ROW, [(i, i ^ 1) for i in range(64)])
    far_rows = lax.ppermute(target, ROW, [(i, (i - 1 if i % 2 == 0 else i + 1) % 64) for i in range(64)])

    packed = pl.pallas_call(
        analyse_kernel,
        out_shape=jax.ShapeDtypeStruct((8, 40, BAND), jnp.float32),
        in_specs=[HERE] * 2,
        out_specs=VMEM,
        scratch_shapes=[
            pltpu.VMEM(layout.shape, jnp.bfloat16),
            pltpu.VMEM((2 * TILE, 2 * BAND), jnp.bfloat16),
            pltpu.SemaphoreType.DMA((2,)),
        ],
        compiler_params=params(8),
        name="analyse",
    )(*homes(layout, analysis_table()))
    gathered = lax.all_to_all(packed, "z", 0, 0, tiled=True)
    tables = resist_tables(first_taps, first_bias, second_taps, rows)
    at = 2 * lax.axis_index("y") + lax.axis_index("core")
    row_table = lax.dynamic_index_in_dim(row_transform_tables(), at, 0, keepdims=False)
    gathered, near_rows, far_rows, row_table, *tables = lax.optimization_barrier(
        (gathered, near_rows, far_rows, row_table, *tables)
    )
    slabs = [gathered] + [lax.ppermute(gathered, "y", [(i, (i + k) % 4) for i in range(4)]) for k in (1, 2, 3)]
    slabs = slabs + [lax.ppermute(slab, "core", [(0, 1), (1, 0)]) for slab in slabs]

    synth = synthesis_table(norm)
    columns, fields, intensity, wanted, first_edge, last_edge = fields_block(
        slabs, row_table, synth, kernel_real, kernel_imaginary, weights, target, near_rows, far_rows, norm
    )
    left = lax.ppermute(last_edge, "x", [(i, (i + 1) % 4) for i in range(4)])
    right = lax.ppermute(first_edge, "x", [((i + 1) % 4, i) for i in range(4)])
    back = synth.reshape(2, 64, 2, 2 * TILE).transpose(1, 2, 0, 3).reshape(256, 2 * TILE)
    back = np.concatenate(constant_split(back), 0)
    middle = middle_block(intensity, tables)
    resist, send = resist_block(
        intensity, wanted, left, right, tables, second_bias, weights, fields, middle, back, (rows, cols)
    )

    got = lax.all_to_all(send, ROW, 0, 0, tiled=True)
    table, turn = adjoint_tables()
    mine = pl.pallas_call(
        adjoint_kernel,
        out_shape=jax.ShapeDtypeStruct((2, 2, kernels, BAND), jnp.float32),
        in_specs=[VMEM] * 2 + [HERE] * 2,
        out_specs=VMEM,
        scratch_shapes=[
            pltpu.VMEM(table.shape, jnp.bfloat16),
            pltpu.VMEM(turn.shape, jnp.float32),
            pltpu.SemaphoreType.DMA((2,)),
        ],
        compiler_params=params(12),
        name="adjoint",
    )(*near(got.reshape(64 * 24, BAND), columns), *homes(table, turn))
    others = [lax.ppermute(mine, "x", [(i, (i + k) % 4) for i in range(4)]) for k in (1, 2, 3)]
    whole, squares = pl.pallas_call(
        total_kernel,
        out_shape=[jax.ShapeDtypeStruct(mine.shape, jnp.float32), jax.ShapeDtypeStruct((64, 1, BAND), jnp.float32)],
        in_specs=[VMEM] * 4,
        out_specs=[VMEM] * 2,
        compiler_params=params(8),
        name="total",
    )(mine, *others)
    squares = lax.all_to_all(squares, ROW, 0, 0, tiled=True)
    grads = pl.pallas_call(
        functools.partial(scale_kernel, entries=2 * kernels * BAND * BAND),
        out_shape=jax.ShapeDtypeStruct((2, kernels, 2, BAND), jnp.float32),
        in_specs=[VMEM] * 2,
        out_specs=VMEM,
        compiler_params=params(8),
        name="scale",
    )(whole, squares)
    return resist, grads.transpose(0, 1, 3, 2)


def solution(mesh):
    devices = mesh.devices.reshape(4, 8, 2, 4)
    fine = Mesh(devices, ALL)
    grid = P(ROW, "x")
    in_specs = (grid, grid, P(), P(), P(), P(), P(), P(), P())
    out_specs = (grid, P(None, None, None, ROW))
    return jax.shard_map(on_device, mesh=fine, in_specs=in_specs, out_specs=out_specs, check_vma=False)
```

```python
import functools
import math

import jax
import jax.numpy as jnp
import numpy as np
from jax import lax
from jax.experimental import pallas as pl
from jax.experimental.pallas import tpu as pltpu
from jax.sharding import Mesh, PartitionSpec as P

TILE = 512
BAND = 128
ROW = ("y", "z", "core")
ALL = ("y", "z", "core", "x")


def phase_angles(freqs, positions):
    return 2.0 * math.pi * ((freqs[:, None] * positions[None, :]) % TILE) / TILE


def dot(a, b):
    return jnp.dot(a, b, preferred_element_type=jnp.float32)


def constant_split(x):
    x = np.asarray(x, np.float32)
    hi = x.astype(jnp.bfloat16)
    return hi, (x - hi.astype(np.float32)).astype(jnp.bfloat16)


VMEM = pl.BlockSpec(memory_space=pltpu.VMEM)
SMEM = pl.BlockSpec(memory_space=pltpu.SMEM)
HERE = pl.BlockSpec(memory_space=pltpu.HBM)


def near(*arrays):
    return [pltpu.with_memory_space_constraint(jnp.asarray(x), pltpu.VMEM) for x in arrays]


def homes(*arrays):
    return [pltpu.with_memory_space_constraint(jnp.asarray(x), pltpu.HBM) for x in arrays]


def fetch(sources, targets, sems):
    copies = [pltpu.make_async_copy(a, b, sems.at[i]) for i, (a, b) in enumerate(zip(sources, targets, strict=True))]
    for copy in copies:
        copy.start()
    return copies


def params(mib):
    return pltpu.CompilerParams(vmem_limit_bytes=mib * 1024 * 1024)


FREQ = np.arange(BAND) - BAND // 2


def analysis_table():
    ang = phase_angles(np.arange(65), np.arange(TILE))
    table = np.zeros((TILE, 2 * BAND))
    table[:, :64], table[:, 64:BAND] = np.cos(ang[:64]).T, np.sin(ang[1:]).T
    table[:, BAND : BAND + 4] = np.cos(ang[64])[:, None]
    return np.concatenate(constant_split(table), 0)


def row_transform_tables():
    tables = []
    for y in range(4):
        for core in range(2):
            slabs = [128 * ((y - k) % 4) + 8 * (core ^ other) for other in range(2) for k in range(4)]
            n = (np.array(slabs)[:, None, None] + 16 * np.arange(8)[:, None] + np.arange(8)).reshape(-1)
            ang = phase_angles(FREQ, n)
            tables.append(np.concatenate(constant_split(np.concatenate([np.cos(ang), np.sin(ang)], 0)), 0))
    return np.stack(tables)


def expand_table(norm):
    table = np.zeros((2, BAND, 2, BAND))
    for g in range(BAND):
        q = g - 64
        m = abs(q)
        if m < 64:
            table[0, m, 0, g] = 1.0
            table[1, m, 1, g] = -1.0
        if m:
            sign = -1.0 if q > 0 else 1.0
            table[1, 63 + m, 0, g] = sign
            table[0, 63 + m, 1, g] = sign
    return (table.reshape(2 * BAND, 2 * BAND) * norm).astype(jnp.bfloat16)


def synthesis_table(norm):
    ang = phase_angles(FREQ, np.arange(TILE))
    c, s = np.cos(ang), np.sin(ang)
    return np.concatenate([np.concatenate([c, s], 1), np.concatenate([-s, c], 1)], 0) * norm


def line_tables(groups, height):
    at = np.arange(groups)[:, None] * height + np.array(FIELD_ROWS)[None, :]
    ang = phase_angles(at.reshape(-1), FREQ)
    return np.concatenate([np.cos(ang), np.sin(ang)], 1).reshape(groups, 16, 2 * BAND).astype(np.float32)


FIELD_ROWS = list(range(8)) + [-4, -3, -2, -1, 8, 9, 10, 11]
HIDDEN_ROWS = list(range(-1, 9)) + [-3, -2, 9, 10]
SLOPE_ROWS = list(range(8)) + [-2, -1, 8, 9] + [None] * 4
WIDE = 17 * 128


def halves(x):
    hi = x.astype(jnp.bfloat16)
    return hi, (x - hi.astype(jnp.float32)).astype(jnp.bfloat16)


def pick(out_rows, in_rows, sign):
    hit = lambda a, b, dy: float(a is not None and b is not None and b - a == sign * (dy - 1))
    return np.array([[[hit(a, b, dy) for b in in_rows] for a in out_rows] for dy in range(3)])


INNER = HIDDEN_ROWS[:10]
CHANNELS = 64


def choose_tables():
    choose = np.zeros((3, 48, 7, 256))
    for dy in range(3):
        for dx in range(3):
            for slot in range(16):
                lane = 16 * dx + slot
                for part, section in ((0, 0), (1, 1), (0, 2)):
                    choose[part, 3 * dy + dx, dy, 48 * section + lane] = 1.0
                    choose[part, 16 + 3 * dy + dx, 4 + dy, 48 * section + lane] = 1.0
    for part in range(3):
        choose[part, 32, 3, 144 + part] = 1.0
    return choose.reshape(144, 7 * 256).astype(jnp.bfloat16)


def lane_masks():
    fore = pick(HIDDEN_ROWS, FIELD_ROWS, 1).transpose(1, 0, 2)
    back = pick(INNER, SLOPE_ROWS, -1).transpose(1, 0, 2)
    masks = np.zeros((80, 256), np.float32)
    masks[:42, :144] = np.tile(fore, (1, 1, 9)).reshape(42, 144)
    masks[42:72, :144] = np.tile(back, (1, 1, 9)).reshape(30, 144)
    return masks


def row_masks():
    fore = np.repeat(pick(SLOPE_ROWS, HIDDEN_ROWS, 1), CHANNELS, 2)
    back = np.repeat(pick(list(range(8)), INNER, -1), CHANNELS, 2)
    return fore.astype(np.float32), back.astype(np.float32)


def tables_kernel(
    first_taps_any, second_taps_any, bias_any, choose_any, lane_masks_any, fore_any, aft_any,
    first_ref, second_ref, second_back_ref, first_back_ref,
    first_taps_ref, second_taps_ref, bias_ref, choose_ref, lane_masks_ref, fore_ref, aft_ref, wide_ref, sems, *, rows
):
    sources = (first_taps_any, second_taps_any, bias_any, choose_any, lane_masks_any, fore_any, aft_any)
    targets = (first_taps_ref, second_taps_ref, bias_ref, choose_ref, lane_masks_ref, fore_ref, aft_ref)
    for copy in fetch(sources, targets, sems):
        copy.wait()
    row0 = lax.axis_index(ROW) * 8
    wide_ref[...] = jnp.zeros_like(wide_ref)
    wide_ref[0:9, 0:CHANNELS] = first_taps_ref[...]
    wide_ref[16:25, 0:CHANNELS] = second_taps_ref[...]
    wide_ref[32:33, 0:CHANNELS] = bias_ref[...]
    tall = wide_ref[...].T[:CHANNELS, :48]
    hi = tall.astype(jnp.bfloat16)
    rest = tall - hi.astype(jnp.float32)
    mid = rest.astype(jnp.bfloat16)
    low = (rest - mid.astype(jnp.float32)).astype(jnp.bfloat16)
    parts = dot(jnp.concatenate([hi, mid, low], 1), choose_ref[...])
    for h, n in enumerate(HIDDEN_ROWS):
        here = row0 + n
        valid = jnp.where((here >= 0) & (here < rows), 1.0, 0.0)
        block = parts[:, 768:1024]
        for dy in range(3):
            block = block + parts[:, 256 * dy : 256 * dy + 256] * lane_masks_ref[3 * h + dy : 3 * h + dy + 1]
        first_ref[64 * h : 64 * h + 64] = (block * valid)[:, :160].astype(jnp.bfloat16)
        if h < 10:
            block = 0.0
            for dy in range(3):
                at = 1024 + 256 * dy
                block = block + parts[:, at : at + 256] * lane_masks_ref[42 + 3 * h + dy : 43 + 3 * h + dy]
            second_back_ref[64 * h : 64 * h + 64] = (block * valid)[:, :144].astype(jnp.bfloat16)
    for taps_ref, mask_ref, out_ref, height in ((second_taps_ref, fore_ref, second_ref, 16), (first_taps_ref, aft_ref, first_back_ref, 8)):
        lanes = out_ref.shape[1]
        taps = taps_ref[...]
        taps = jnp.concatenate([taps] * (lanes // CHANNELS), 1)
        taps_hi = taps.astype(jnp.bfloat16).astype(jnp.float32)
        for at, part in ((0, taps_hi), (out_ref.shape[0] // 2, taps - taps_hi)):
            blocks = []
            for dx in range(3):
                block = 0.0
                for dy in range(3):
                    block = block + part[3 * dy + dx : 3 * dy + dx + 1] * mask_ref[dy]
                blocks.append(block)
            if height == 8:
                blocks.append(jnp.zeros((8, lanes), jnp.float32))
            whole = jnp.concatenate(blocks, 0)
            out_ref[at : at + whole.shape[0]] = whole.astype(jnp.bfloat16)


def resist_tables(first_taps, first_bias, second_taps, rows):
    args = (first_taps, second_taps, first_bias.reshape(1, -1), choose_tables(), lane_masks(), *row_masks())
    return pl.pallas_call(
        functools.partial(tables_kernel, rows=rows),
        out_shape=[
            jax.ShapeDtypeStruct((14 * CHANNELS, 160), jnp.bfloat16),
            jax.ShapeDtypeStruct((96, 14 * CHANNELS), jnp.bfloat16),
            jax.ShapeDtypeStruct((10 * CHANNELS, 144), jnp.bfloat16),
            jax.ShapeDtypeStruct((64, 10 * CHANNELS), jnp.bfloat16),
        ],
        in_specs=[HERE] * 7,
        out_specs=[VMEM] * 4,
        scratch_shapes=[pltpu.VMEM(a.shape, a.dtype) for a in args]
        + [pltpu.VMEM((BAND, BAND), jnp.float32), pltpu.SemaphoreType.DMA((7,))],
        compiler_params=params(12),
        name="tables",
    )(*homes(*args))


SIDE = 256


def hide(first_ref, second_ref, views_ref, here, inner):
    hidden = jnp.tanh(dot(first_ref[...], views_ref[:, here]))
    hi, lo = halves(hidden)
    both = dot(second_ref[...], hi)
    return both[:48] + both[48:] + dot(second_ref[0:48], lo), 1.0 - hidden[:inner] * hidden[:inner]


def place_views(views_ref, dx, moved):
    hi, lo = halves(moved)
    views_ref[16 * dx : 16 * dx + 16] = hi
    views_ref[48 + 16 * dx : 64 + 16 * dx] = hi
    views_ref[96 + 16 * dx : 112 + 16 * dx] = lo


def middle_kernel(field_ref, first_ref, second_ref, mixed_ref, keep_ref, views_ref):
    width = field_ref.shape[1]
    for dx in range(3):
        place_views(views_ref, dx, field_ref[...] if dx == 1 else pltpu.roll(field_ref[...], (1 - dx) % width, 1))
    views_ref[144:160] = jnp.ones((16, width), jnp.bfloat16)

    def step(i, carry):
        at = pl.multiple_of(i * 256, 256)
        there = pl.ds(pl.multiple_of(at + SIDE, 256), 256)
        mixed_ref[:, pl.ds(at, 256)], keep_ref[:, pl.ds(at, 256)] = hide(first_ref, second_ref, views_ref, there, keep_ref.shape[0])
        return carry

    lax.fori_loop(0, (width - 2 * SIDE) // 256, step, 0, unroll=3)


def resist_kernel(
    field_ref, target_ref, left_ref, right_ref, first_ref, second_ref, second_back_ref, first_back_ref, offset_ref,
    fields_ref, mixed_mid_ref, keep_mid_ref, weights_any, back_any,
    resist_any, out_ref, resist_ref, weights_ref, back_ref,
    views_ref, keep_ref, mixed_ref, spread_ref, summed_ref, all_ref, sems, *, rows, cols
):
    copies = fetch((weights_any, back_any), (weights_ref, back_ref), sems)
    row0 = lax.axis_index(ROW) * resist_ref.shape[0]
    col0 = lax.axis_index("x") * resist_ref.shape[1]
    width = resist_ref.shape[1]
    inner = keep_ref.shape[0]

    def columns(shape):
        lane = lax.broadcasted_iota(jnp.int32, shape, 1)
        m = jnp.where(lane < width + 64, lane, lane - WIDE)
        return m, (col0 + m >= 0) & (col0 + m < cols)

    m, in_grid = columns((16, WIDE))
    keep_col = (in_grid & (m >= -3) & (m < width + 3)).astype(jnp.float32)
    lane = lax.broadcasted_iota(jnp.int32, (16, BAND), 1)
    gap = [jnp.where(lane < 64, right_ref[i : i + 16], left_ref[i : i + 16]) for i in (0, 16)]
    field = jnp.concatenate([field_ref[...], jnp.where(in_grid[:, width:], gap[0], 0.0)], 1)
    target = jnp.concatenate([target_ref[...], gap[1]], 1)
    for dx in range(3):
        place_views(views_ref, dx, (field if dx == 1 else pltpu.roll(field, (1 - dx) % WIDE, 1)) * keep_col)
    views_ref[144:160] = keep_col.astype(jnp.bfloat16)

    edges = (slice(0, SIDE), slice(width - SIDE, width), slice(width, WIDE))
    kept = (slice(0, SIDE), slice(SIDE, 2 * SIDE), slice(2 * SIDE, 2 * SIDE + BAND))
    mixed_ref[:, SIDE : width - SIDE] = mixed_mid_ref[...]
    for here, place in zip(edges, kept, strict=True):
        mixed_ref[:, here], keep_ref[:, place] = hide(first_ref, second_ref, views_ref, here, inner)

    logits = offset_ref[0] + mixed_ref[16:32] + pltpu.roll(mixed_ref[0:16], 1, 1) + pltpu.roll(mixed_ref[32:48], WIDE - 1, 1)
    resist = 1.0 / (1.0 + jnp.exp(-logits))
    resist_ref[...] = resist[:8, :width]
    sent = pltpu.make_async_copy(resist_ref, resist_any, sems.at[2])
    sent.start()
    slot = lax.broadcasted_iota(jnp.int32, (16, WIDE), 0)
    n = jnp.where(slot < 8, slot, jnp.where(slot < 10, slot - 10, slot - 2))
    use = in_grid & (m >= -2) & (m < width + 2) & (slot < 12) & (row0 + n >= 0) & (row0 + n < rows)
    slope = jnp.where(use, (resist - target) * (TILE / cols), 0.0)
    grid_col = in_grid.astype(jnp.float32)
    for dx in range(3):
        place_views(spread_ref, dx, (slope if dx == 1 else pltpu.roll(slope, (dx - 1) % WIDE, 1)) * grid_col)

    def backward(here, kept):
        hidden_grad = dot(second_back_ref[...], spread_ref[:, here])
        hi, lo = halves(hidden_grad * kept)
        both = dot(first_back_ref[...], hi)
        summed_ref[:, here] = both[:32] + both[32:] + dot(first_back_ref[0:32], lo)

    def middle(i, carry):
        at = pl.multiple_of(i * 768, 256)
        backward(pl.ds(pl.multiple_of(SIDE + at, 256), 768), keep_mid_ref[:, pl.ds(at, 768)])
        return carry

    lax.fori_loop(0, keep_mid_ref.shape[1] // 768, middle, 0)
    for here, place in zip(edges, kept, strict=True):
        backward(here, keep_ref[:, place])
    grad = summed_ref[8:16] + pltpu.roll(summed_ref[0:8], WIDE - 1, 1) + pltpu.roll(summed_ref[16:24], 1, 1)
    for copy in copies:
        copy.wait()
    grad = jnp.concatenate([grad[:, t * TILE : (t + 1) * TILE] for t in range(4)], 0)
    grad = jnp.concatenate([grad, grad], 1) * 2.0
    half = back_ref.shape[0] // 2
    for i in range(3):
        piece = jnp.concatenate([fields_ref[8 * i + j] * (grad * weights_ref[8 * i + j]) for j in range(8)], 0)
        hi, lo = halves(piece)
        sides = (((1,), (1,)), ((), ()))
        both = lax.dot_general(back_ref[...], hi, sides, preferred_element_type=jnp.float32)
        small = lax.dot_general(back_ref[0:half], lo, sides, preferred_element_type=jnp.float32)
        all_ref[:, 256 * i : 256 * i + 256] = both[:half] + both[half:] + small
    low = lax.broadcasted_iota(jnp.int32, (8, 384), 0) < 4
    for d in range(32):
        first, second = all_ref[8 * d : 8 * d + 8, 0:384], all_ref[8 * d : 8 * d + 8, 384:768]
        even, odd = jnp.where(low, first, pltpu.roll(second, 4, 0)), jnp.where(low, pltpu.roll(first, 4, 0), second)
        for b in range(3):
            out_ref[2 * d, 8 * b : 8 * b + 8] = even[:, BAND * b : BAND * (b + 1)]
            out_ref[2 * d + 1, 8 * b : 8 * b + 8] = odd[:, BAND * b : BAND * (b + 1)]
    sent.wait()


def middle_block(field, tables):
    inner, width = tables[2].shape[0], field.shape[1]
    return pl.pallas_call(
        middle_kernel,
        out_shape=[pltpu.VMEM((48, width - 2 * SIDE), jnp.float32), pltpu.VMEM((inner, width - 2 * SIDE), jnp.float32)],
        in_specs=[VMEM] * 3,
        out_specs=[VMEM] * 2,
        scratch_shapes=[pltpu.VMEM((160, width), jnp.bfloat16)],
        compiler_params=params(16),
        name="middle",
    )(*near(field, tables[0], tables[1]))


def resist_block(field, target, left, right, tables, second_bias, weights, fields, middle, back, dims):
    rows, cols = dims
    inner, width = tables[2].shape[0], field.shape[1]
    return pl.pallas_call(
        functools.partial(resist_kernel, rows=rows, cols=cols),
        out_shape=[pltpu.HBM((8, width), jnp.float32), pltpu.VMEM((64, 24, BAND), jnp.float32)],
        in_specs=[VMEM] * 8 + [SMEM] + [VMEM] * 3 + [HERE] * 2,
        out_specs=[HERE, VMEM],
        scratch_shapes=[
            pltpu.VMEM((8, width), jnp.float32),
            pltpu.SMEM(weights.shape, jnp.float32),
            pltpu.VMEM(back.shape, jnp.bfloat16),
            pltpu.VMEM((160, WIDE), jnp.bfloat16),
            pltpu.VMEM((inner, 2 * SIDE + BAND), jnp.float32),
            pltpu.VMEM((48, WIDE), jnp.float32),
            pltpu.VMEM((144, WIDE), jnp.bfloat16),
            pltpu.VMEM((32, WIDE), jnp.float32),
            pltpu.VMEM((256, 768), jnp.float32),
            pltpu.SemaphoreType.DMA((3,)),
        ],
        compiler_params=params(28),
        name="resist",
    )(field, target, left, right, *tables, second_bias, *near(fields, *middle), *homes(weights, back))


def analyse_kernel(layout_any, table_any, out_ref, layout_ref, table_ref, sems):
    for copy in fetch((layout_any, table_any), (layout_ref, table_ref), sems):
        copy.wait()
    x = layout_ref[...].astype(jnp.float32)
    x = jnp.concatenate([x[:, t * TILE : (t + 1) * TILE] for t in range(4)], 0).astype(jnp.bfloat16)
    sums = dot(x, table_ref[0:TILE]) + dot(x, table_ref[TILE:])
    lane = lax.broadcasted_iota(jnp.int32, (8, BAND), 1)
    last = jnp.zeros((8, BAND), jnp.float32)
    for t in range(4):
        last = jnp.where(lane == t, sums[8 * t : 8 * t + 8, BAND:], last)
    packed = jnp.concatenate([sums[:, :BAND], last], 0)
    for i in range(out_ref.shape[0]):
        out_ref[i] = packed


def repack_kernel(in_ref, out_ref):
    last = in_ref[0, 32:40]
    for z in range(8):
        for t in range(4):
            out_ref[4 * z + t] = in_ref[z, 8 * t : 8 * t + 8]
        if z:
            last = last + pltpu.roll(in_ref[z, 32:40], 4 * z, 1)
    out_ref[32] = last


def fields_kernel(*refs, rows, norm):
    slabs, refs = refs[:8], refs[8:]
    (
        near_rows_ref, far_rows_ref, rows_ref, expand_any, line_any, weights_any, synth_any, target_any, real_any, imag_any,
        cols_ref, fields_ref, intensity_ref, wanted_ref, first_edge_ref, last_edge_ref, *refs
    ) = refs
    (
        expand_ref, line_ref, weights_ref, synth_ref, target_ref, real_ref, imag_ref,
        spec_ref, seen_ref, line_hi_ref, line_lo_ref, sum_ref, sems
    ) = refs
    r = lax.axis_index(ROW)
    sources = [expand_any, line_any.at[r], weights_any, synth_any, target_any]
    targets = [expand_ref, line_ref, weights_ref, synth_ref, target_ref]
    for i in range(0, real_ref.shape[0], 4):
        sources += [real_any.at[i : i + 4], imag_any.at[i : i + 4]]
        targets += [real_ref.at[i : i + 4], imag_ref.at[i : i + 4]]
    copies = fetch(sources, targets, sems)
    row0 = r * 8
    kernels = real_ref.shape[0]
    for p, slab in enumerate(slabs):
        last = slab[32]
        last = jnp.concatenate([pltpu.roll(last, (BAND - 4 * z) % BAND, 1) if z else last for z in range(8)], 0)
        for t in range(5):
            tile = jnp.concatenate([slab[4 * z + t] for z in range(8)], 0) if t < 4 else last
            hi, lo = halves(tile)
            seen_ref[64 * p : 64 * p + 64, t * BAND : (t + 1) * BAND] = hi
            seen_ref[rows + 64 * p : rows + 64 * p + 64, t * BAND : (t + 1) * BAND] = lo
    table_hi = rows_ref[0 : 2 * BAND]
    u = dot(table_hi, seen_ref[0:rows]) + dot(rows_ref[2 * BAND :], seen_ref[0:rows]) + dot(table_hi, seen_ref[rows:])

    def pair(t):
        both = u[:, t * BAND : (t + 1) * BAND]
        return halves(jnp.concatenate([both[:BAND], both[BAND:]], 1))

    copies[0].wait()
    lane = lax.broadcasted_iota(jnp.int32, (BAND, 2 * BAND), 1)
    last = u[:, 4 * BAND :] * norm
    for t in range(4):
        hi, lo = pair(t)
        moved = pltpu.roll(last, (BAND - t) % BAND, 1)
        moved = jnp.concatenate([moved[:BAND], -moved[BAND:]], 1)
        spec_ref[t] = dot(hi, expand_ref[...]) + dot(lo, expand_ref[...]) + jnp.where((lane == 0) | (lane == BAND), moved, 0.0)

    copies[1].wait()
    phase = line_ref[...]
    c, s = phase[:, :BAND], phase[:, BAND:]
    table = jnp.concatenate([jnp.concatenate([c, -s], 1), jnp.concatenate([s, c], 1)], 0)
    lines_hi, lines_lo = halves(table)
    lines_both = jnp.concatenate([lines_hi, lines_lo], 0)
    sum_ref[...] = jnp.zeros_like(sum_ref)

    def lines(k, slot, j):
        kr, ki = real_ref[k], imag_ref[k]
        pieces = []
        for p in range(2):
            columns = []
            for t in (2 * p, 2 * p + 1):
                sr, si = spec_ref[t, :, :BAND], spec_ref[t, :, BAND:]
                columns.append(jnp.concatenate([kr * sr - ki * si, kr * si + ki * sr], 0))
            hi, lo = halves(jnp.concatenate(columns, 1))
            both = dot(lines_both, hi)
            out = both[:32] + both[32:] + dot(lines_hi, lo)
            for t in range(2):
                pieces.append(jnp.concatenate([out[:16, t * BAND : (t + 1) * BAND], out[16:, t * BAND : (t + 1) * BAND]], 1))
        hi, lo = halves(jnp.concatenate(pieces, 0))
        line_hi_ref[slot, 64 * j : 64 * j + 64] = hi
        line_lo_ref[slot, 64 * j : 64 * j + 64] = lo

    def waves(k0, slot, q):
        here = slice(q * 256, q * 256 + 256)
        synth_hi = synth_ref[0 : 2 * BAND, here]
        line_hi = line_hi_ref[slot]
        f = dot(line_hi, synth_hi) + dot(line_lo_ref[slot], synth_hi) + dot(line_hi, synth_ref[2 * BAND :, here])
        total = sum_ref[:, here]
        for j in range(4):
            part = f[64 * j : 64 * j + 64]
            total = total + weights_ref[k0 + j] * (part * part)
            fields_ref[k0 + j, :, here] = jnp.concatenate([part[16 * t : 16 * t + 8] for t in range(4)], 0)
        sum_ref[:, here] = total

    for copy in copies[5:7]:
        copy.wait()
    for j in range(4):
        lines(j, 0, j)
    for copy in copies[2:5]:
        copy.wait()
    for copy in copies[7:]:
        copy.wait()

    def group(i, slot, more):
        for j in range(4):
            waves(4 * i, slot, j)
            if more:
                lines(4 * i + 4 + j, 1 - slot, j)

    def both(m, carry):
        group(2 * m, 0, True)
        group(2 * m + 1, 1, True)
        return carry

    lax.fori_loop(0, 2, both, 0)
    group(4, 0, True)
    group(5, 1, False)
    row = lax.broadcasted_iota(jnp.int32, (16, 2 * BAND), 0)
    lane = lax.broadcasted_iota(jnp.int32, (16, 2 * BAND), 1)
    chosen = ((row < 4) & (lane == 2 * r + row % 2 + BAND * (row // 2))).astype(jnp.bfloat16)
    for t in range(4):
        hi, lo = halves(spec_ref[t])
        sides = (((1,), (1,)), ((), ()))
        picked = lax.dot_general(chosen, hi, sides, preferred_element_type=jnp.float32)
        cols_ref[t] = (picked + lax.dot_general(chosen, lo, sides, preferred_element_type=jnp.float32))[:8]
    slot = lax.broadcasted_iota(jnp.int32, (16, TILE), 0)
    n = row0 + jnp.where(slot < 8, slot, jnp.where(slot < 12, slot - 12, slot - 4))
    inside = (n >= 0) & (n < rows)
    for t in range(4):
        both = sum_ref[16 * t : 16 * t + 16]
        intensity_ref[:, t * TILE : (t + 1) * TILE] = jnp.where(inside, both[:, :TILE] + both[:, TILE:], 0.0)
    wanted_ref[0:8] = target_ref[...].astype(jnp.float32)
    one, other = near_rows_ref[...].astype(jnp.float32), far_rows_ref[...].astype(jnp.float32)
    even = r % 2 == 0
    above, below = jnp.where(even, other, one), jnp.where(even, one, other)
    wanted_ref[8:16] = jnp.concatenate([above[6:8], below[0:2], jnp.zeros((4, above.shape[1]), jnp.float32)], 0)
    width = intensity_ref.shape[1]
    for i, ref in ((0, intensity_ref), (16, wanted_ref)):
        first_edge_ref[i : i + 16] = ref[:, 0:BAND]
        last_edge_ref[i : i + 16] = ref[:, width - BAND :]


def adjoint_tables():
    wide = phase_angles(8 * np.arange(64), FREQ)
    c, s = np.cos(wide), np.sin(wide)
    w = np.concatenate([np.concatenate([c, -s], 1), np.concatenate([s, c], 1)], 0)
    near_rows = phase_angles(np.arange(8), FREQ)
    return np.concatenate(constant_split(w), 0), np.concatenate([np.cos(near_rows), np.sin(near_rows)], 0).astype(np.float32)


def adjoint_kernel(got_ref, columns_ref, table_any, turn_any, out_ref, table_ref, turn_ref, sems):
    copies = fetch((table_any, turn_any), (table_ref, turn_ref), sems)
    split = {}
    for h in range(2):
        for g in range(2):
            at = 4 * h + 2 * g
            x = [[got_ref[pl.ds(8 * b + at + i, 64, stride=24), :] for b in range(3)] for i in range(2)]
            split[h, g] = halves(jnp.concatenate([jnp.concatenate(part, 1) for part in x], 0))
    for copy in copies:
        copy.wait()
    table_hi, table_lo = table_ref[0:BAND], table_ref[BAND:]
    c, s = turn_ref[0:8], turn_ref[8:16]
    for g in range(2):
        turned = []
        for t in range(4):
            re, im = columns_ref[t, g : g + 1], columns_ref[t, 2 + g : 3 + g]
            turned.append((c * re - s * im, s * re + c * im))
        a, b = (jnp.concatenate([x[i] for x in turned], 0)[None] for i in range(2))
        for h in range(2):
            hi, lo = split[h, g]
            sides = (((0,), (0,)), ((), ()))
            y = lax.dot_general(hi, table_hi, sides, preferred_element_type=jnp.float32)
            y = y + lax.dot_general(lo, table_hi, sides, preferred_element_type=jnp.float32)
            y = y + lax.dot_general(hi, table_lo, sides, preferred_element_type=jnp.float32)
            y = y.reshape(12, 32, 2 * BAND)
            re, im = y[:, :, :BAND], y[:, :, BAND:]
            out_ref[0, g, 12 * h : 12 * h + 12] = jnp.sum(re * a + im * b, 1)
            out_ref[1, g, 12 * h : 12 * h + 12] = jnp.sum(im * a - re * b, 1)


def total_kernel(x_ref, one_ref, two_ref, three_ref, whole_ref, square_ref):
    whole = (x_ref[...] + two_ref[...]) + (one_ref[...] + three_ref[...])
    whole_ref[...] = whole
    flat = jnp.sum(whole * whole, (0, 1, 2))[None]
    square_ref[...] = jnp.broadcast_to(flat[None], square_ref.shape)


def scale_kernel(whole_ref, squares_ref, out_ref, *, entries):
    total = jnp.sum(jnp.sum(squares_ref[...], 0), 1, keepdims=True)
    factor = lax.rsqrt(total / entries + 1e-06)
    for i in range(2):
        for g in range(2):
            out_ref[i, :, g, :] = whole_ref[i, g] * factor


def fields_block(slabs, row_table, synth, kernel_real, kernel_imaginary, weights, target, near_rows, far_rows, norm):
    kernels = kernel_real.shape[0]
    height, width = target.shape
    tiles, rows = width // TILE, 64 * height
    return pl.pallas_call(
        functools.partial(fields_kernel, rows=rows, norm=norm),
        out_shape=[
            jax.ShapeDtypeStruct((tiles, 8, BAND), jnp.float32),
            pltpu.VMEM((kernels, tiles * height, 2 * TILE), jnp.float32),
            jax.ShapeDtypeStruct((16, width), jnp.float32),
            jax.ShapeDtypeStruct((16, width), jnp.float32),
            jax.ShapeDtypeStruct((32, BAND), jnp.float32),
            jax.ShapeDtypeStruct((32, BAND), jnp.float32),
        ],
        in_specs=[VMEM] * 11 + [HERE] * 7,
        out_specs=[VMEM] * 6,
        scratch_shapes=[
            pltpu.VMEM((2 * BAND, 2 * BAND), jnp.bfloat16),
            pltpu.VMEM((16, 2 * BAND), jnp.float32),
            pltpu.SMEM(weights.shape, jnp.float32),
            pltpu.VMEM((4 * BAND, 2 * TILE), jnp.bfloat16),
            pltpu.VMEM(target.shape, jnp.bfloat16),
            pltpu.VMEM(kernel_real.shape, jnp.float32),
            pltpu.VMEM(kernel_real.shape, jnp.float32),
            pltpu.VMEM((tiles, BAND, 2 * BAND), jnp.float32),
            pltpu.VMEM((2 * rows, 5 * BAND), jnp.bfloat16),
            pltpu.VMEM((2, 256, 2 * BAND), jnp.bfloat16),
            pltpu.VMEM((2, 256, 2 * BAND), jnp.bfloat16),
            pltpu.VMEM((64, 2 * TILE), jnp.float32),
            pltpu.SemaphoreType.DMA((5 + kernels // 2,)),
        ],
        compiler_params=params(28),
        name="fields",
    )(
        *near(*slabs, near_rows, far_rows, row_table),
        *homes(
            expand_table(norm), line_tables(64, height), weights,
            np.concatenate(constant_split(synth), 0), target, kernel_real, kernel_imaginary,
        ),
    )


def on_device(
    layout, target, kernel_real, kernel_imaginary, weights, first_taps, first_bias, second_taps, second_bias
):
    height, width = layout.shape
    tiles = width // TILE
    kernels = kernel_real.shape[0]
    rows, cols = height * 64, width * 4
    r = lax.axis_index(ROW)
    norm = 1.0 / math.sqrt(rows * TILE)

    near_rows = lax.ppermute(target, ROW, [(i, i ^ 1) for i in range(64)])
    far_rows = lax.ppermute(target, ROW, [(i, (i - 1 if i % 2 == 0 else i + 1) % 64) for i in range(64)])

    packed = pl.pallas_call(
        analyse_kernel,
        out_shape=jax.ShapeDtypeStruct((8, 40, BAND), jnp.float32),
        in_specs=[HERE] * 2,
        out_specs=VMEM,
        scratch_shapes=[
            pltpu.VMEM(layout.shape, jnp.bfloat16),
            pltpu.VMEM((2 * TILE, 2 * BAND), jnp.bfloat16),
            pltpu.SemaphoreType.DMA((2,)),
        ],
        compiler_params=params(8),
        name="analyse",
    )(*homes(layout, analysis_table()))
    gathered = lax.all_to_all(packed, "z", 0, 0, tiled=True)
    tables = resist_tables(first_taps, first_bias, second_taps, rows)
    at = 2 * lax.axis_index("y") + lax.axis_index("core")
    row_table = lax.dynamic_index_in_dim(row_transform_tables(), at, 0, keepdims=False)
    gathered, near_rows, far_rows, row_table, *tables = lax.optimization_barrier(
        (gathered, near_rows, far_rows, row_table, *tables)
    )
    gathered = pl.pallas_call(
        repack_kernel,
        out_shape=jax.ShapeDtypeStruct((33, 8, BAND), jnp.float32),
        in_specs=[VMEM],
        out_specs=VMEM,
        compiler_params=params(8),
        name="repack",
    )(gathered)
    slabs = [gathered] + [lax.ppermute(gathered, "y", [(i, (i + k) % 4) for i in range(4)]) for k in (1, 2, 3)]
    slabs = slabs + [lax.ppermute(slab, "core", [(0, 1), (1, 0)]) for slab in slabs]

    synth = synthesis_table(norm)
    columns, fields, intensity, wanted, first_edge, last_edge = fields_block(
        slabs, row_table, synth, kernel_real, kernel_imaginary, weights, target, near_rows, far_rows, norm
    )
    left = lax.ppermute(last_edge, "x", [(i, (i + 1) % 4) for i in range(4)])
    right = lax.ppermute(first_edge, "x", [((i + 1) % 4, i) for i in range(4)])
    back = synth.reshape(2, 64, 2, 2 * TILE).transpose(1, 2, 0, 3).reshape(256, 2 * TILE)
    back = np.concatenate(constant_split(back), 0)
    middle = middle_block(intensity, tables)
    resist, send = resist_block(
        intensity, wanted, left, right, tables, second_bias, weights, fields, middle, back, (rows, cols)
    )

    got = lax.all_to_all(send, ROW, 0, 0, tiled=True)
    table, turn = adjoint_tables()
    mine = pl.pallas_call(
        adjoint_kernel,
        out_shape=jax.ShapeDtypeStruct((2, 2, kernels, BAND), jnp.float32),
        in_specs=[VMEM] * 2 + [HERE] * 2,
        out_specs=VMEM,
        scratch_shapes=[
            pltpu.VMEM(table.shape, jnp.bfloat16),
            pltpu.VMEM(turn.shape, jnp.float32),
            pltpu.SemaphoreType.DMA((2,)),
        ],
        compiler_params=params(12),
        name="adjoint",
    )(*near(got.reshape(64 * 24, BAND), columns), *homes(table, turn))
    others = [lax.ppermute(mine, "x", [(i, (i + k) % 4) for i in range(4)]) for k in (1, 2, 3)]
    whole, squares = pl.pallas_call(
        total_kernel,
        out_shape=[jax.ShapeDtypeStruct(mine.shape, jnp.float32), jax.ShapeDtypeStruct((64, 1, BAND), jnp.float32)],
        in_specs=[VMEM] * 4,
        out_specs=[VMEM] * 2,
        compiler_params=params(8),
        name="total",
    )(mine, *others)
    squares = lax.all_to_all(squares, ROW, 0, 0, tiled=True)
    grads = pl.pallas_call(
        functools.partial(scale_kernel, entries=2 * kernels * BAND * BAND),
        out_shape=jax.ShapeDtypeStruct((2, kernels, 2, BAND), jnp.float32),
        in_specs=[VMEM] * 2,
        out_specs=VMEM,
        compiler_params=params(8),
        name="scale",
    )(whole, squares)
    return resist, grads.transpose(0, 1, 3, 2)


def solution(mesh):
    devices = mesh.devices.reshape(4, 8, 2, 4)
    fine = Mesh(devices, ALL)
    grid = P(ROW, "x")
    in_specs = (grid, grid, P(), P(), P(), P(), P(), P(), P())
    out_specs = (grid, P(None, None, None, ROW))
    return jax.shard_map(on_device, mesh=fine, in_specs=in_specs, out_specs=out_specs, check_vma=False)
```

```python
import functools
import math

import jax
import jax.numpy as jnp
import numpy as np
from jax import lax
from jax.experimental import pallas as pl
from jax.experimental.pallas import tpu as pltpu
from jax.sharding import Mesh, PartitionSpec as P

TILE = 512
BAND = 128
ROW = ("y", "z", "core")
ALL = ("y", "z", "core", "x")


def phase_angles(freqs, positions):
    return 2.0 * math.pi * ((freqs[:, None] * positions[None, :]) % TILE) / TILE


def dot(a, b):
    return jnp.dot(a, b, preferred_element_type=jnp.float32)


def constant_split(x):
    x = np.asarray(x, np.float32)
    hi = x.astype(jnp.bfloat16)
    return hi, (x - hi.astype(np.float32)).astype(jnp.bfloat16)


VMEM = pl.BlockSpec(memory_space=pltpu.VMEM)
SMEM = pl.BlockSpec(memory_space=pltpu.SMEM)
HERE = pl.BlockSpec(memory_space=pltpu.HBM)


def near(*arrays):
    return [pltpu.with_memory_space_constraint(jnp.asarray(x), pltpu.VMEM) for x in arrays]


def homes(*arrays):
    return [pltpu.with_memory_space_constraint(jnp.asarray(x), pltpu.HBM) for x in arrays]


def fetch(sources, targets, sems):
    copies = [pltpu.make_async_copy(a, b, sems.at[i]) for i, (a, b) in enumerate(zip(sources, targets, strict=True))]
    for copy in copies:
        copy.start()
    return copies


def params(mib):
    return pltpu.CompilerParams(vmem_limit_bytes=mib * 1024 * 1024)


FREQ = np.arange(BAND) - BAND // 2


def analysis_table():
    ang = phase_angles(np.arange(65), np.arange(TILE))
    table = np.zeros((TILE, 2 * BAND))
    table[:, :64], table[:, 64:BAND] = np.cos(ang[:64]).T, np.sin(ang[1:]).T
    table[:, BAND : BAND + 4] = np.cos(ang[64])[:, None]
    return np.concatenate(constant_split(table), 0)


def row_transform_tables():
    tables = []
    for y in range(4):
        for core in range(2):
            slabs = [128 * ((y - k) % 4) + 8 * (core ^ other) for other in range(2) for k in range(4)]
            n = (np.array(slabs)[:, None, None] + 16 * np.arange(8)[:, None] + np.arange(8)).reshape(-1)
            ang = phase_angles(FREQ, n)
            tables.append(np.concatenate(constant_split(np.concatenate([np.cos(ang), np.sin(ang)], 0)), 0))
    return np.stack(tables)


def expand_table(norm):
    table = np.zeros((2, BAND, 2, BAND))
    for g in range(BAND):
        q = g - 64
        m = abs(q)
        if m < 64:
            table[0, m, 0, g] = 1.0
            table[1, m, 1, g] = -1.0
        if m:
            sign = -1.0 if q > 0 else 1.0
            table[1, 63 + m, 0, g] = sign
            table[0, 63 + m, 1, g] = sign
    return (table.reshape(2 * BAND, 2 * BAND) * norm).astype(jnp.bfloat16)


def synthesis_table(norm):
    ang = phase_angles(FREQ, np.arange(TILE))
    c, s = np.cos(ang), np.sin(ang)
    return np.concatenate([np.concatenate([c, s], 1), np.concatenate([-s, c], 1)], 0) * norm


def line_tables(groups, height):
    at = np.arange(groups)[:, None] * height + np.array(FIELD_ROWS)[None, :]
    ang = phase_angles(at.reshape(-1), FREQ)
    return np.concatenate([np.cos(ang), np.sin(ang)], 1).reshape(groups, 16, 2 * BAND).astype(np.float32)


FIELD_ROWS = list(range(8)) + [-4, -3, -2, -1, 8, 9, 10, 11]
HIDDEN_ROWS = list(range(-1, 9)) + [-3, -2, 9, 10]
SLOPE_ROWS = list(range(8)) + [-2, -1, 8, 9] + [None] * 4
WIDE = 17 * 128


def halves(x):
    hi = x.astype(jnp.bfloat16)
    return hi, (x - hi.astype(jnp.float32)).astype(jnp.bfloat16)


def pick(out_rows, in_rows, sign):
    hit = lambda a, b, dy: float(a is not None and b is not None and b - a == sign * (dy - 1))
    return np.array([[[hit(a, b, dy) for b in in_rows] for a in out_rows] for dy in range(3)])


INNER = HIDDEN_ROWS[:10]
CHANNELS = 64


def choose_tables():
    choose = np.zeros((3, 48, 7, 256))
    for dy in range(3):
        for dx in range(3):
            for slot in range(16):
                lane = 16 * dx + slot
                for part, section in ((0, 0), (1, 1), (0, 2)):
                    choose[part, 3 * dy + dx, dy, 48 * section + lane] = 1.0
                    choose[part, 16 + 3 * dy + dx, 4 + dy, 48 * section + lane] = 1.0
    for part in range(3):
        choose[part, 32, 3, 144 + part] = 1.0
    return choose.reshape(144, 7 * 256).astype(jnp.bfloat16)


def lane_masks():
    fore = pick(HIDDEN_ROWS, FIELD_ROWS, 1).transpose(1, 0, 2)
    back = pick(INNER, SLOPE_ROWS, -1).transpose(1, 0, 2)
    masks = np.zeros((80, 256), np.float32)
    masks[:42, :144] = np.tile(fore, (1, 1, 9)).reshape(42, 144)
    masks[42:72, :144] = np.tile(back, (1, 1, 9)).reshape(30, 144)
    return masks


def row_masks():
    fore = np.repeat(pick(SLOPE_ROWS, HIDDEN_ROWS, 1), CHANNELS, 2)
    back = np.repeat(pick(list(range(8)), INNER, -1), CHANNELS, 2)
    return fore.astype(np.float32), back.astype(np.float32)


def tables_kernel(
    first_taps_any, second_taps_any, bias_any, choose_any, lane_masks_any, fore_any, aft_any,
    first_ref, second_ref, second_back_ref, first_back_ref,
    first_taps_ref, second_taps_ref, bias_ref, choose_ref, lane_masks_ref, fore_ref, aft_ref, wide_ref, sems, *, rows
):
    sources = (first_taps_any, second_taps_any, bias_any, choose_any, lane_masks_any, fore_any, aft_any)
    targets = (first_taps_ref, second_taps_ref, bias_ref, choose_ref, lane_masks_ref, fore_ref, aft_ref)
    for copy in fetch(sources, targets, sems):
        copy.wait()
    row0 = lax.axis_index(ROW) * 8
    wide_ref[...] = jnp.zeros_like(wide_ref)
    wide_ref[0:9, 0:CHANNELS] = first_taps_ref[...]
    wide_ref[16:25, 0:CHANNELS] = second_taps_ref[...]
    wide_ref[32:33, 0:CHANNELS] = bias_ref[...]
    tall = wide_ref[...].T[:CHANNELS, :48]
    hi = tall.astype(jnp.bfloat16)
    rest = tall - hi.astype(jnp.float32)
    mid = rest.astype(jnp.bfloat16)
    low = (rest - mid.astype(jnp.float32)).astype(jnp.bfloat16)
    parts = dot(jnp.concatenate([hi, mid, low], 1), choose_ref[...])
    for h, n in enumerate(HIDDEN_ROWS):
        here = row0 + n
        valid = jnp.where((here >= 0) & (here < rows), 1.0, 0.0)
        block = parts[:, 768:1024]
        for dy in range(3):
            block = block + parts[:, 256 * dy : 256 * dy + 256] * lane_masks_ref[3 * h + dy : 3 * h + dy + 1]
        first_ref[64 * h : 64 * h + 64] = (block * valid)[:, :160].astype(jnp.bfloat16)
        if h < 10:
            block = 0.0
            for dy in range(3):
                at = 1024 + 256 * dy
                block = block + parts[:, at : at + 256] * lane_masks_ref[42 + 3 * h + dy : 43 + 3 * h + dy]
            second_back_ref[64 * h : 64 * h + 64] = (block * valid)[:, :144].astype(jnp.bfloat16)
    for taps_ref, mask_ref, out_ref, height in ((second_taps_ref, fore_ref, second_ref, 16), (first_taps_ref, aft_ref, first_back_ref, 8)):
        lanes = out_ref.shape[1]
        taps = taps_ref[...]
        taps = jnp.concatenate([taps] * (lanes // CHANNELS), 1)
        taps_hi = taps.astype(jnp.bfloat16).astype(jnp.float32)
        for at, part in ((0, taps_hi), (out_ref.shape[0] // 2, taps - taps_hi)):
            blocks = []
            for dx in range(3):
                block = 0.0
                for dy in range(3):
                    block = block + part[3 * dy + dx : 3 * dy + dx + 1] * mask_ref[dy]
                blocks.append(block)
            if height == 8:
                blocks.append(jnp.zeros((8, lanes), jnp.float32))
            whole = jnp.concatenate(blocks, 0)
            out_ref[at : at + whole.shape[0]] = whole.astype(jnp.bfloat16)


def resist_tables(first_taps, first_bias, second_taps, rows):
    args = (first_taps, second_taps, first_bias.reshape(1, -1), choose_tables(), lane_masks(), *row_masks())
    return pl.pallas_call(
        functools.partial(tables_kernel, rows=rows),
        out_shape=[
            jax.ShapeDtypeStruct((14 * CHANNELS, 160), jnp.bfloat16),
            jax.ShapeDtypeStruct((96, 14 * CHANNELS), jnp.bfloat16),
            jax.ShapeDtypeStruct((10 * CHANNELS, 144), jnp.bfloat16),
            jax.ShapeDtypeStruct((64, 10 * CHANNELS), jnp.bfloat16),
        ],
        in_specs=[HERE] * 7,
        out_specs=[VMEM] * 4,
        scratch_shapes=[pltpu.VMEM(a.shape, a.dtype) for a in args]
        + [pltpu.VMEM((BAND, BAND), jnp.float32), pltpu.SemaphoreType.DMA((7,))],
        compiler_params=params(12),
        name="tables",
    )(*homes(*args))


SIDE = 256


def hide(first_ref, second_ref, views_ref, here, inner):
    hidden = jnp.tanh(dot(first_ref[...], views_ref[:, here]))
    hi, lo = halves(hidden)
    both = dot(second_ref[...], hi)
    return both[:48] + both[48:] + dot(second_ref[0:48], lo), 1.0 - hidden[:inner] * hidden[:inner]


def place_views(views_ref, dx, moved):
    hi, lo = halves(moved)
    views_ref[16 * dx : 16 * dx + 16] = hi
    views_ref[48 + 16 * dx : 64 + 16 * dx] = hi
    views_ref[96 + 16 * dx : 112 + 16 * dx] = lo


def middle_kernel(field_ref, first_ref, second_ref, mixed_ref, keep_ref, views_ref):
    width = field_ref.shape[1]
    for dx in range(3):
        place_views(views_ref, dx, field_ref[...] if dx == 1 else pltpu.roll(field_ref[...], (1 - dx) % width, 1))
    views_ref[144:160] = jnp.ones((16, width), jnp.bfloat16)

    def step(i, carry):
        at = pl.multiple_of(i * 768, 256)
        there = pl.ds(pl.multiple_of(at + SIDE, 256), 768)
        mixed_ref[:, pl.ds(at, 768)], keep_ref[:, pl.ds(at, 768)] = hide(first_ref, second_ref, views_ref, there, keep_ref.shape[0])
        return carry

    lax.fori_loop(0, (width - 2 * SIDE) // 768, step, 0)


def resist_kernel(
    field_ref, target_ref, left_ref, right_ref, first_ref, second_ref, second_back_ref, first_back_ref, offset_ref,
    fields_ref, mixed_mid_ref, keep_mid_ref, weights_any, back_any,
    resist_any, out_ref, resist_ref, weights_ref, back_ref,
    views_ref, keep_ref, mixed_ref, spread_ref, summed_ref, all_ref, sems, *, rows, cols
):
    copies = fetch((weights_any, back_any), (weights_ref, back_ref), sems)
    row0 = lax.axis_index(ROW) * resist_ref.shape[0]
    col0 = lax.axis_index("x") * resist_ref.shape[1]
    width = resist_ref.shape[1]
    inner = keep_ref.shape[0]

    def columns(shape):
        lane = lax.broadcasted_iota(jnp.int32, shape, 1)
        m = jnp.where(lane < width + 64, lane, lane - WIDE)
        return m, (col0 + m >= 0) & (col0 + m < cols)

    m, in_grid = columns((16, WIDE))
    keep_col = (in_grid & (m >= -3) & (m < width + 3)).astype(jnp.float32)
    lane = lax.broadcasted_iota(jnp.int32, (16, BAND), 1)
    gap = [jnp.where(lane < 64, right_ref[i : i + 16], left_ref[i : i + 16]) for i in (0, 16)]
    field = jnp.concatenate([field_ref[...], jnp.where(in_grid[:, width:], gap[0], 0.0)], 1)
    target = jnp.concatenate([target_ref[...], gap[1]], 1)
    for dx in range(3):
        place_views(views_ref, dx, (field if dx == 1 else pltpu.roll(field, (1 - dx) % WIDE, 1)) * keep_col)
    views_ref[144:160] = keep_col.astype(jnp.bfloat16)

    edges = (slice(0, SIDE), slice(width - SIDE, width), slice(width, WIDE))
    kept = (slice(0, SIDE), slice(SIDE, 2 * SIDE), slice(2 * SIDE, 2 * SIDE + BAND))
    mixed_ref[:, SIDE : width - SIDE] = mixed_mid_ref[...]
    for here, place in zip(edges, kept, strict=True):
        mixed_ref[:, here], keep_ref[:, place] = hide(first_ref, second_ref, views_ref, here, inner)

    logits = offset_ref[0] + mixed_ref[16:32] + pltpu.roll(mixed_ref[0:16], 1, 1) + pltpu.roll(mixed_ref[32:48], WIDE - 1, 1)
    resist = 1.0 / (1.0 + jnp.exp(-logits))
    resist_ref[...] = resist[:8, :width]
    sent = pltpu.make_async_copy(resist_ref, resist_any, sems.at[2])
    sent.start()
    slot = lax.broadcasted_iota(jnp.int32, (16, WIDE), 0)
    n = jnp.where(slot < 8, slot, jnp.where(slot < 10, slot - 10, slot - 2))
    use = in_grid & (m >= -2) & (m < width + 2) & (slot < 12) & (row0 + n >= 0) & (row0 + n < rows)
    slope = jnp.where(use, (resist - target) * (TILE / cols), 0.0)
    grid_col = in_grid.astype(jnp.float32)
    for dx in range(3):
        place_views(spread_ref, dx, (slope if dx == 1 else pltpu.roll(slope, (dx - 1) % WIDE, 1)) * grid_col)

    def backward(here, kept):
        hidden_grad = dot(second_back_ref[...], spread_ref[:, here])
        hi, lo = halves(hidden_grad * kept)
        both = dot(first_back_ref[...], hi)
        summed_ref[:, here] = both[:32] + both[32:] + dot(first_back_ref[0:32], lo)

    def middle(i, carry):
        at = pl.multiple_of(i * 768, 256)
        backward(pl.ds(pl.multiple_of(SIDE + at, 256), 768), keep_mid_ref[:, pl.ds(at, 768)])
        return carry

    lax.fori_loop(0, keep_mid_ref.shape[1] // 768, middle, 0)
    for here, place in zip(edges, kept, strict=True):
        backward(here, keep_ref[:, place])
    grad = summed_ref[8:16] + pltpu.roll(summed_ref[0:8], WIDE - 1, 1) + pltpu.roll(summed_ref[16:24], 1, 1)
    for copy in copies:
        copy.wait()
    grad = jnp.concatenate([grad[:, t * TILE : (t + 1) * TILE] for t in range(4)], 0)
    grad = jnp.concatenate([grad, grad], 1) * 2.0
    half = back_ref.shape[0] // 2
    for i in range(3):
        piece = jnp.concatenate([fields_ref[8 * i + j] * (grad * weights_ref[8 * i + j]) for j in range(8)], 0)
        hi, lo = halves(piece)
        sides = (((1,), (1,)), ((), ()))
        both = lax.dot_general(back_ref[...], hi, sides, preferred_element_type=jnp.float32)
        small = lax.dot_general(back_ref[0:half], lo, sides, preferred_element_type=jnp.float32)
        all_ref[:, 256 * i : 256 * i + 256] = both[:half] + both[half:] + small
    low = lax.broadcasted_iota(jnp.int32, (8, 384), 0) < 4
    for d in range(32):
        first, second = all_ref[8 * d : 8 * d + 8, 0:384], all_ref[8 * d : 8 * d + 8, 384:768]
        even, odd = jnp.where(low, first, pltpu.roll(second, 4, 0)), jnp.where(low, pltpu.roll(first, 4, 0), second)
        for b in range(3):
            out_ref[2 * d, 8 * b : 8 * b + 8] = even[:, BAND * b : BAND * (b + 1)]
            out_ref[2 * d + 1, 8 * b : 8 * b + 8] = odd[:, BAND * b : BAND * (b + 1)]
    sent.wait()


def middle_block(field, tables):
    inner, width = tables[2].shape[0], field.shape[1]
    return pl.pallas_call(
        middle_kernel,
        out_shape=[pltpu.VMEM((48, width - 2 * SIDE), jnp.float32), pltpu.VMEM((inner, width - 2 * SIDE), jnp.float32)],
        in_specs=[VMEM] * 3,
        out_specs=[VMEM] * 2,
        scratch_shapes=[pltpu.VMEM((160, width), jnp.bfloat16)],
        compiler_params=params(24),
        name="middle",
    )(*near(field, tables[0], tables[1]))


def resist_block(field, target, left, right, tables, second_bias, weights, fields, middle, back, dims):
    rows, cols = dims
    inner, width = tables[2].shape[0], field.shape[1]
    return pl.pallas_call(
        functools.partial(resist_kernel, rows=rows, cols=cols),
        out_shape=[pltpu.HBM((8, width), jnp.float32), pltpu.VMEM((64, 24, BAND), jnp.float32)],
        in_specs=[VMEM] * 8 + [SMEM] + [VMEM] * 3 + [HERE] * 2,
        out_specs=[HERE, VMEM],
        scratch_shapes=[
            pltpu.VMEM((8, width), jnp.float32),
            pltpu.SMEM(weights.shape, jnp.float32),
            pltpu.VMEM(back.shape, jnp.bfloat16),
            pltpu.VMEM((160, WIDE), jnp.bfloat16),
            pltpu.VMEM((inner, 2 * SIDE + BAND), jnp.float32),
            pltpu.VMEM((48, WIDE), jnp.float32),
            pltpu.VMEM((144, WIDE), jnp.bfloat16),
            pltpu.VMEM((32, WIDE), jnp.float32),
            pltpu.VMEM((256, 768), jnp.float32),
            pltpu.SemaphoreType.DMA((3,)),
        ],
        compiler_params=params(28),
        name="resist",
    )(field, target, left, right, *tables, second_bias, *near(fields, *middle), *homes(weights, back))


def analyse_kernel(layout_any, table_any, out_ref, layout_ref, table_ref, sems):
    for copy in fetch((layout_any, table_any), (layout_ref, table_ref), sems):
        copy.wait()
    x = layout_ref[...].astype(jnp.float32)
    x = jnp.concatenate([x[:, t * TILE : (t + 1) * TILE] for t in range(4)], 0).astype(jnp.bfloat16)
    sums = dot(x, table_ref[0:TILE]) + dot(x, table_ref[TILE:])
    lane = lax.broadcasted_iota(jnp.int32, (8, BAND), 1)
    last = jnp.zeros((8, BAND), jnp.float32)
    for t in range(4):
        last = jnp.where(lane == t, sums[8 * t : 8 * t + 8, BAND:], last)
    packed = jnp.concatenate([sums[:, :BAND], last], 0)
    for i in range(out_ref.shape[0]):
        out_ref[i] = packed


def repack_kernel(in_ref, out_ref):
    last = in_ref[0, 32:40]
    for z in range(8):
        for t in range(4):
            out_ref[4 * z + t] = in_ref[z, 8 * t : 8 * t + 8]
        if z:
            last = last + pltpu.roll(in_ref[z, 32:40], 4 * z, 1)
    out_ref[32] = last


def fields_kernel(*refs, rows, norm):
    slabs, refs = refs[:8], refs[8:]
    (
        near_rows_ref, far_rows_ref, rows_ref, expand_any, line_any, weights_any, synth_any, target_any, real_any, imag_any,
        cols_ref, fields_ref, intensity_ref, wanted_ref, first_edge_ref, last_edge_ref, *refs
    ) = refs
    (
        expand_ref, line_ref, weights_ref, synth_ref, target_ref, real_ref, imag_ref,
        spec_ref, seen_ref, line_hi_ref, line_lo_ref, sum_ref, sems
    ) = refs
    r = lax.axis_index(ROW)
    sources = [expand_any, line_any.at[r], weights_any, synth_any, target_any]
    targets = [expand_ref, line_ref, weights_ref, synth_ref, target_ref]
    for i in range(0, real_ref.shape[0], 4):
        sources += [real_any.at[i : i + 4], imag_any.at[i : i + 4]]
        targets += [real_ref.at[i : i + 4], imag_ref.at[i : i + 4]]
    copies = fetch(sources, targets, sems)
    row0 = r * 8
    kernels = real_ref.shape[0]
    for p, slab in enumerate(slabs):
        last = slab[32]
        last = jnp.concatenate([pltpu.roll(last, (BAND - 4 * z) % BAND, 1) if z else last for z in range(8)], 0)
        for t in range(5):
            tile = jnp.concatenate([slab[4 * z + t] for z in range(8)], 0) if t < 4 else last
            hi, lo = halves(tile)
            seen_ref[64 * p : 64 * p + 64, t * BAND : (t + 1) * BAND] = hi
            seen_ref[rows + 64 * p : rows + 64 * p + 64, t * BAND : (t + 1) * BAND] = lo
    table_hi = rows_ref[0 : 2 * BAND]
    u = dot(table_hi, seen_ref[0:rows]) + dot(rows_ref[2 * BAND :], seen_ref[0:rows]) + dot(table_hi, seen_ref[rows:])

    def pair(t):
        both = u[:, t * BAND : (t + 1) * BAND]
        return halves(jnp.concatenate([both[:BAND], both[BAND:]], 1))

    copies[0].wait()
    lane = lax.broadcasted_iota(jnp.int32, (BAND, 2 * BAND), 1)
    last = u[:, 4 * BAND :] * norm
    for t in range(4):
        hi, lo = pair(t)
        moved = pltpu.roll(last, (BAND - t) % BAND, 1)
        moved = jnp.concatenate([moved[:BAND], -moved[BAND:]], 1)
        spec_ref[t] = dot(hi, expand_ref[...]) + dot(lo, expand_ref[...]) + jnp.where((lane == 0) | (lane == BAND), moved, 0.0)

    copies[1].wait()
    phase = line_ref[...]
    c, s = phase[:, :BAND], phase[:, BAND:]
    table = jnp.concatenate([jnp.concatenate([c, -s], 1), jnp.concatenate([s, c], 1)], 0)
    lines_hi, lines_lo = halves(table)
    lines_both = jnp.concatenate([lines_hi, lines_lo], 0)
    sum_ref[...] = jnp.zeros_like(sum_ref)

    def lines(k, slot, j):
        kr, ki = real_ref[k], imag_ref[k]
        pieces = []
        for p in range(2):
            columns = []
            for t in (2 * p, 2 * p + 1):
                sr, si = spec_ref[t, :, :BAND], spec_ref[t, :, BAND:]
                columns.append(jnp.concatenate([kr * sr - ki * si, kr * si + ki * sr], 0))
            hi, lo = halves(jnp.concatenate(columns, 1))
            both = dot(lines_both, hi)
            out = both[:32] + both[32:] + dot(lines_hi, lo)
            for t in range(2):
                pieces.append(jnp.concatenate([out[:16, t * BAND : (t + 1) * BAND], out[16:, t * BAND : (t + 1) * BAND]], 1))
        hi, lo = halves(jnp.concatenate(pieces, 0))
        line_hi_ref[slot, 64 * j : 64 * j + 64] = hi
        line_lo_ref[slot, 64 * j : 64 * j + 64] = lo

    def waves(k0, slot, q):
        here = slice(q * 256, q * 256 + 256)
        synth_hi = synth_ref[0 : 2 * BAND, here]
        line_hi = line_hi_ref[slot]
        f = dot(line_hi, synth_hi) + dot(line_lo_ref[slot], synth_hi) + dot(line_hi, synth_ref[2 * BAND :, here])
        total = sum_ref[:, here]
        for j in range(4):
            part = f[64 * j : 64 * j + 64]
            total = total + weights_ref[k0 + j] * (part * part)
            fields_ref[k0 + j, :, here] = jnp.concatenate([part[16 * t : 16 * t + 8] for t in range(4)], 0)
        sum_ref[:, here] = total

    for copy in copies[5:7]:
        copy.wait()
    for j in range(4):
        lines(j, 0, j)
    for copy in copies[2:5]:
        copy.wait()
    for copy in copies[7:]:
        copy.wait()

    def group(i, slot, more):
        for j in range(4):
            waves(4 * i, slot, j)
            if more:
                lines(4 * i + 4 + j, 1 - slot, j)

    def both(m, carry):
        group(2 * m, 0, True)
        group(2 * m + 1, 1, True)
        return carry

    lax.fori_loop(0, 2, both, 0)
    group(4, 0, True)
    group(5, 1, False)
    row = lax.broadcasted_iota(jnp.int32, (16, 2 * BAND), 0)
    lane = lax.broadcasted_iota(jnp.int32, (16, 2 * BAND), 1)
    chosen = ((row < 4) & (lane == 2 * r + row % 2 + BAND * (row // 2))).astype(jnp.bfloat16)
    for t in range(4):
        hi, lo = halves(spec_ref[t])
        sides = (((1,), (1,)), ((), ()))
        picked = lax.dot_general(chosen, hi, sides, preferred_element_type=jnp.float32)
        cols_ref[t] = (picked + lax.dot_general(chosen, lo, sides, preferred_element_type=jnp.float32))[:8]
    slot = lax.broadcasted_iota(jnp.int32, (16, TILE), 0)
    n = row0 + jnp.where(slot < 8, slot, jnp.where(slot < 12, slot - 12, slot - 4))
    inside = (n >= 0) & (n < rows)
    for t in range(4):
        both = sum_ref[16 * t : 16 * t + 16]
        intensity_ref[:, t * TILE : (t + 1) * TILE] = jnp.where(inside, both[:, :TILE] + both[:, TILE:], 0.0)
    wanted_ref[0:8] = target_ref[...].astype(jnp.float32)
    one, other = near_rows_ref[...].astype(jnp.float32), far_rows_ref[...].astype(jnp.float32)
    even = r % 2 == 0
    above, below = jnp.where(even, other, one), jnp.where(even, one, other)
    wanted_ref[8:16] = jnp.concatenate([above[6:8], below[0:2], jnp.zeros((4, above.shape[1]), jnp.float32)], 0)
    width = intensity_ref.shape[1]
    for i, ref in ((0, intensity_ref), (16, wanted_ref)):
        first_edge_ref[i : i + 16] = ref[:, 0:BAND]
        last_edge_ref[i : i + 16] = ref[:, width - BAND :]


def adjoint_tables():
    wide = phase_angles(8 * np.arange(64), FREQ)
    c, s = np.cos(wide), np.sin(wide)
    w = np.concatenate([np.concatenate([c, -s], 1), np.concatenate([s, c], 1)], 0)
    near_rows = phase_angles(np.arange(8), FREQ)
    return np.concatenate(constant_split(w), 0), np.concatenate([np.cos(near_rows), np.sin(near_rows)], 0).astype(np.float32)


def adjoint_kernel(got_ref, columns_ref, table_any, turn_any, out_ref, table_ref, turn_ref, sems):
    copies = fetch((table_any, turn_any), (table_ref, turn_ref), sems)
    split = {}
    for h in range(2):
        for g in range(2):
            at = 4 * h + 2 * g
            x = [[got_ref[pl.ds(8 * b + at + i, 64, stride=24), :] for b in range(3)] for i in range(2)]
            split[h, g] = halves(jnp.concatenate([jnp.concatenate(part, 1) for part in x], 0))
    for copy in copies:
        copy.wait()
    table_hi, table_lo = table_ref[0:BAND], table_ref[BAND:]
    c, s = turn_ref[0:8], turn_ref[8:16]
    for g in range(2):
        turned = []
        for t in range(4):
            re, im = columns_ref[t, g : g + 1], columns_ref[t, 2 + g : 3 + g]
            turned.append((c * re - s * im, s * re + c * im))
        a, b = (jnp.concatenate([x[i] for x in turned], 0)[None] for i in range(2))
        for h in range(2):
            hi, lo = split[h, g]
            sides = (((0,), (0,)), ((), ()))
            y = lax.dot_general(hi, table_hi, sides, preferred_element_type=jnp.float32)
            y = y + lax.dot_general(lo, table_hi, sides, preferred_element_type=jnp.float32)
            y = y + lax.dot_general(hi, table_lo, sides, preferred_element_type=jnp.float32)
            y = y.reshape(12, 32, 2 * BAND)
            re, im = y[:, :, :BAND], y[:, :, BAND:]
            out_ref[0, g, 12 * h : 12 * h + 12] = jnp.sum(re * a + im * b, 1)
            out_ref[1, g, 12 * h : 12 * h + 12] = jnp.sum(im * a - re * b, 1)


def total_kernel(x_ref, one_ref, two_ref, three_ref, whole_ref, square_ref):
    whole = (x_ref[...] + two_ref[...]) + (one_ref[...] + three_ref[...])
    whole_ref[...] = whole
    flat = jnp.sum(whole * whole, (0, 1, 2))[None]
    square_ref[...] = jnp.broadcast_to(flat[None], square_ref.shape)


def scale_kernel(whole_ref, squares_ref, out_ref, *, entries):
    total = jnp.sum(jnp.sum(squares_ref[...], 0), 1, keepdims=True)
    factor = lax.rsqrt(total / entries + 1e-06)
    for i in range(2):
        for g in range(2):
            out_ref[i, :, g, :] = whole_ref[i, g] * factor


def fields_block(slabs, row_table, synth, kernel_real, kernel_imaginary, weights, target, near_rows, far_rows, norm):
    kernels = kernel_real.shape[0]
    height, width = target.shape
    tiles, rows = width // TILE, 64 * height
    return pl.pallas_call(
        functools.partial(fields_kernel, rows=rows, norm=norm),
        out_shape=[
            jax.ShapeDtypeStruct((tiles, 8, BAND), jnp.float32),
            pltpu.VMEM((kernels, tiles * height, 2 * TILE), jnp.float32),
            jax.ShapeDtypeStruct((16, width), jnp.float32),
            jax.ShapeDtypeStruct((16, width), jnp.float32),
            jax.ShapeDtypeStruct((32, BAND), jnp.float32),
            jax.ShapeDtypeStruct((32, BAND), jnp.float32),
        ],
        in_specs=[VMEM] * 11 + [HERE] * 7,
        out_specs=[VMEM] * 6,
        scratch_shapes=[
            pltpu.VMEM((2 * BAND, 2 * BAND), jnp.bfloat16),
            pltpu.VMEM((16, 2 * BAND), jnp.float32),
            pltpu.SMEM(weights.shape, jnp.float32),
            pltpu.VMEM((4 * BAND, 2 * TILE), jnp.bfloat16),
            pltpu.VMEM(target.shape, jnp.bfloat16),
            pltpu.VMEM(kernel_real.shape, jnp.float32),
            pltpu.VMEM(kernel_real.shape, jnp.float32),
            pltpu.VMEM((tiles, BAND, 2 * BAND), jnp.float32),
            pltpu.VMEM((2 * rows, 5 * BAND), jnp.bfloat16),
            pltpu.VMEM((2, 256, 2 * BAND), jnp.bfloat16),
            pltpu.VMEM((2, 256, 2 * BAND), jnp.bfloat16),
            pltpu.VMEM((64, 2 * TILE), jnp.float32),
            pltpu.SemaphoreType.DMA((5 + kernels // 2,)),
        ],
        compiler_params=params(28),
        name="fields",
    )(
        *near(*slabs, near_rows, far_rows, row_table),
        *homes(
            expand_table(norm), line_tables(64, height), weights,
            np.concatenate(constant_split(synth), 0), target, kernel_real, kernel_imaginary,
        ),
    )


def on_device(
    layout, target, kernel_real, kernel_imaginary, weights, first_taps, first_bias, second_taps, second_bias
):
    height, width = layout.shape
    tiles = width // TILE
    kernels = kernel_real.shape[0]
    rows, cols = height * 64, width * 4
    r = lax.axis_index(ROW)
    norm = 1.0 / math.sqrt(rows * TILE)

    near_rows = lax.ppermute(target, ROW, [(i, i ^ 1) for i in range(64)])
    far_rows = lax.ppermute(target, ROW, [(i, (i - 1 if i % 2 == 0 else i + 1) % 64) for i in range(64)])

    packed = pl.pallas_call(
        analyse_kernel,
        out_shape=jax.ShapeDtypeStruct((8, 40, BAND), jnp.float32),
        in_specs=[HERE] * 2,
        out_specs=VMEM,
        scratch_shapes=[
            pltpu.VMEM(layout.shape, jnp.bfloat16),
            pltpu.VMEM((2 * TILE, 2 * BAND), jnp.bfloat16),
            pltpu.SemaphoreType.DMA((2,)),
        ],
        compiler_params=params(8),
        name="analyse",
    )(*homes(layout, analysis_table()))
    gathered = lax.all_to_all(packed, "z", 0, 0, tiled=True)
    tables = resist_tables(first_taps, first_bias, second_taps, rows)
    at = 2 * lax.axis_index("y") + lax.axis_index("core")
    row_table = lax.dynamic_index_in_dim(row_transform_tables(), at, 0, keepdims=False)
    gathered, near_rows, far_rows, row_table, *tables = lax.optimization_barrier(
        (gathered, near_rows, far_rows, row_table, *tables)
    )
    gathered = pl.pallas_call(
        repack_kernel,
        out_shape=jax.ShapeDtypeStruct((33, 8, BAND), jnp.float32),
        in_specs=[VMEM],
        out_specs=VMEM,
        compiler_params=params(8),
        name="repack",
    )(gathered)
    slabs = [gathered] + [lax.ppermute(gathered, "y", [(i, (i + k) % 4) for i in range(4)]) for k in (1, 2, 3)]
    slabs = slabs + [lax.ppermute(slab, "core", [(0, 1), (1, 0)]) for slab in slabs]

    synth = synthesis_table(norm)
    columns, fields, intensity, wanted, first_edge, last_edge = fields_block(
        slabs, row_table, synth, kernel_real, kernel_imaginary, weights, target, near_rows, far_rows, norm
    )
    left = lax.ppermute(last_edge, "x", [(i, (i + 1) % 4) for i in range(4)])
    right = lax.ppermute(first_edge, "x", [((i + 1) % 4, i) for i in range(4)])
    back = synth.reshape(2, 64, 2, 2 * TILE).transpose(1, 2, 0, 3).reshape(256, 2 * TILE)
    back = np.concatenate(constant_split(back), 0)
    middle = middle_block(intensity, tables)
    resist, send = resist_block(
        intensity, wanted, left, right, tables, second_bias, weights, fields, middle, back, (rows, cols)
    )

    got = lax.all_to_all(send, ROW, 0, 0, tiled=True)
    table, turn = adjoint_tables()
    mine = pl.pallas_call(
        adjoint_kernel,
        out_shape=jax.ShapeDtypeStruct((2, 2, kernels, BAND), jnp.float32),
        in_specs=[VMEM] * 2 + [HERE] * 2,
        out_specs=VMEM,
        scratch_shapes=[
            pltpu.VMEM(table.shape, jnp.bfloat16),
            pltpu.VMEM(turn.shape, jnp.float32),
            pltpu.SemaphoreType.DMA((2,)),
        ],
        compiler_params=params(12),
        name="adjoint",
    )(*near(got.reshape(64 * 24, BAND), columns), *homes(table, turn))
    others = [lax.ppermute(mine, "x", [(i, (i + k) % 4) for i in range(4)]) for k in (1, 2, 3)]
    whole, squares = pl.pallas_call(
        total_kernel,
        out_shape=[jax.ShapeDtypeStruct(mine.shape, jnp.float32), jax.ShapeDtypeStruct((64, 1, BAND), jnp.float32)],
        in_specs=[VMEM] * 4,
        out_specs=[VMEM] * 2,
        compiler_params=params(8),
        name="total",
    )(mine, *others)
    squares = lax.all_to_all(squares, ROW, 0, 0, tiled=True)
    grads = pl.pallas_call(
        functools.partial(scale_kernel, entries=2 * kernels * BAND * BAND),
        out_shape=jax.ShapeDtypeStruct((2, kernels, 2, BAND), jnp.float32),
        in_specs=[VMEM] * 2,
        out_specs=VMEM,
        compiler_params=params(8),
        name="scale",
    )(whole, squares)
    return resist, grads.transpose(0, 1, 3, 2)


def solution(mesh):
    devices = mesh.devices.reshape(4, 8, 2, 4)
    fine = Mesh(devices, ALL)
    grid = P(ROW, "x")
    in_specs = (grid, grid, P(), P(), P(), P(), P(), P(), P())
    out_specs = (grid, P(None, None, None, ROW))
    return jax.shard_map(on_device, mesh=fine, in_specs=in_specs, out_specs=out_specs, check_vma=False)
```

```python
import functools
import math

import jax
import jax.numpy as jnp
import numpy as np
from jax import lax
from jax.experimental import pallas as pl
from jax.experimental.pallas import tpu as pltpu
from jax.sharding import Mesh, PartitionSpec as P

TILE = 512
BAND = 128
ROW = ("y", "z", "core")
ALL = ("y", "z", "core", "x")


def phase_angles(freqs, positions):
    return 2.0 * math.pi * ((freqs[:, None] * positions[None, :]) % TILE) / TILE


def dot(a, b):
    return jnp.dot(a, b, preferred_element_type=jnp.float32)


def constant_split(x):
    x = np.asarray(x, np.float32)
    hi = x.astype(jnp.bfloat16)
    return hi, (x - hi.astype(np.float32)).astype(jnp.bfloat16)


VMEM = pl.BlockSpec(memory_space=pltpu.VMEM)
SMEM = pl.BlockSpec(memory_space=pltpu.SMEM)
HERE = pl.BlockSpec(memory_space=pltpu.HBM)


def near(*arrays):
    return [pltpu.with_memory_space_constraint(jnp.asarray(x), pltpu.VMEM) for x in arrays]


def homes(*arrays):
    return [pltpu.with_memory_space_constraint(jnp.asarray(x), pltpu.HBM) for x in arrays]


def fetch(sources, targets, sems):
    copies = [pltpu.make_async_copy(a, b, sems.at[i]) for i, (a, b) in enumerate(zip(sources, targets, strict=True))]
    for copy in copies:
        copy.start()
    return copies


def params(mib):
    return pltpu.CompilerParams(vmem_limit_bytes=mib * 1024 * 1024)


FREQ = np.arange(BAND) - BAND // 2


def analysis_table():
    ang = phase_angles(np.arange(65), np.arange(TILE))
    table = np.zeros((TILE, 2 * BAND))
    table[:, :64], table[:, 64:BAND] = np.cos(ang[:64]).T, np.sin(ang[1:]).T
    table[:, BAND : BAND + 4] = np.cos(ang[64])[:, None]
    return np.concatenate(constant_split(table), 0)


def row_transform_tables():
    tables = []
    for y in range(4):
        for core in range(2):
            slabs = [128 * ((y - k) % 4) + 8 * (core ^ other) for other in range(2) for k in range(4)]
            n = (np.array(slabs)[:, None, None] + 16 * np.arange(8)[:, None] + np.arange(8)).reshape(-1)
            ang = phase_angles(FREQ, n)
            tables.append(np.concatenate(constant_split(np.concatenate([np.cos(ang), np.sin(ang)], 0)), 0))
    return np.stack(tables)


def expand_table(norm):
    table = np.zeros((2, BAND, 2, BAND))
    for g in range(BAND):
        q = g - 64
        m = abs(q)
        if m < 64:
            table[0, m, 0, g] = 1.0
            table[1, m, 1, g] = -1.0
        if m:
            sign = -1.0 if q > 0 else 1.0
            table[1, 63 + m, 0, g] = sign
            table[0, 63 + m, 1, g] = sign
    return (table.reshape(2 * BAND, 2 * BAND) * norm).astype(jnp.bfloat16)


def synthesis_table(norm):
    ang = phase_angles(FREQ, np.arange(TILE))
    c, s = np.cos(ang), np.sin(ang)
    return np.concatenate([np.concatenate([c, s], 1), np.concatenate([-s, c], 1)], 0) * norm


def line_tables(groups, height):
    at = np.arange(groups)[:, None] * height + np.array(FIELD_ROWS)[None, :]
    ang = phase_angles(at.reshape(-1), FREQ)
    return np.concatenate([np.cos(ang), np.sin(ang)], 1).reshape(groups, 16, 2 * BAND).astype(np.float32)


FIELD_ROWS = list(range(8)) + [-4, -3, -2, -1, 8, 9, 10, 11]
HIDDEN_ROWS = list(range(-1, 9)) + [-3, -2, 9, 10]
SLOPE_ROWS = list(range(8)) + [-2, -1, 8, 9] + [None] * 4
WIDE = 17 * 128


def halves(x):
    hi = x.astype(jnp.bfloat16)
    return hi, (x - hi.astype(jnp.float32)).astype(jnp.bfloat16)


def pick(out_rows, in_rows, sign):
    hit = lambda a, b, dy: float(a is not None and b is not None and b - a == sign * (dy - 1))
    return np.array([[[hit(a, b, dy) for b in in_rows] for a in out_rows] for dy in range(3)])


INNER = HIDDEN_ROWS[:10]
CHANNELS = 64


def choose_tables():
    choose = np.zeros((3, 48, 7, 256))
    for dy in range(3):
        for dx in range(3):
            for slot in range(16):
                lane = 16 * dx + slot
                for part, section in ((0, 0), (1, 1), (0, 2)):
                    choose[part, 3 * dy + dx, dy, 48 * section + lane] = 1.0
                    choose[part, 16 + 3 * dy + dx, 4 + dy, 48 * section + lane] = 1.0
    for part in range(3):
        choose[part, 32, 3, 144 + part] = 1.0
    return choose.reshape(144, 7 * 256).astype(jnp.bfloat16)


def lane_masks():
    fore = pick(HIDDEN_ROWS, FIELD_ROWS, 1).transpose(1, 0, 2)
    back = pick(INNER, SLOPE_ROWS, -1).transpose(1, 0, 2)
    masks = np.zeros((80, 256), np.float32)
    masks[:42, :144] = np.tile(fore, (1, 1, 9)).reshape(42, 144)
    masks[42:72, :144] = np.tile(back, (1, 1, 9)).reshape(30, 144)
    return masks


def row_masks():
    fore = np.repeat(pick(SLOPE_ROWS, HIDDEN_ROWS, 1), CHANNELS, 2)
    back = np.repeat(pick(list(range(8)), INNER, -1), CHANNELS, 2)
    return fore.astype(np.float32), back.astype(np.float32)


def tables_kernel(
    first_taps_any, second_taps_any, bias_any, choose_any, lane_masks_any, fore_any, aft_any,
    first_ref, second_ref, second_back_ref, first_back_ref,
    first_taps_ref, second_taps_ref, bias_ref, choose_ref, lane_masks_ref, fore_ref, aft_ref, wide_ref, sems, *, rows
):
    sources = (first_taps_any, second_taps_any, bias_any, choose_any, lane_masks_any, fore_any, aft_any)
    targets = (first_taps_ref, second_taps_ref, bias_ref, choose_ref, lane_masks_ref, fore_ref, aft_ref)
    for copy in fetch(sources, targets, sems):
        copy.wait()
    row0 = lax.axis_index(ROW) * 8
    wide_ref[...] = jnp.zeros_like(wide_ref)
    wide_ref[0:9, 0:CHANNELS] = first_taps_ref[...]
    wide_ref[16:25, 0:CHANNELS] = second_taps_ref[...]
    wide_ref[32:33, 0:CHANNELS] = bias_ref[...]
    tall = wide_ref[...].T[:CHANNELS, :48]
    hi = tall.astype(jnp.bfloat16)
    rest = tall - hi.astype(jnp.float32)
    mid = rest.astype(jnp.bfloat16)
    low = (rest - mid.astype(jnp.float32)).astype(jnp.bfloat16)
    parts = dot(jnp.concatenate([hi, mid, low], 1), choose_ref[...])
    for h, n in enumerate(HIDDEN_ROWS):
        here = row0 + n
        valid = jnp.where((here >= 0) & (here < rows), 1.0, 0.0)
        block = parts[:, 768:1024]
        for dy in range(3):
            block = block + parts[:, 256 * dy : 256 * dy + 256] * lane_masks_ref[3 * h + dy : 3 * h + dy + 1]
        first_ref[64 * h : 64 * h + 64] = (block * valid)[:, :160].astype(jnp.bfloat16)
        if h < 10:
            block = 0.0
            for dy in range(3):
                at = 1024 + 256 * dy
                block = block + parts[:, at : at + 256] * lane_masks_ref[42 + 3 * h + dy : 43 + 3 * h + dy]
            second_back_ref[64 * h : 64 * h + 64] = (block * valid)[:, :144].astype(jnp.bfloat16)
    for taps_ref, mask_ref, out_ref, height in ((second_taps_ref, fore_ref, second_ref, 16), (first_taps_ref, aft_ref, first_back_ref, 8)):
        lanes = out_ref.shape[1]
        taps = taps_ref[...]
        taps = jnp.concatenate([taps] * (lanes // CHANNELS), 1)
        taps_hi = taps.astype(jnp.bfloat16).astype(jnp.float32)
        for at, part in ((0, taps_hi), (out_ref.shape[0] // 2, taps - taps_hi)):
            blocks = []
            for dx in range(3):
                block = 0.0
                for dy in range(3):
                    block = block + part[3 * dy + dx : 3 * dy + dx + 1] * mask_ref[dy]
                blocks.append(block)
            if height == 8:
                blocks.append(jnp.zeros((8, lanes), jnp.float32))
            whole = jnp.concatenate(blocks, 0)
            out_ref[at : at + whole.shape[0]] = whole.astype(jnp.bfloat16)


def resist_tables(first_taps, first_bias, second_taps, rows):
    args = (first_taps, second_taps, first_bias.reshape(1, -1), choose_tables(), lane_masks(), *row_masks())
    return pl.pallas_call(
        functools.partial(tables_kernel, rows=rows),
        out_shape=[
            jax.ShapeDtypeStruct((14 * CHANNELS, 160), jnp.bfloat16),
            jax.ShapeDtypeStruct((96, 14 * CHANNELS), jnp.bfloat16),
            jax.ShapeDtypeStruct((10 * CHANNELS, 144), jnp.bfloat16),
            jax.ShapeDtypeStruct((64, 10 * CHANNELS), jnp.bfloat16),
        ],
        in_specs=[HERE] * 7,
        out_specs=[VMEM] * 4,
        scratch_shapes=[pltpu.VMEM(a.shape, a.dtype) for a in args]
        + [pltpu.VMEM((BAND, BAND), jnp.float32), pltpu.SemaphoreType.DMA((7,))],
        compiler_params=params(12),
        name="tables",
    )(*homes(*args))


SIDE = 256


def hide(first_ref, second_ref, views_ref, here, inner):
    hidden = jnp.tanh(dot(first_ref[...], views_ref[:, here]))
    hi, lo = halves(hidden)
    both = dot(second_ref[...], hi)
    return both[:48] + both[48:] + dot(second_ref[0:48], lo), 1.0 - hidden[:inner] * hidden[:inner]


def place_views(views_ref, dx, moved):
    hi, lo = halves(moved)
    views_ref[16 * dx : 16 * dx + 16] = hi
    views_ref[48 + 16 * dx : 64 + 16 * dx] = hi
    views_ref[96 + 16 * dx : 112 + 16 * dx] = lo


def middle_kernel(field_ref, first_ref, second_ref, mixed_ref, keep_ref, views_ref):
    width = field_ref.shape[1]
    for dx in range(3):
        place_views(views_ref, dx, field_ref[...] if dx == 1 else pltpu.roll(field_ref[...], (1 - dx) % width, 1))
    views_ref[144:160] = jnp.ones((16, width), jnp.bfloat16)

    def step(i, carry):
        at = pl.multiple_of(i * 1536, 256)
        there = pl.ds(pl.multiple_of(at + SIDE, 256), 1536)
        mixed_ref[:, pl.ds(at, 1536)], keep_ref[:, pl.ds(at, 1536)] = hide(first_ref, second_ref, views_ref, there, keep_ref.shape[0])
        return carry

    lax.fori_loop(0, (width - 2 * SIDE) // 1536, step, 0)


def resist_kernel(
    field_ref, target_ref, left_ref, right_ref, first_ref, second_ref, second_back_ref, first_back_ref, offset_ref,
    fields_ref, mixed_mid_ref, keep_mid_ref, weights_any, back_any,
    resist_any, out_ref, resist_ref, weights_ref, back_ref,
    views_ref, keep_ref, mixed_ref, spread_ref, summed_ref, all_ref, sems, *, rows, cols
):
    copies = fetch((weights_any, back_any), (weights_ref, back_ref), sems)
    row0 = lax.axis_index(ROW) * resist_ref.shape[0]
    col0 = lax.axis_index("x") * resist_ref.shape[1]
    width = resist_ref.shape[1]
    inner = keep_ref.shape[0]

    def columns(shape):
        lane = lax.broadcasted_iota(jnp.int32, shape, 1)
        m = jnp.where(lane < width + 64, lane, lane - WIDE)
        return m, (col0 + m >= 0) & (col0 + m < cols)

    m, in_grid = columns((16, WIDE))
    keep_col = (in_grid & (m >= -3) & (m < width + 3)).astype(jnp.float32)
    lane = lax.broadcasted_iota(jnp.int32, (16, BAND), 1)
    gap = [jnp.where(lane < 64, right_ref[i : i + 16], left_ref[i : i + 16]) for i in (0, 16)]
    field = jnp.concatenate([field_ref[...], jnp.where(in_grid[:, width:], gap[0], 0.0)], 1)
    target = jnp.concatenate([target_ref[...], gap[1]], 1)
    for dx in range(3):
        place_views(views_ref, dx, (field if dx == 1 else pltpu.roll(field, (1 - dx) % WIDE, 1)) * keep_col)
    views_ref[144:160] = keep_col.astype(jnp.bfloat16)

    edges = (slice(0, SIDE), slice(width - SIDE, width), slice(width, WIDE))
    kept = (slice(0, SIDE), slice(SIDE, 2 * SIDE), slice(2 * SIDE, 2 * SIDE + BAND))
    mixed_ref[:, SIDE : width - SIDE] = mixed_mid_ref[...]
    for here, place in zip(edges, kept, strict=True):
        mixed_ref[:, here], keep_ref[:, place] = hide(first_ref, second_ref, views_ref, here, inner)

    logits = offset_ref[0] + mixed_ref[16:32] + pltpu.roll(mixed_ref[0:16], 1, 1) + pltpu.roll(mixed_ref[32:48], WIDE - 1, 1)
    resist = 1.0 / (1.0 + jnp.exp(-logits))
    resist_ref[...] = resist[:8, :width]
    sent = pltpu.make_async_copy(resist_ref, resist_any, sems.at[2])
    sent.start()
    slot = lax.broadcasted_iota(jnp.int32, (16, WIDE), 0)
    n = jnp.where(slot < 8, slot, jnp.where(slot < 10, slot - 10, slot - 2))
    use = in_grid & (m >= -2) & (m < width + 2) & (slot < 12) & (row0 + n >= 0) & (row0 + n < rows)
    slope = jnp.where(use, (resist - target) * (TILE / cols), 0.0)
    grid_col = in_grid.astype(jnp.float32)
    for dx in range(3):
        place_views(spread_ref, dx, (slope if dx == 1 else pltpu.roll(slope, (dx - 1) % WIDE, 1)) * grid_col)

    def backward(here, kept):
        hidden_grad = dot(second_back_ref[...], spread_ref[:, here])
        hi, lo = halves(hidden_grad * kept)
        both = dot(first_back_ref[...], hi)
        summed_ref[:, here] = both[:32] + both[32:] + dot(first_back_ref[0:32], lo)

    def middle(i, carry):
        at = pl.multiple_of(i * 1536, 256)
        backward(pl.ds(pl.multiple_of(SIDE + at, 256), 1536), keep_mid_ref[:, pl.ds(at, 1536)])
        return carry

    lax.fori_loop(0, keep_mid_ref.shape[1] // 1536, middle, 0)
    for here, place in zip(edges, kept, strict=True):
        backward(here, keep_ref[:, place])
    grad = summed_ref[8:16] + pltpu.roll(summed_ref[0:8], WIDE - 1, 1) + pltpu.roll(summed_ref[16:24], 1, 1)
    for copy in copies:
        copy.wait()
    grad = jnp.concatenate([grad[:, t * TILE : (t + 1) * TILE] for t in range(4)], 0)
    grad = jnp.concatenate([grad, grad], 1) * 2.0
    half = back_ref.shape[0] // 2
    for i in range(3):
        piece = jnp.concatenate([fields_ref[8 * i + j] * (grad * weights_ref[8 * i + j]) for j in range(8)], 0)
        hi, lo = halves(piece)
        sides = (((1,), (1,)), ((), ()))
        both = lax.dot_general(back_ref[...], hi, sides, preferred_element_type=jnp.float32)
        small = lax.dot_general(back_ref[0:half], lo, sides, preferred_element_type=jnp.float32)
        all_ref[:, 256 * i : 256 * i + 256] = both[:half] + both[half:] + small
    low = lax.broadcasted_iota(jnp.int32, (8, 384), 0) < 4
    for d in range(32):
        first, second = all_ref[8 * d : 8 * d + 8, 0:384], all_ref[8 * d : 8 * d + 8, 384:768]
        even, odd = jnp.where(low, first, pltpu.roll(second, 4, 0)), jnp.where(low, pltpu.roll(first, 4, 0), second)
        for b in range(3):
            out_ref[2 * d, 8 * b : 8 * b + 8] = even[:, BAND * b : BAND * (b + 1)]
            out_ref[2 * d + 1, 8 * b : 8 * b + 8] = odd[:, BAND * b : BAND * (b + 1)]
    sent.wait()


def middle_block(field, tables):
    inner, width = tables[2].shape[0], field.shape[1]
    return pl.pallas_call(
        middle_kernel,
        out_shape=[pltpu.VMEM((48, width - 2 * SIDE), jnp.float32), pltpu.VMEM((inner, width - 2 * SIDE), jnp.float32)],
        in_specs=[VMEM] * 3,
        out_specs=[VMEM] * 2,
        scratch_shapes=[pltpu.VMEM((160, width), jnp.bfloat16)],
        compiler_params=params(32),
        name="middle",
    )(*near(field, tables[0], tables[1]))


def resist_block(field, target, left, right, tables, second_bias, weights, fields, middle, back, dims):
    rows, cols = dims
    inner, width = tables[2].shape[0], field.shape[1]
    return pl.pallas_call(
        functools.partial(resist_kernel, rows=rows, cols=cols),
        out_shape=[pltpu.HBM((8, width), jnp.float32), pltpu.VMEM((64, 24, BAND), jnp.float32)],
        in_specs=[VMEM] * 8 + [SMEM] + [VMEM] * 3 + [HERE] * 2,
        out_specs=[HERE, VMEM],
        scratch_shapes=[
            pltpu.VMEM((8, width), jnp.float32),
            pltpu.SMEM(weights.shape, jnp.float32),
            pltpu.VMEM(back.shape, jnp.bfloat16),
            pltpu.VMEM((160, WIDE), jnp.bfloat16),
            pltpu.VMEM((inner, 2 * SIDE + BAND), jnp.float32),
            pltpu.VMEM((48, WIDE), jnp.float32),
            pltpu.VMEM((144, WIDE), jnp.bfloat16),
            pltpu.VMEM((32, WIDE), jnp.float32),
            pltpu.VMEM((256, 768), jnp.float32),
            pltpu.SemaphoreType.DMA((3,)),
        ],
        compiler_params=params(28),
        name="resist",
    )(field, target, left, right, *tables, second_bias, *near(fields, *middle), *homes(weights, back))


def analyse_kernel(layout_any, table_any, out_ref, layout_ref, table_ref, sems):
    for copy in fetch((layout_any, table_any), (layout_ref, table_ref), sems):
        copy.wait()
    x = layout_ref[...].astype(jnp.float32)
    x = jnp.concatenate([x[:, t * TILE : (t + 1) * TILE] for t in range(4)], 0).astype(jnp.bfloat16)
    sums = dot(x, table_ref[0:TILE]) + dot(x, table_ref[TILE:])
    lane = lax.broadcasted_iota(jnp.int32, (8, BAND), 1)
    last = jnp.zeros((8, BAND), jnp.float32)
    for t in range(4):
        last = jnp.where(lane == t, sums[8 * t : 8 * t + 8, BAND:], last)
    packed = jnp.concatenate([sums[:, :BAND], last], 0)
    for i in range(out_ref.shape[0]):
        out_ref[i] = packed


def repack_kernel(in_ref, out_ref):
    last = in_ref[0, 32:40]
    for z in range(8):
        for t in range(4):
            out_ref[4 * z + t] = in_ref[z, 8 * t : 8 * t + 8]
        if z:
            last = last + pltpu.roll(in_ref[z, 32:40], 4 * z, 1)
    out_ref[32] = last


def fields_kernel(*refs, rows, norm):
    slabs, refs = refs[:8], refs[8:]
    (
        near_rows_ref, far_rows_ref, rows_ref, expand_any, line_any, weights_any, synth_any, target_any, real_any, imag_any,
        cols_ref, fields_ref, intensity_ref, wanted_ref, first_edge_ref, last_edge_ref, *refs
    ) = refs
    (
        expand_ref, line_ref, weights_ref, synth_ref, target_ref, real_ref, imag_ref,
        spec_ref, seen_ref, line_hi_ref, line_lo_ref, sum_ref, sems
    ) = refs
    r = lax.axis_index(ROW)
    sources = [expand_any, line_any.at[r], weights_any, synth_any, target_any]
    targets = [expand_ref, line_ref, weights_ref, synth_ref, target_ref]
    for i in range(0, real_ref.shape[0], 4):
        sources += [real_any.at[i : i + 4], imag_any.at[i : i + 4]]
        targets += [real_ref.at[i : i + 4], imag_ref.at[i : i + 4]]
    copies = fetch(sources, targets, sems)
    row0 = r * 8
    kernels = real_ref.shape[0]
    for p, slab in enumerate(slabs):
        last = slab[32]
        last = jnp.concatenate([pltpu.roll(last, (BAND - 4 * z) % BAND, 1) if z else last for z in range(8)], 0)
        for t in range(5):
            tile = jnp.concatenate([slab[4 * z + t] for z in range(8)], 0) if t < 4 else last
            hi, lo = halves(tile)
            seen_ref[64 * p : 64 * p + 64, t * BAND : (t + 1) * BAND] = hi
            seen_ref[rows + 64 * p : rows + 64 * p + 64, t * BAND : (t + 1) * BAND] = lo
    table_hi = rows_ref[0 : 2 * BAND]
    u = dot(table_hi, seen_ref[0:rows]) + dot(rows_ref[2 * BAND :], seen_ref[0:rows]) + dot(table_hi, seen_ref[rows:])

    def pair(t):
        both = u[:, t * BAND : (t + 1) * BAND]
        return halves(jnp.concatenate([both[:BAND], both[BAND:]], 1))

    copies[0].wait()
    lane = lax.broadcasted_iota(jnp.int32, (BAND, 2 * BAND), 1)
    last = u[:, 4 * BAND :] * norm
    for t in range(4):
        hi, lo = pair(t)
        moved = pltpu.roll(last, (BAND - t) % BAND, 1)
        moved = jnp.concatenate([moved[:BAND], -moved[BAND:]], 1)
        spec_ref[t] = dot(hi, expand_ref[...]) + dot(lo, expand_ref[...]) + jnp.where((lane == 0) | (lane == BAND), moved, 0.0)

    copies[1].wait()
    phase = line_ref[...]
    c, s = phase[:, :BAND], phase[:, BAND:]
    table = jnp.concatenate([jnp.concatenate([c, -s], 1), jnp.concatenate([s, c], 1)], 0)
    lines_hi, lines_lo = halves(table)
    lines_both = jnp.concatenate([lines_hi, lines_lo], 0)
    sum_ref[...] = jnp.zeros_like(sum_ref)

    def lines(k, slot, j):
        kr, ki = real_ref[k], imag_ref[k]
        pieces = []
        for p in range(2):
            columns = []
            for t in (2 * p, 2 * p + 1):
                sr, si = spec_ref[t, :, :BAND], spec_ref[t, :, BAND:]
                columns.append(jnp.concatenate([kr * sr - ki * si, kr * si + ki * sr], 0))
            hi, lo = halves(jnp.concatenate(columns, 1))
            both = dot(lines_both, hi)
            out = both[:32] + both[32:] + dot(lines_hi, lo)
            for t in range(2):
                pieces.append(jnp.concatenate([out[:16, t * BAND : (t + 1) * BAND], out[16:, t * BAND : (t + 1) * BAND]], 1))
        hi, lo = halves(jnp.concatenate(pieces, 0))
        line_hi_ref[slot, 64 * j : 64 * j + 64] = hi
        line_lo_ref[slot, 64 * j : 64 * j + 64] = lo

    def waves(k0, slot, q):
        here = slice(q * 256, q * 256 + 256)
        synth_hi = synth_ref[0 : 2 * BAND, here]
        line_hi = line_hi_ref[slot]
        f = dot(line_hi, synth_hi) + dot(line_lo_ref[slot], synth_hi) + dot(line_hi, synth_ref[2 * BAND :, here])
        total = sum_ref[:, here]
        for j in range(4):
            part = f[64 * j : 64 * j + 64]
            total = total + weights_ref[k0 + j] * (part * part)
            fields_ref[k0 + j, :, here] = jnp.concatenate([part[16 * t : 16 * t + 8] for t in range(4)], 0)
        sum_ref[:, here] = total

    for copy in copies[5:7]:
        copy.wait()
    for j in range(4):
        lines(j, 0, j)
    for copy in copies[2:5]:
        copy.wait()
    for copy in copies[7:]:
        copy.wait()

    def group(i, slot, more):
        for j in range(4):
            waves(4 * i, slot, j)
            if more:
                lines(4 * i + 4 + j, 1 - slot, j)

    def both(m, carry):
        group(2 * m, 0, True)
        group(2 * m + 1, 1, True)
        return carry

    lax.fori_loop(0, 2, both, 0)
    group(4, 0, True)
    group(5, 1, False)
    row = lax.broadcasted_iota(jnp.int32, (16, 2 * BAND), 0)
    lane = lax.broadcasted_iota(jnp.int32, (16, 2 * BAND), 1)
    chosen = ((row < 4) & (lane == 2 * r + row % 2 + BAND * (row // 2))).astype(jnp.bfloat16)
    for t in range(4):
        hi, lo = halves(spec_ref[t])
        sides = (((1,), (1,)), ((), ()))
        picked = lax.dot_general(chosen, hi, sides, preferred_element_type=jnp.float32)
        cols_ref[t] = (picked + lax.dot_general(chosen, lo, sides, preferred_element_type=jnp.float32))[:8]
    slot = lax.broadcasted_iota(jnp.int32, (16, TILE), 0)
    n = row0 + jnp.where(slot < 8, slot, jnp.where(slot < 12, slot - 12, slot - 4))
    inside = (n >= 0) & (n < rows)
    for t in range(4):
        both = sum_ref[16 * t : 16 * t + 16]
        intensity_ref[:, t * TILE : (t + 1) * TILE] = jnp.where(inside, both[:, :TILE] + both[:, TILE:], 0.0)
    wanted_ref[0:8] = target_ref[...].astype(jnp.float32)
    one, other = near_rows_ref[...].astype(jnp.float32), far_rows_ref[...].astype(jnp.float32)
    even = r % 2 == 0
    above, below = jnp.where(even, other, one), jnp.where(even, one, other)
    wanted_ref[8:16] = jnp.concatenate([above[6:8], below[0:2], jnp.zeros((4, above.shape[1]), jnp.float32)], 0)
    width = intensity_ref.shape[1]
    for i, ref in ((0, intensity_ref), (16, wanted_ref)):
        first_edge_ref[i : i + 16] = ref[:, 0:BAND]
        last_edge_ref[i : i + 16] = ref[:, width - BAND :]


def adjoint_tables():
    wide = phase_angles(8 * np.arange(64), FREQ)
    c, s = np.cos(wide), np.sin(wide)
    w = np.concatenate([np.concatenate([c, -s], 1), np.concatenate([s, c], 1)], 0)
    near_rows = phase_angles(np.arange(8), FREQ)
    return np.concatenate(constant_split(w), 0), np.concatenate([np.cos(near_rows), np.sin(near_rows)], 0).astype(np.float32)


def adjoint_kernel(got_ref, columns_ref, table_any, turn_any, out_ref, table_ref, turn_ref, sems):
    copies = fetch((table_any, turn_any), (table_ref, turn_ref), sems)
    split = {}
    for h in range(2):
        for g in range(2):
            at = 4 * h + 2 * g
            x = [[got_ref[pl.ds(8 * b + at + i, 64, stride=24), :] for b in range(3)] for i in range(2)]
            split[h, g] = halves(jnp.concatenate([jnp.concatenate(part, 1) for part in x], 0))
    for copy in copies:
        copy.wait()
    table_hi, table_lo = table_ref[0:BAND], table_ref[BAND:]
    c, s = turn_ref[0:8], turn_ref[8:16]
    for g in range(2):
        turned = []
        for t in range(4):
            re, im = columns_ref[t, g : g + 1], columns_ref[t, 2 + g : 3 + g]
            turned.append((c * re - s * im, s * re + c * im))
        a, b = (jnp.concatenate([x[i] for x in turned], 0)[None] for i in range(2))
        for h in range(2):
            hi, lo = split[h, g]
            sides = (((0,), (0,)), ((), ()))
            y = lax.dot_general(hi, table_hi, sides, preferred_element_type=jnp.float32)
            y = y + lax.dot_general(lo, table_hi, sides, preferred_element_type=jnp.float32)
            y = y + lax.dot_general(hi, table_lo, sides, preferred_element_type=jnp.float32)
            y = y.reshape(12, 32, 2 * BAND)
            re, im = y[:, :, :BAND], y[:, :, BAND:]
            out_ref[0, g, 12 * h : 12 * h + 12] = jnp.sum(re * a + im * b, 1)
            out_ref[1, g, 12 * h : 12 * h + 12] = jnp.sum(im * a - re * b, 1)


def total_kernel(x_ref, one_ref, two_ref, three_ref, whole_ref, square_ref):
    whole = (x_ref[...] + two_ref[...]) + (one_ref[...] + three_ref[...])
    whole_ref[...] = whole
    flat = jnp.sum(whole * whole, (0, 1, 2))[None]
    square_ref[...] = jnp.broadcast_to(flat[None], square_ref.shape)


def scale_kernel(whole_ref, squares_ref, out_ref, *, entries):
    total = jnp.sum(jnp.sum(squares_ref[...], 0), 1, keepdims=True)
    factor = lax.rsqrt(total / entries + 1e-06)
    for i in range(2):
        for g in range(2):
            out_ref[i, :, g, :] = whole_ref[i, g] * factor


def fields_block(slabs, row_table, synth, kernel_real, kernel_imaginary, weights, target, near_rows, far_rows, norm):
    kernels = kernel_real.shape[0]
    height, width = target.shape
    tiles, rows = width // TILE, 64 * height
    return pl.pallas_call(
        functools.partial(fields_kernel, rows=rows, norm=norm),
        out_shape=[
            jax.ShapeDtypeStruct((tiles, 8, BAND), jnp.float32),
            pltpu.VMEM((kernels, tiles * height, 2 * TILE), jnp.float32),
            jax.ShapeDtypeStruct((16, width), jnp.float32),
            jax.ShapeDtypeStruct((16, width), jnp.float32),
            jax.ShapeDtypeStruct((32, BAND), jnp.float32),
            jax.ShapeDtypeStruct((32, BAND), jnp.float32),
        ],
        in_specs=[VMEM] * 11 + [HERE] * 7,
        out_specs=[VMEM] * 6,
        scratch_shapes=[
            pltpu.VMEM((2 * BAND, 2 * BAND), jnp.bfloat16),
            pltpu.VMEM((16, 2 * BAND), jnp.float32),
            pltpu.SMEM(weights.shape, jnp.float32),
            pltpu.VMEM((4 * BAND, 2 * TILE), jnp.bfloat16),
            pltpu.VMEM(target.shape, jnp.bfloat16),
            pltpu.VMEM(kernel_real.shape, jnp.float32),
            pltpu.VMEM(kernel_real.shape, jnp.float32),
            pltpu.VMEM((tiles, BAND, 2 * BAND), jnp.float32),
            pltpu.VMEM((2 * rows, 5 * BAND), jnp.bfloat16),
            pltpu.VMEM((2, 256, 2 * BAND), jnp.bfloat16),
            pltpu.VMEM((2, 256, 2 * BAND), jnp.bfloat16),
            pltpu.VMEM((64, 2 * TILE), jnp.float32),
            pltpu.SemaphoreType.DMA((5 + kernels // 2,)),
        ],
        compiler_params=params(28),
        name="fields",
    )(
        *near(*slabs, near_rows, far_rows, row_table),
        *homes(
            expand_table(norm), line_tables(64, height), weights,
            np.concatenate(constant_split(synth), 0), target, kernel_real, kernel_imaginary,
        ),
    )


def on_device(
    layout, target, kernel_real, kernel_imaginary, weights, first_taps, first_bias, second_taps, second_bias
):
    height, width = layout.shape
    tiles = width // TILE
    kernels = kernel_real.shape[0]
    rows, cols = height * 64, width * 4
    r = lax.axis_index(ROW)
    norm = 1.0 / math.sqrt(rows * TILE)

    near_rows = lax.ppermute(target, ROW, [(i, i ^ 1) for i in range(64)])
    far_rows = lax.ppermute(target, ROW, [(i, (i - 1 if i % 2 == 0 else i + 1) % 64) for i in range(64)])

    packed = pl.pallas_call(
        analyse_kernel,
        out_shape=jax.ShapeDtypeStruct((8, 40, BAND), jnp.float32),
        in_specs=[HERE] * 2,
        out_specs=VMEM,
        scratch_shapes=[
            pltpu.VMEM(layout.shape, jnp.bfloat16),
            pltpu.VMEM((2 * TILE, 2 * BAND), jnp.bfloat16),
            pltpu.SemaphoreType.DMA((2,)),
        ],
        compiler_params=params(8),
        name="analyse",
    )(*homes(layout, analysis_table()))
    gathered = lax.all_to_all(packed, "z", 0, 0, tiled=True)
    tables = resist_tables(first_taps, first_bias, second_taps, rows)
    at = 2 * lax.axis_index("y") + lax.axis_index("core")
    row_table = lax.dynamic_index_in_dim(row_transform_tables(), at, 0, keepdims=False)
    gathered, near_rows, far_rows, row_table, *tables = lax.optimization_barrier(
        (gathered, near_rows, far_rows, row_table, *tables)
    )
    gathered = pl.pallas_call(
        repack_kernel,
        out_shape=jax.ShapeDtypeStruct((33, 8, BAND), jnp.float32),
        in_specs=[VMEM],
        out_specs=VMEM,
        compiler_params=params(8),
        name="repack",
    )(gathered)
    slabs = [gathered] + [lax.ppermute(gathered, "y", [(i, (i + k) % 4) for i in range(4)]) for k in (1, 2, 3)]
    slabs = slabs + [lax.ppermute(slab, "core", [(0, 1), (1, 0)]) for slab in slabs]

    synth = synthesis_table(norm)
    columns, fields, intensity, wanted, first_edge, last_edge = fields_block(
        slabs, row_table, synth, kernel_real, kernel_imaginary, weights, target, near_rows, far_rows, norm
    )
    left = lax.ppermute(last_edge, "x", [(i, (i + 1) % 4) for i in range(4)])
    right = lax.ppermute(first_edge, "x", [((i + 1) % 4, i) for i in range(4)])
    back = synth.reshape(2, 64, 2, 2 * TILE).transpose(1, 2, 0, 3).reshape(256, 2 * TILE)
    back = np.concatenate(constant_split(back), 0)
    middle = middle_block(intensity, tables)
    resist, send = resist_block(
        intensity, wanted, left, right, tables, second_bias, weights, fields, middle, back, (rows, cols)
    )

    got = lax.all_to_all(send, ROW, 0, 0, tiled=True)
    table, turn = adjoint_tables()
    mine = pl.pallas_call(
        adjoint_kernel,
        out_shape=jax.ShapeDtypeStruct((2, 2, kernels, BAND), jnp.float32),
        in_specs=[VMEM] * 2 + [HERE] * 2,
        out_specs=VMEM,
        scratch_shapes=[
            pltpu.VMEM(table.shape, jnp.bfloat16),
            pltpu.VMEM(turn.shape, jnp.float32),
            pltpu.SemaphoreType.DMA((2,)),
        ],
        compiler_params=params(12),
        name="adjoint",
    )(*near(got.reshape(64 * 24, BAND), columns), *homes(table, turn))
    others = [lax.ppermute(mine, "x", [(i, (i + k) % 4) for i in range(4)]) for k in (1, 2, 3)]
    whole, squares = pl.pallas_call(
        total_kernel,
        out_shape=[jax.ShapeDtypeStruct(mine.shape, jnp.float32), jax.ShapeDtypeStruct((64, 1, BAND), jnp.float32)],
        in_specs=[VMEM] * 4,
        out_specs=[VMEM] * 2,
        compiler_params=params(8),
        name="total",
    )(mine, *others)
    squares = lax.all_to_all(squares, ROW, 0, 0, tiled=True)
    grads = pl.pallas_call(
        functools.partial(scale_kernel, entries=2 * kernels * BAND * BAND),
        out_shape=jax.ShapeDtypeStruct((2, kernels, 2, BAND), jnp.float32),
        in_specs=[VMEM] * 2,
        out_specs=VMEM,
        compiler_params=params(8),
        name="scale",
    )(whole, squares)
    return resist, grads.transpose(0, 1, 3, 2)


def solution(mesh):
    devices = mesh.devices.reshape(4, 8, 2, 4)
    fine = Mesh(devices, ALL)
    grid = P(ROW, "x")
    in_specs = (grid, grid, P(), P(), P(), P(), P(), P(), P())
    out_specs = (grid, P(None, None, None, ROW))
    return jax.shard_map(on_device, mesh=fine, in_specs=in_specs, out_specs=out_specs, check_vma=False)
```
